32 devices in a mesh: dp: 8 (over y, x, core), tensor: 4 (over z).
Axes of the slice: x: 2, y: 2, z: 4, core: 2. Of those that a mesh axis runs over, the one named last changes fastest.
Arguments:
- hidden_in: bfloat16 [24576, 1024], P(('dp', 'tensor')), may hold values from -6 to 6
- seq_lengths: int32 [8, 5], P('dp'), may hold values from 1 to 2048, as said below
- cotangent: bfloat16 [24576, 1024], P(('dp', 'tensor')), may hold values from -6 to 6
- w_qkv: float32 [1024, 3, 1024], P('dp', None, 'tensor'), may hold values from -0.1875 to 0.1875
- w_proj: float32 [1024, 1024], P('dp', 'tensor'), may hold values from -1.5 to 1.5
- w_in: float32 [1024, 2, 2624], P('dp', None, 'tensor'), may hold values from -0.1875 to 0.1875
- w_down: float32 [1024, 2624], P('dp', 'tensor'), may hold values from -0.15625 to 0.15625
- norm_gains: float32 [2, 1024], P(None, 'dp'), may hold values from 0.5 to 1.5
- qkv_first: float32 [1024, 3, 1024], P('dp', None, 'tensor'), may hold values from -112 to 112
- qkv_second: float32 [1024, 3, 1024], P('dp', None, 'tensor'), may hold values from 501.3504 to 2005.4016
- proj_first: float32 [1024, 1024], P('dp', 'tensor'), may hold values from -8 to 8
- proj_second: float32 [1024, 1024], P('dp', 'tensor'), may hold values from 3.9168 to 15.6672
- in_first: float32 [1024, 2, 2624], P('dp', None, 'tensor'), may hold values from -56 to 56
- in_second: float32 [1024, 2, 2624], P('dp', None, 'tensor'), may hold values from 125.3376 to 501.3504
- down_first: float32 [1024, 2624], P('dp', 'tensor'), may hold values from -64 to 64
- down_second: float32 [1024, 2624], P('dp', 'tensor'), may hold values from 211.3536 to 845.4144
- gain_first: float32 [2, 1024], P(None, 'dp'), may hold values from -160 to 160
- gain_second: float32 [2, 1024], P(None, 'dp'), may hold values from 1130.496 to 4521.984
Outputs:
- hidden_out: bfloat16 [24576, 1024], P(('dp', 'tensor'))
- grad_input: float32 [24576, 1024], P(('dp', 'tensor'))
- qkv_first_new: float32 [1024, 3, 1024], P('dp', None, 'tensor')
- qkv_second_new: float32 [1024, 3, 1024], P('dp', None, 'tensor')
- qkv_new: float32 [1024, 3, 1024], P('dp', None, 'tensor')
- proj_first_new: float32 [1024, 1024], P('dp', 'tensor')
- proj_second_new: float32 [1024, 1024], P('dp', 'tensor')
- proj_new: float32 [1024, 1024], P('dp', 'tensor')
- in_first_new: float32 [1024, 2, 2624], P('dp', None, 'tensor')
- in_second_new: float32 [1024, 2, 2624], P('dp', None, 'tensor')
- in_new: float32 [1024, 2, 2624], P('dp', None, 'tensor')
- down_first_new: float32 [1024, 2624], P('dp', 'tensor')
- down_second_new: float32 [1024, 2624], P('dp', 'tensor')
- down_new: float32 [1024, 2624], P('dp', 'tensor')
- gain_first_new: float32 [2, 1024], P(None, 'dp')
- gain_second_new: float32 [2, 1024], P(None, 'dp')
- gains_new: float32 [2, 1024], P(None, 'dp')
The draws below stay inside these ranges and needn't reach their ends.
Inputs may be any that keep to these rules, and one draw needn't show every extreme that they name: `seq_lengths`: each row lists the lengths of 5 sequences that fill the 3072 tokens of its group exactly; one of them has length 2048 and starts within the group's first 768 tokens; the others are shorter.
All inputs are finite; a program needn't handle non-finite values.
Results may differ from the reference program's by a relative error of at most 0.023.
Values may be sent and summed in bfloat16 or wider, within the bound.
No kernel may reach another device: no remote copies, remote signals or barrier semaphores. Data moves between devices by JAX's collectives and lax.ppermute only.
A program may use at most 192 MiB of HBM per device.

```python
import math
import jax
import jax.numpy as jnp
from jax import lax

D = 1024
HEADS = 16
HEAD_DIM = 64
FF = 2624
HALF = 64
BLOCK = 512
STEP = 10
TOK_DEV = 768
TOK_GRP = 3072
GROUPS = 8
TOKENS = 24576
LONGEST = 2048


def draw_seq_lengths(key, part):
    key = jax.random.fold_in(key, 11)
    subkeys = jax.random.split(key, 6)
    group_shape = (GROUPS,)
    long_start = jax.random.randint(subkeys[0], group_shape, TOK_DEV // 3 + 1, TOK_DEV)
    finish = long_start + LONGEST
    room_after = TOK_GRP - finish
    before_one = jax.random.randint(subkeys[1], group_shape, 1, long_start // 2 + 1)
    before_two = jax.random.randint(subkeys[2], group_shape, long_start // 2 + 1, long_start)
    after_one = jax.random.randint(subkeys[3], group_shape, finish + 1, finish + room_after // 2 + 1)
    after_two = jax.random.randint(subkeys[4], group_shape, finish + room_after // 2 + 1, TOK_GRP)
    count_before = jax.random.randint(subkeys[5], group_shape, 1, 4)
    cut_low = jnp.where(count_before == 1, after_one, before_one)
    cut_high = jnp.where(count_before == 3, before_two, after_two)
    zeros_col = jnp.zeros(group_shape, jnp.int32)
    bounds = jnp.stack([zeros_col, cut_low, cut_high, long_start, finish, zeros_col + TOK_GRP], axis=1)
    bounds = jnp.sort(bounds, axis=1)
    return (bounds[:, 1:] - bounds[:, :-1]).astype(jnp.int32)


def with_spikes(values, stream_key, source, target, blocks, factor):
    owner, partner = [(jnp.arange(values.shape[axis_at]) // (values.shape[axis_at] // blocks)).reshape([-1 if axis == axis_at else 1 for axis in range(values.ndim)]) for axis_at in (source, target)]
    chosen = jax.random.permutation(stream_key, blocks)[partner]
    strong = (owner == chosen) | (owner == (partner + blocks // 2) % blocks)
    return jnp.where(strong, factor * values, values)


def block_scale(key, shape, shards, least, high):
    factor_of = 1.0
    for dim, shards_of in shards:
        heights = jax.random.uniform(jax.random.fold_in(jax.random.fold_in(key, 6), dim), (shards_of,), jnp.float32, least / len(shards), high / len(shards))
        factor_of = factor_of * jnp.repeat(jnp.exp(heights), shape[dim] // shards_of).reshape((-1,) + (1,) * (len(shape) - 1 - dim))
    return factor_of


def noise(key, dims, spread, limit, cuts=(), kind=jnp.bfloat16):
    array = jax.random.normal(key, dims, jnp.float32) * spread
    if len(cuts) > 0:
        array = block_scale(key, dims, cuts, -0.22, 0.18) * array
    return jnp.clip(array, min=-limit, max=limit).astype(kind)


def gaussian_with(rng, dims, spread, bound, cuts, heavy, dtype=jnp.bfloat16):
    drawn = spread * jax.random.normal(rng, dims, jnp.float32)
    if cuts:
        drawn = drawn * block_scale(rng, dims, cuts, -0.22, 0.18)
    return jnp.clip(with_spikes(drawn, jax.random.fold_in(rng, 3), *heavy), -bound, bound).astype(dtype)


def setup_inputs(seed: int = 0) -> dict:
    streams_of = jax.random.split(jax.random.key(seed), 19)
    return {
        "hidden_in": noise(streams_of[0], (TOKENS, D), 1.0, 6.0, ((0, 32),)),
        "seq_lengths": draw_seq_lengths(jax.random.fold_in(streams_of[18], 71), 0),
        "cotangent": gaussian_with(streams_of[2], (TOKENS, D), 1.0, 6.0, ((0, 32),), (0, 1, 32, 2.75)),
        "w_qkv": noise(streams_of[3], (D, 3, D), D ** -0.5, 0.1875, ((0, 8), (2, 4)), jnp.float32),
        "w_proj": noise(streams_of[4], (D, D), (D // HALF) ** -0.5, 1.5, ((0, 8), (1, 4)), jnp.float32),
        "w_in": noise(streams_of[5], (D, 2, FF), D ** -0.5, 0.1875, ((0, 8), (2, 4)), jnp.float32),
        "w_down": noise(streams_of[6], (D, FF), (FF // 2) ** -0.5, 0.15625, ((0, 8), (1, 4)), jnp.float32),
        "norm_gains": jnp.clip(1.0 + 0.1 * jax.random.normal(streams_of[7], (2, D), jnp.float32), 0.5, 1.5),
        "qkv_first": noise(streams_of[8], (D, 3, D), (0.111 * TOKENS ** 0.5), 112.0, ((0, 8), (2, 4)), jnp.float32),
        "qkv_second": jnp.clip(jnp.exp(math.log(2005.4016) - 1.3862944 * jax.random.uniform(streams_of[9], (D, 3, D), jnp.float32) ** block_scale(streams_of[9], (D, 3, D), ((0, 8), (2, 4)), -0.2, 0.2)), 501.3504, 2005.4016),
        "proj_first": noise(streams_of[10], (D, D), (0.0785 * (TOKENS * HALF ** -1) ** 0.5), 8.0, ((0, 8), (1, 4)), jnp.float32),
        "proj_second": jnp.clip(jnp.exp(math.log(15.6672) - 1.3862944 * jax.random.uniform(streams_of[11], (D, D), jnp.float32) ** block_scale(streams_of[11], (D, D), ((0, 8), (1, 4)), -0.2, 0.2)), 3.9168, 15.6672),
        "in_first": noise(streams_of[12], (D, 2, FF), (0.0555 * TOKENS ** 0.5), 56.0, ((0, 8), (2, 4)), jnp.float32),
        "in_second": jnp.clip(jnp.exp(math.log(501.3504) - 1.3862944 * jax.random.uniform(streams_of[13], (D, 2, FF), jnp.float32) ** block_scale(streams_of[13], (D, 2, FF), ((0, 8), (2, 4)), -0.2, 0.2)), 125.3376, 501.3504),
        "down_first": noise(streams_of[14], (D, FF), (0.072 * TOKENS ** 0.5), 64.0, ((0, 8), (1, 4)), jnp.float32),
        "down_second": jnp.clip(jnp.exp(math.log(845.4144) - 1.3862944 * jax.random.uniform(streams_of[15], (D, FF), jnp.float32) ** block_scale(streams_of[15], (D, FF), ((0, 8), (1, 4)), -0.2, 0.2)), 211.3536, 845.4144),
        "gain_first": noise(streams_of[16], (2, D), (0.167 * TOKENS ** 0.5), 160.0, ((1, 8),), jnp.float32),
        "gain_second": jnp.clip(jnp.exp(math.log(4521.984) - 1.3862944 * jax.random.uniform(streams_of[17], (2, D), jnp.float32) ** block_scale(streams_of[17], (2, D), ((1, 8),), -0.2, 0.2)), 1130.496, 4521.984),
    }


NORM_EPS = 1e-05
THETA_BASE = 10000.0
BETA_ONE = 0.9
BETA_TWO = 0.98
ADAM_EPS = 1e-06
WEIGHT_DECAY = 0.01
GAIN_RATE = 0.5
MASKED = -1e+30

@jax.custom_vjp
def low(v):
    return lax.optimization_barrier(v.astype(jnp.bfloat16)).astype(jnp.float32)

@jax.custom_vjp
def low_back(v):
    return v

def low_keep(v):
    return (low(v), None)

def low_pass(kept, grad):
    return (grad,)

def back_keep(v):
    return (v, None)

def back_low(kept, grad):
    return (low(grad),)
low.defvjp(low_keep, low_pass)
low_back.defvjp(back_keep, back_low)

def layer_norm(values, gain_row):
    mean_value = lax.optimization_barrier(jnp.mean(values, axis=-1, keepdims=True))
    centered = values - mean_value
    variance = lax.optimization_barrier(jnp.mean(centered * centered, axis=-1, keepdims=True))
    return centered * lax.rsqrt(variance + NORM_EPS) * gain_row

def geglu(gate_in, gate_up):
    return jax.nn.gelu(gate_in, approximate=False) * gate_up

def layout(lengths, group_rows):
    seq_ends = jnp.cumsum(lengths).astype(jnp.int32)
    seq_starts = (seq_ends - lengths).astype(jnp.int32)
    token_index = jnp.arange(group_rows).astype(jnp.int32)
    segment = lax.optimization_barrier(jnp.sum((token_index[:, None] >= seq_ends[None, :]).astype(jnp.int32), axis=1)).astype(jnp.int32)
    member = segment[:, None] == jnp.arange(lengths.shape[0]).astype(jnp.int32)[None, :]
    position = (token_index - lax.optimization_barrier(jnp.sum(jnp.where(member, seq_starts[None, :], 0), axis=1))).astype(jnp.int32)
    return (segment, position)

def rotary_tables(position):
    half_dim = HEAD_DIM // 2
    exponent = jnp.arange(half_dim).astype(jnp.float32) * (2.0 / HEAD_DIM)
    inverse = jnp.power(jnp.float32(THETA_BASE), -exponent)
    angle_table = position.astype(jnp.float32)[:, None] * inverse[None, :]
    return (jnp.cos(angle_table), jnp.sin(angle_table))

def rotate(values, cosine_table, sine_table):
    half_dim = values.shape[-1] // 2
    front_half = values[..., :half_dim]
    back_half = values[..., half_dim:]
    cos_rows = cosine_table[:, None, :]
    sin_rows = sine_table[:, None, :]
    return jnp.concatenate([front_half * cos_rows - back_half * sin_rows, back_half * cos_rows + front_half * sin_rows], axis=-1)

def block_mask(segment_pad, block_first):
    query_seg = lax.dynamic_slice_in_dim(segment_pad, block_first + HALF, BLOCK)
    key_seg = lax.dynamic_slice_in_dim(segment_pad, block_first, BLOCK + 2 * HALF)
    offset = jnp.arange(BLOCK)[:, None] + HALF - jnp.arange(BLOCK + 2 * HALF)[None, :]
    return (query_seg[:, None] == key_seg[None, :]) & (jnp.abs(offset) <= HALF)

def attend(queries, key_rows, values, segment):
    group_rows = queries.shape[0]
    score_scale = HEAD_DIM ** (-0.5)
    keys_pad = jnp.pad(key_rows, ((HALF, HALF), (0, 0), (0, 0)))
    values_pad = jnp.pad(values, ((HALF, HALF), (0, 0), (0, 0)))
    segment_pad = jnp.pad(segment, HALF, constant_values=-1)

    def one_block(block_number):
        block_first = (block_number * BLOCK).astype(jnp.int32)
        query_block = lax.dynamic_slice_in_dim(queries, block_first, BLOCK)
        key_block = lax.dynamic_slice_in_dim(keys_pad, block_first, BLOCK + 2 * HALF)
        value_block = lax.dynamic_slice_in_dim(values_pad, block_first, BLOCK + 2 * HALF)
        allowed = block_mask(segment_pad, block_first)
        scores = jnp.einsum('qhd,khd->hqk', query_block, key_block, precision=lax.Precision.HIGHEST) * score_scale
        scores = low_back(jnp.where(allowed[None], scores, MASKED))
        row_top = lax.optimization_barrier(jnp.max(scores, axis=-1, keepdims=True))
        lifted = jnp.exp(scores - row_top)
        attention_probs = low(lifted / lax.optimization_barrier(jnp.sum(lifted, axis=-1, keepdims=True)))
        return jnp.einsum('hqk,khd->qhd', attention_probs, value_block, precision=lax.Precision.HIGHEST)
    blocks = lax.map(jax.checkpoint(one_block), jnp.arange(group_rows // BLOCK).astype(jnp.int32))
    return blocks.reshape(queries.shape)

def group_forward(hidden, lengths, w_qkv, w_proj, w_in, w_down, gains):
    group_rows = hidden.shape[0]
    segment, position = layout(lengths, group_rows)
    cosine_table, sine_table = rotary_tables(position)
    head_shape = (group_rows, HEADS, HEAD_DIM)
    normed_one = low(layer_norm(hidden, gains[0]))
    mixed_qkv = low_back(jnp.einsum('td,dcf->tcf', normed_one, w_qkv, precision=lax.Precision.HIGHEST))
    queries = low(rotate(mixed_qkv[:, 0].reshape(head_shape), cosine_table, sine_table))
    key_rows = low(rotate(mixed_qkv[:, 1].reshape(head_shape), cosine_table, sine_table))
    values = low(mixed_qkv[:, 2].reshape(head_shape))
    attended = low_back(low(attend(queries, key_rows, values, segment).reshape(group_rows, D)))
    branch = low_back(jnp.einsum('tj,oj->to', attended, w_proj, precision=lax.Precision.HIGHEST))
    middle = hidden + branch
    normed_two = low(layer_norm(middle, gains[1]))
    gate_pair = low_back(jnp.einsum('td,dcf->tcf', normed_two, w_in, precision=lax.Precision.HIGHEST))
    active = low(geglu(gate_pair[:, 0], gate_pair[:, 1]))
    branch_two = low_back(jnp.einsum('tf,of->to', active, w_down, precision=lax.Precision.HIGHEST))
    return middle + branch_two

def adam_update(master, gradient, moment_one, moment_two, step_rate):
    one_new = BETA_ONE * moment_one + (1.0 - BETA_ONE) * gradient
    two_new = BETA_TWO * moment_two + (1.0 - BETA_TWO) * gradient * gradient
    one_hat = one_new / (1.0 - BETA_ONE ** STEP)
    two_hat = two_new / (1.0 - BETA_TWO ** STEP)
    master_new = master - step_rate * (one_hat / (jnp.sqrt(two_hat) + ADAM_EPS) + WEIGHT_DECAY * master)
    return (one_new, two_new, master_new)

def reference(hidden_in, seq_lengths, cotangent, w_qkv, w_proj, w_in, w_down, norm_gains, qkv_first, qkv_second, proj_first, proj_second, in_first, in_second, down_first, down_second, gain_first, gain_second):
    hidden_all = hidden_in.astype(jnp.float32).reshape(GROUPS, TOK_GRP, D)
    cot_all = cotangent.astype(jnp.float32).reshape(GROUPS, TOK_GRP, D)
    rounded = (low(w_qkv), low(w_proj), low(w_in), low(w_down), low(norm_gains))

    def whole(hidden_groups, qkv_weight, proj_weight, in_weight, down_weight, gain_pair):

        def one_group(packed):
            return group_forward(packed[0], packed[1], qkv_weight, proj_weight, in_weight, down_weight, gain_pair)
        return lax.map(jax.checkpoint(one_group), (hidden_groups, seq_lengths))
    output, pullback = jax.vjp(whole, hidden_all, *rounded)
    grads = pullback(cot_all)
    hidden_out = output.reshape(TOKENS, D).astype(jnp.bfloat16)
    grad_input = grads[0].reshape(TOKENS, D)
    qkv_one, qkv_two, qkv_new = adam_update(w_qkv, grads[1], qkv_first, qkv_second, D ** (-0.5))
    proj_one, proj_two, proj_new = adam_update(w_proj, grads[2], proj_first, proj_second, (D // HALF) ** (-0.5))
    in_one, in_two, in_new = adam_update(w_in, grads[3], in_first, in_second, D ** (-0.5))
    down_one, down_two, down_new = adam_update(w_down, grads[4], down_first, down_second, (FF // 2) ** (-0.5))
    gain_one, gain_two, gains_new = adam_update(norm_gains, grads[5], gain_first, gain_second, GAIN_RATE)
    return (hidden_out, grad_input, qkv_one, qkv_two, qkv_new, proj_one, proj_two, proj_new, in_one, in_two, in_new, down_one, down_two, down_new, gain_one, gain_two, gains_new)
```

```python
import jax
import jax.numpy as jnp
from jax import lax
from jax.sharding import PartitionSpec as P

D = 1024
HEADS = 16
HEAD_DIM = 64
FF = 2624
HALF = 64
BLOCK = 128
STEP = 10

NORM_EPS = 1e-05
THETA_BASE = 10000.0
BETA_ONE = 0.9
BETA_TWO = 0.98
ADAM_EPS = 1e-06
WEIGHT_DECAY = 0.01
GAIN_RATE = 0.5
MASKED = -1e30


def layer_norm(values, gain_row):
    mean_value = jnp.mean(values, axis=-1, keepdims=True)
    centered = values - mean_value
    variance = jnp.mean(centered * centered, axis=-1, keepdims=True)
    return centered * lax.rsqrt(variance + NORM_EPS) * gain_row


def geglu(gate_in, gate_up):
    return jax.nn.gelu(gate_in, approximate=False) * gate_up


def layout(lengths, token_index, group_rows):
    seq_ends = jnp.cumsum(lengths)
    seq_starts = seq_ends - lengths
    segment = jnp.sum((token_index[:, None] >= seq_ends[None, :]).astype(jnp.int32), axis=1)
    member = segment[:, None] == jnp.arange(lengths.shape[0])[None, :]
    position = token_index - jnp.sum(jnp.where(member, seq_starts[None, :], 0), axis=1)
    inside = (token_index >= 0) & (token_index < group_rows)
    return (jnp.where(inside, segment, -1), jnp.where(inside, position, 0))


def rotary_tables(position):
    half_dim = HEAD_DIM // 2
    exponent = jnp.arange(half_dim).astype(jnp.float32) * (2.0 / HEAD_DIM)
    inverse = jnp.power(jnp.float32(THETA_BASE), -exponent)
    angle_table = position.astype(jnp.float32)[:, None] * inverse[None, :]
    return (jnp.cos(angle_table), jnp.sin(angle_table))


def rotate(values, cosine_table, sine_table):
    half_dim = values.shape[-1] // 2
    front_half = values[..., :half_dim]
    back_half = values[..., half_dim:]
    cos_rows = cosine_table[:, None, :]
    sin_rows = sine_table[:, None, :]
    return jnp.concatenate(
        [
            front_half * cos_rows - back_half * sin_rows,
            back_half * cos_rows + front_half * sin_rows,
        ],
        axis=-1,
    )


def windows(rows):
    count = (rows.shape[0] - 2 * HALF) // BLOCK
    return jnp.stack([rows[n * BLOCK : n * BLOCK + BLOCK + 2 * HALF] for n in range(count)])


def unwindows(parts):
    count = parts.shape[0]
    total = jnp.zeros((count * BLOCK + 2 * HALF,) + parts.shape[2:], parts.dtype)
    for n in range(count):
        total = total.at[n * BLOCK : n * BLOCK + BLOCK + 2 * HALF].add(parts[n])
    return total


def allowed_pairs(segment):
    key_seg = windows(segment)
    query_seg = segment[HALF:-HALF].reshape(-1, BLOCK)
    offset = jnp.arange(BLOCK)[:, None] + HALF - jnp.arange(BLOCK + 2 * HALF)[None, :]
    return (query_seg[:, :, None] == key_seg[:, None, :]) & (jnp.abs(offset) <= HALF)[None]


def attend_forward(queries, key_rows, values, allowed):
    score_scale = HEAD_DIM ** (-0.5)
    query_blocks = queries.reshape(-1, BLOCK, HEADS, HEAD_DIM)
    scores = (
        jnp.einsum(
            "nqhd,nkhd->nhqk", query_blocks, windows(key_rows), preferred_element_type=jnp.float32
        )
        * score_scale
    )
    scores = jnp.where(allowed[:, None], scores, MASKED)
    row_top = jnp.max(scores, axis=-1, keepdims=True)
    lifted = jnp.exp(scores - row_top)
    row_total = jnp.sum(lifted, axis=-1, keepdims=True)
    probs_low = (lifted / row_total).astype(jnp.bfloat16)
    block_out = jnp.einsum(
        "nhqk,nkhd->nqhd", probs_low, windows(values), preferred_element_type=jnp.float32
    )
    return (block_out.reshape(queries.shape), row_top + jnp.log(row_total))


def attend_backward(queries, key_rows, values, allowed, log_totals, grad_output):
    score_scale = HEAD_DIM ** (-0.5)
    query_blocks = queries.reshape(-1, BLOCK, HEADS, HEAD_DIM)
    grad_blocks = grad_output.reshape(-1, BLOCK, HEADS, HEAD_DIM)
    key_blocks = windows(key_rows)
    scores = (
        jnp.einsum("nqhd,nkhd->nhqk", query_blocks, key_blocks, preferred_element_type=jnp.float32)
        * score_scale
    )
    scores = jnp.where(allowed[:, None], scores, MASKED)
    attention_probs = jnp.exp(scores - log_totals)
    grad_probs = jnp.einsum(
        "nqhd,nkhd->nhqk", grad_blocks, windows(values), preferred_element_type=jnp.float32
    )
    row_delta = jnp.sum(attention_probs * grad_probs, axis=-1, keepdims=True)
    grad_scores = (attention_probs * (grad_probs - row_delta)).astype(jnp.bfloat16)
    grad_query = (
        jnp.einsum("nhqk,nkhd->nqhd", grad_scores, key_blocks, preferred_element_type=jnp.float32)
        * score_scale
    )
    grad_key = (
        jnp.einsum("nhqk,nqhd->nkhd", grad_scores, query_blocks, preferred_element_type=jnp.float32)
        * score_scale
    )
    grad_value = jnp.einsum(
        "nhqk,nqhd->nkhd",
        attention_probs.astype(jnp.bfloat16),
        grad_blocks,
        preferred_element_type=jnp.float32,
    )
    return (grad_query.reshape(queries.shape), unwindows(grad_key), unwindows(grad_value))


def adam_update(master, gradient, moment_one, moment_two, step_rate):
    one_new = BETA_ONE * moment_one + (1.0 - BETA_ONE) * gradient
    two_new = BETA_TWO * moment_two + (1.0 - BETA_TWO) * gradient * gradient
    one_hat = one_new / (1.0 - BETA_ONE**STEP)
    two_hat = two_new / (1.0 - BETA_TWO**STEP)
    master_new = master - step_rate * (
        one_hat / (jnp.sqrt(two_hat) + ADAM_EPS) + WEIGHT_DECAY * master
    )
    return (one_new, two_new, master_new)


def dot(left, right, left_dims, right_dims):
    return lax.dot_general(
        left, right, ((left_dims, right_dims), ((), ())), preferred_element_type=jnp.float32
    )


def gather(slab):
    return lax.all_gather(lax.all_gather(slab, "tensor", axis=0), "dp", axis=0)


def scatter(parts):
    return lax.psum_scatter(
        lax.psum_scatter(parts, "dp", scatter_dimension=0, tiled=False),
        "tensor",
        scatter_dimension=0,
        tiled=False,
    )


def shift(rows, step):
    size = lax.axis_size("tensor")
    pairs = [(n, n + step) for n in range(size) if 0 <= n + step < size]
    return lax.ppermute(rows, "tensor", pairs)


def local(
    hidden_in,
    seq_lengths,
    cotangent,
    w_qkv,
    w_proj,
    w_in,
    w_down,
    norm_gains,
    qkv_first,
    qkv_second,
    proj_first,
    proj_second,
    in_first,
    in_second,
    down_first,
    down_second,
    gain_first,
    gain_second,
):
    row_count = hidden_in.shape[0]
    tensor_size = lax.axis_size("tensor")
    group_rows = row_count * tensor_size
    low = jnp.bfloat16

    def slab(weight):
        return weight.reshape(weight.shape[0], -1).T.astype(low)

    def whole(weight, kinds):
        gathered = gather(slab(weight))
        dp_size, tp_size, wide, chunk = gathered.shape
        full = gathered.reshape(dp_size, tp_size, kinds, wide // kinds, chunk)
        return jnp.transpose(full, (2, 1, 3, 0, 4)).reshape(
            kinds, tp_size * wide // kinds, dp_size * chunk
        )

    def split(grad):
        kinds, wide, depth = grad.shape
        dp_size = lax.axis_size("dp")
        parts = grad.astype(low).reshape(
            kinds, tensor_size, wide // tensor_size, dp_size, depth // dp_size
        )
        parts = jnp.transpose(parts, (3, 1, 0, 2, 4)).reshape(
            dp_size, tensor_size, kinds * wide // tensor_size, depth // dp_size
        )
        return scatter(parts).astype(jnp.float32).T

    gains_full = lax.all_gather(norm_gains.astype(low), "dp", axis=1, tiled=True).astype(
        jnp.float32
    )
    edges = (shift(hidden_in[-HALF:], 1), shift(hidden_in[:HALF], -1))
    qkv_full = whole(w_qkv, 3)
    proj_full = whole(w_proj, 1)[0]
    in_full = whole(w_in, 2)
    down_full = whole(w_down, 1)[0]

    first_row = lax.axis_index("tensor") * row_count
    segment, position = layout(
        seq_lengths[0], first_row - HALF + jnp.arange(row_count + 2 * HALF), group_rows
    )
    cosine_table, sine_table = rotary_tables(position)
    allowed = allowed_pairs(segment)

    hidden = hidden_in.astype(jnp.float32)
    normed_one, norm_pull_one = jax.vjp(layer_norm, hidden, gains_full[0])
    normed_edges = layer_norm(jnp.concatenate(edges).astype(jnp.float32), gains_full[0])
    rows_one = normed_one.astype(low)
    rows_edges = normed_edges.astype(low)
    rows_wide = jnp.concatenate([rows_edges[:HALF], rows_one, rows_edges[HALF:]])
    query_pre = dot(rows_one, qkv_full[0], (1,), (1,))
    key_pre = dot(rows_wide, qkv_full[1], (1,), (1,))
    values = dot(rows_wide, qkv_full[2], (1,), (1,)).astype(low).reshape(-1, HEADS, HEAD_DIM)

    def rotate_pair(query_pre, key_pre):
        return (
            rotate(
                query_pre.reshape(-1, HEADS, HEAD_DIM),
                cosine_table[HALF:-HALF],
                sine_table[HALF:-HALF],
            ),
            rotate(key_pre.reshape(-1, HEADS, HEAD_DIM), cosine_table, sine_table),
        )

    (query_turned, key_turned), turn_pull = jax.vjp(rotate_pair, query_pre, key_pre)
    queries = query_turned.astype(low)
    key_rows = key_turned.astype(low)
    attended_heads, log_totals = attend_forward(queries, key_rows, values, allowed)
    attended = attended_heads.reshape(row_count, D).astype(low)
    middle = hidden + dot(attended, proj_full, (1,), (0,))
    normed_two, norm_pull_two = jax.vjp(layer_norm, middle, gains_full[1])
    rows_two = normed_two.astype(low)
    gate_in = dot(rows_two, in_full[0], (1,), (1,))
    gate_up = dot(rows_two, in_full[1], (1,), (1,))
    active_full, geglu_pull = jax.vjp(geglu, gate_in, gate_up)
    active = active_full.astype(low)
    output = middle + dot(active, down_full, (1,), (0,))

    grad_active = dot(cotangent, down_full, (1,), (1,))
    down_sum = split(dot(active, cotangent, (0,), (0,))[None]).reshape(w_down.shape)
    grad_gate_in, grad_gate_up = geglu_pull(grad_active)
    grad_gate_in = grad_gate_in.astype(low)
    grad_gate_up = grad_gate_up.astype(low)
    in_sum = split(
        jnp.stack(
            [
                dot(grad_gate_in, rows_two, (0,), (0,)),
                dot(grad_gate_up, rows_two, (0,), (0,)),
            ]
        )
    ).reshape(w_in.shape)
    grad_normed_two = dot(grad_gate_in, in_full[0], (1,), (0,)) + dot(
        grad_gate_up, in_full[1], (1,), (0,)
    )
    grad_middle_norm, grad_gain_two = norm_pull_two(grad_normed_two)
    grad_middle = cotangent.astype(jnp.float32) + grad_middle_norm
    grad_middle_low = grad_middle.astype(low)
    grad_attended = dot(grad_middle_low, proj_full, (1,), (1,)).astype(low)
    proj_sum = split(dot(attended, grad_middle_low, (0,), (0,))[None]).reshape(w_proj.shape)
    grad_queries, grad_keys, grad_values = attend_backward(
        queries,
        key_rows,
        values,
        allowed,
        log_totals,
        grad_attended.reshape(row_count, HEADS, HEAD_DIM),
    )
    grad_query_pre, grad_key_pre = turn_pull((grad_queries, grad_keys))
    grad_pair = jnp.stack([grad_key_pre, grad_values.reshape(-1, D)])
    from_after = shift(grad_pair[:, :HALF].astype(low), -1).astype(jnp.float32)
    from_before = shift(grad_pair[:, -HALF:].astype(low), 1).astype(jnp.float32)
    grad_pair = grad_pair[:, HALF:-HALF]
    grad_pair = grad_pair.at[:, :HALF].add(from_before).at[:, -HALF:].add(from_after)
    grad_mixed = jnp.concatenate([grad_query_pre[None], grad_pair]).astype(low)
    qkv_sum = split(
        jnp.stack([dot(grad_mixed[c], rows_one, (0,), (0,)) for c in range(3)])
    ).reshape(w_qkv.shape)
    grad_normed_one = sum(dot(grad_mixed[c], qkv_full[c], (1,), (0,)) for c in range(3))
    grad_hidden_norm, grad_gain_one = norm_pull_one(grad_normed_one)
    grad_input = grad_middle + grad_hidden_norm
    gain_sum = lax.psum(
        lax.psum_scatter(
            jnp.stack([grad_gain_one, grad_gain_two]), "dp", scatter_dimension=1, tiled=True
        ),
        "tensor",
    )
    qkv_one, qkv_two, qkv_new = adam_update(w_qkv, qkv_sum, qkv_first, qkv_second, D ** (-0.5))
    proj_one, proj_two, proj_new = adam_update(
        w_proj, proj_sum, proj_first, proj_second, (D // HALF) ** (-0.5)
    )
    in_one, in_two, in_new = adam_update(w_in, in_sum, in_first, in_second, D ** (-0.5))
    down_one, down_two, down_new = adam_update(
        w_down, down_sum, down_first, down_second, (FF // 2) ** (-0.5)
    )
    gain_one, gain_two, gains_new = adam_update(
        norm_gains, gain_sum, gain_first, gain_second, GAIN_RATE
    )
    return (
        output.astype(jnp.bfloat16),
        grad_input,
        qkv_one,
        qkv_two,
        qkv_new,
        proj_one,
        proj_two,
        proj_new,
        in_one,
        in_two,
        in_new,
        down_one,
        down_two,
        down_new,
        gain_one,
        gain_two,
        gains_new,
    )


def solution(mesh):
    placed = (
        P(("dp", "tensor"), None),
        P("dp", None),
        P(("dp", "tensor"), None),
        P("dp", None, "tensor"),
        P("dp", "tensor"),
        P("dp", None, "tensor"),
        P("dp", "tensor"),
        P(None, "dp"),
        P("dp", None, "tensor"),
        P("dp", None, "tensor"),
        P("dp", "tensor"),
        P("dp", "tensor"),
        P("dp", None, "tensor"),
        P("dp", None, "tensor"),
        P("dp", "tensor"),
        P("dp", "tensor"),
        P(None, "dp"),
        P(None, "dp"),
    )
    return jax.shard_map(
        local,
        mesh=mesh,
        in_specs=placed,
        out_specs=(
            P(("dp", "tensor"), None),
            P(("dp", "tensor"), None),
            P("dp", None, "tensor"),
            P("dp", None, "tensor"),
            P("dp", None, "tensor"),
            P("dp", "tensor"),
            P("dp", "tensor"),
            P("dp", "tensor"),
            P("dp", None, "tensor"),
            P("dp", None, "tensor"),
            P("dp", None, "tensor"),
            P("dp", "tensor"),
            P("dp", "tensor"),
            P("dp", "tensor"),
            P(None, "dp"),
            P(None, "dp"),
            P(None, "dp"),
        ),
        check_vma=False,
    )
```

```python
import jax
import jax.numpy as jnp
from jax import lax
from jax.sharding import PartitionSpec as P

D = 1024
HEADS = 16
HEAD_DIM = 64
FF = 2624
HALF = 64
BLOCK = 128
STEP = 10

NORM_EPS = 1e-05
THETA_BASE = 10000.0
BETA_ONE = 0.9
BETA_TWO = 0.98
ADAM_EPS = 1e-06
WEIGHT_DECAY = 0.01
GAIN_RATE = 0.5
MASKED = -1e30


def layer_norm(values, gain_row):
    mean_value = jnp.mean(values, axis=-1, keepdims=True)
    centered = values - mean_value
    variance = jnp.mean(centered * centered, axis=-1, keepdims=True)
    return centered * lax.rsqrt(variance + NORM_EPS) * gain_row


def geglu(gate_in, gate_up):
    return jax.nn.gelu(gate_in, approximate=False) * gate_up


def layout(lengths, token_index, group_rows):
    seq_ends = jnp.cumsum(lengths)
    seq_starts = seq_ends - lengths
    segment = jnp.sum((token_index[:, None] >= seq_ends[None, :]).astype(jnp.int32), axis=1)
    member = segment[:, None] == jnp.arange(lengths.shape[0])[None, :]
    position = token_index - jnp.sum(jnp.where(member, seq_starts[None, :], 0), axis=1)
    inside = (token_index >= 0) & (token_index < group_rows)
    return (jnp.where(inside, segment, -1), jnp.where(inside, position, 0))


def rotary_tables(position):
    half_dim = HEAD_DIM // 2
    exponent = jnp.arange(half_dim).astype(jnp.float32) * (2.0 / HEAD_DIM)
    inverse = jnp.power(jnp.float32(THETA_BASE), -exponent)
    angle_table = position.astype(jnp.float32)[:, None] * inverse[None, :]
    return (jnp.cos(angle_table), jnp.sin(angle_table))


def rotate(values, cosine_table, sine_table):
    half_dim = values.shape[-1] // 2
    front_half = values[..., :half_dim]
    back_half = values[..., half_dim:]
    cos_rows = cosine_table[:, None, :]
    sin_rows = sine_table[:, None, :]
    return jnp.concatenate(
        [
            front_half * cos_rows - back_half * sin_rows,
            back_half * cos_rows + front_half * sin_rows,
        ],
        axis=-1,
    )


def windows(rows):
    count = (rows.shape[0] - 2 * HALF) // BLOCK
    return jnp.stack([rows[n * BLOCK : n * BLOCK + BLOCK + 2 * HALF] for n in range(count)])


def unwindows(parts):
    count = parts.shape[0]
    total = jnp.zeros((count * BLOCK + 2 * HALF,) + parts.shape[2:], parts.dtype)
    for n in range(count):
        total = total.at[n * BLOCK : n * BLOCK + BLOCK + 2 * HALF].add(parts[n])
    return total


def allowed_pairs(segment):
    key_seg = windows(segment)
    query_seg = segment[HALF:-HALF].reshape(-1, BLOCK)
    offset = jnp.arange(BLOCK)[:, None] + HALF - jnp.arange(BLOCK + 2 * HALF)[None, :]
    return (query_seg[:, :, None] == key_seg[:, None, :]) & (jnp.abs(offset) <= HALF)[None]


def attend_forward(queries, key_rows, values, allowed):
    score_scale = HEAD_DIM ** (-0.5)
    query_blocks = queries.reshape(-1, BLOCK, HEADS, HEAD_DIM)
    scores = (
        jnp.einsum(
            "nqhd,nkhd->nhqk", query_blocks, windows(key_rows), preferred_element_type=jnp.float32
        )
        * score_scale
    )
    scores = jnp.where(allowed[:, None], scores, MASKED)
    row_top = jnp.max(scores, axis=-1, keepdims=True)
    lifted = jnp.exp(scores - row_top)
    row_total = jnp.sum(lifted, axis=-1, keepdims=True)
    probs_low = (lifted / row_total).astype(jnp.bfloat16)
    block_out = jnp.einsum(
        "nhqk,nkhd->nqhd", probs_low, windows(values), preferred_element_type=jnp.float32
    )
    return (block_out.reshape(queries.shape), row_top + jnp.log(row_total))


def attend_backward(queries, key_rows, values, allowed, log_totals, grad_output):
    score_scale = HEAD_DIM ** (-0.5)
    query_blocks = queries.reshape(-1, BLOCK, HEADS, HEAD_DIM)
    grad_blocks = grad_output.reshape(-1, BLOCK, HEADS, HEAD_DIM)
    key_blocks = windows(key_rows)
    scores = (
        jnp.einsum("nqhd,nkhd->nhqk", query_blocks, key_blocks, preferred_element_type=jnp.float32)
        * score_scale
    )
    scores = jnp.where(allowed[:, None], scores, MASKED)
    attention_probs = jnp.exp(scores - log_totals)
    grad_probs = jnp.einsum(
        "nqhd,nkhd->nhqk", grad_blocks, windows(values), preferred_element_type=jnp.float32
    )
    row_delta = jnp.sum(attention_probs * grad_probs, axis=-1, keepdims=True)
    grad_scores = (attention_probs * (grad_probs - row_delta)).astype(jnp.bfloat16)
    grad_query = (
        jnp.einsum("nhqk,nkhd->nqhd", grad_scores, key_blocks, preferred_element_type=jnp.float32)
        * score_scale
    )
    grad_key = (
        jnp.einsum("nhqk,nqhd->nkhd", grad_scores, query_blocks, preferred_element_type=jnp.float32)
        * score_scale
    )
    grad_value = jnp.einsum(
        "nhqk,nqhd->nkhd",
        attention_probs.astype(jnp.bfloat16),
        grad_blocks,
        preferred_element_type=jnp.float32,
    )
    return (grad_query.reshape(queries.shape), unwindows(grad_key), unwindows(grad_value))


def adam_update(master, gradient, moment_one, moment_two, step_rate):
    one_new = BETA_ONE * moment_one + (1.0 - BETA_ONE) * gradient
    two_new = BETA_TWO * moment_two + (1.0 - BETA_TWO) * gradient * gradient
    one_hat = one_new / (1.0 - BETA_ONE**STEP)
    two_hat = two_new / (1.0 - BETA_TWO**STEP)
    master_new = master - step_rate * (
        one_hat / (jnp.sqrt(two_hat) + ADAM_EPS) + WEIGHT_DECAY * master
    )
    return (one_new, two_new, master_new)


def dot(left, right, left_dims, right_dims):
    return lax.dot_general(
        left, right, ((left_dims, right_dims), ((), ())), preferred_element_type=jnp.float32
    )


def line_gather(slab):
    size = lax.axis_size("tensor")
    place = lax.axis_index("tensor")
    from_before, from_after = [slab], [slab]
    for step in range(1, size):
        from_before.append(
            lax.ppermute(from_before[-1], "tensor", [(n, n + 1) for n in range(step - 1, size - 1)])
        )
        from_after.append(
            lax.ppermute(from_after[-1], "tensor", [(n, n - 1) for n in range(1, size - step + 1)])
        )
    return jnp.stack(
        [slab]
        + [
            jnp.where(place >= step, from_before[step], from_after[size - step])
            for step in range(1, size)
        ]
    )


def line_scatter(parts):
    size = lax.axis_size("tensor")
    up, down = 0.0, 0.0
    for step in range(size - 1, 0, -1):
        to_after = (parts[size - step].astype(jnp.float32) + up).astype(parts.dtype)
        to_before = (parts[step].astype(jnp.float32) + down).astype(parts.dtype)
        up = lax.ppermute(to_after, "tensor", [(n, n + 1) for n in range(size - step)])
        down = lax.ppermute(to_before, "tensor", [(n, n - 1) for n in range(step, size)])
        up, down = up.astype(jnp.float32), down.astype(jnp.float32)
    return parts[0].astype(jnp.float32) + up + down


def flip(rows, mask):
    return lax.ppermute(rows, "dp", [(n, n ^ mask) for n in range(lax.axis_size("dp"))])


def far_bits():
    size = lax.axis_size("dp")
    return [1 << n for n in range(3, size.bit_length() - 1)]


def gather(slab, x_first):
    piece = line_gather(slab)
    piece = piece.reshape(-1, piece.shape[-1])
    for mask in far_bits():
        piece = jnp.concatenate([piece, flip(piece, mask)], axis=1)
    by_x, by_y = flip(piece, 2), flip(piece, 4)
    far = flip(by_x, 4) if x_first else flip(by_y, 2)
    mine = [piece, by_x, by_y, far]
    return mine + [flip(part, 1) for part in mine]


def add_low(left, right):
    return (left.astype(jnp.float32) + right.astype(jnp.float32)).astype(left.dtype)


def scatter(pieces, x_first):
    own, by_x, by_y, far = [
        add_low(mine, flip(theirs, 1)) for mine, theirs in zip(pieces[:4], pieces[4:])
    ]
    if x_first:
        by_y = add_low(by_y, flip(far, 2))
    else:
        by_x = add_low(by_x, flip(far, 4))
    total = (
        own.astype(jnp.float32)
        + flip(by_x, 2).astype(jnp.float32)
        + flip(by_y, 4).astype(jnp.float32)
    ).astype(own.dtype)
    for mask in reversed(far_bits()):
        half = total.shape[1] // 2
        total = add_low(total[:, :half], flip(total[:, half:], mask))
    size = lax.axis_size("tensor")
    return line_scatter(total.reshape(size, total.shape[0] // size, total.shape[1]))


def to_relative(rows, back=False):
    size = lax.axis_size("dp")
    place = lax.axis_index("dp")
    bits = size.bit_length() - 1
    lead = rows.shape[:-1]
    axes = len(lead)
    chunk = rows.shape[-1] // size
    wanted = [bits - 1, bits - 3, bits - 2] + list(range(bits - 3))
    order = list(range(axes)) + [axes + n for n in wanted] + [axes + bits]
    cube = rows.reshape(lead + (2,) * bits + (chunk,))
    if back:
        cube = jnp.transpose(cube, [order.index(n) for n in range(len(order))])
    for n in range(bits):
        cube = jnp.where((place >> (bits - 1 - n)) & 1 == 1, jnp.flip(cube, axes + n), cube)
    if not back:
        cube = jnp.transpose(cube, order)
    return cube.reshape(rows.shape)


def shift(rows, step):
    size = lax.axis_size("tensor")
    pairs = [(n, n + step) for n in range(size) if 0 <= n + step < size]
    return lax.ppermute(rows, "tensor", pairs)


def local(
    hidden_in,
    seq_lengths,
    cotangent,
    w_qkv,
    w_proj,
    w_in,
    w_down,
    norm_gains,
    qkv_first,
    qkv_second,
    proj_first,
    proj_second,
    in_first,
    in_second,
    down_first,
    down_second,
    gain_first,
    gain_second,
):
    row_count = hidden_in.shape[0]
    tensor_size = lax.axis_size("tensor")
    group_rows = row_count * tensor_size
    low = jnp.bfloat16
    qkv_wide, proj_wide = w_qkv.shape[1] * w_qkv.shape[2], w_proj.shape[1]
    head_wide = w_qkv.shape[2]
    up_wide = w_down.shape[1]

    def slab(weight):
        return weight.reshape(weight.shape[0], -1).T.astype(low)

    def whole(pieces):
        full = jnp.concatenate(pieces, axis=1)
        return full.reshape(tensor_size, -1, full.shape[1])

    def split(grads):
        stacked = jnp.concatenate(
            [grad.astype(low).reshape(tensor_size, -1, grad.shape[1]) for grad in grads], axis=1
        )
        stacked = stacked.reshape(-1, stacked.shape[2])
        return jnp.split(stacked, 8, axis=1)

    hidden_low = to_relative(hidden_in)
    cot_low = to_relative(cotangent)
    edges = (shift(hidden_low[-HALF:], 1), shift(hidden_low[:HALF], -1))
    gain_rows = jnp.pad(norm_gains.astype(low), ((0, 14), (0, 0)))
    heads_full = whole(
        gather(jnp.concatenate([slab(w_qkv), slab(w_proj), gain_rows], axis=0), True)
    )
    in_full = whole(gather(slab(w_in), False))
    down_full = whole(gather(slab(w_down), True)).reshape(-1, D)
    qkv_full = [
        heads_full[:, c * head_wide : (c + 1) * head_wide].reshape(-1, D) for c in range(3)
    ]
    proj_full = heads_full[:, qkv_wide : qkv_wide + proj_wide].reshape(-1, D)
    gains_full = heads_full[0, qkv_wide + proj_wide : qkv_wide + proj_wide + 2].astype(jnp.float32)
    in_full = [in_full[:, c * up_wide : (c + 1) * up_wide].reshape(-1, D) for c in range(2)]

    first_row = lax.axis_index("tensor") * row_count
    segment, position = layout(
        seq_lengths[0], first_row - HALF + jnp.arange(row_count + 2 * HALF), group_rows
    )
    cosine_table, sine_table = rotary_tables(position)
    allowed = allowed_pairs(segment)

    hidden = hidden_low.astype(jnp.float32)
    normed_one, norm_pull_one = jax.vjp(layer_norm, hidden, gains_full[0])
    normed_edges = layer_norm(jnp.concatenate(edges).astype(jnp.float32), gains_full[0])
    rows_one = normed_one.astype(low)
    rows_edges = normed_edges.astype(low)
    rows_wide = jnp.concatenate([rows_edges[:HALF], rows_one, rows_edges[HALF:]])
    query_pre = dot(rows_one, qkv_full[0], (1,), (1,))
    key_pre = dot(rows_wide, qkv_full[1], (1,), (1,))
    values = dot(rows_wide, qkv_full[2], (1,), (1,)).astype(low).reshape(-1, HEADS, HEAD_DIM)

    def rotate_pair(query_pre, key_pre):
        return (
            rotate(
                query_pre.reshape(-1, HEADS, HEAD_DIM),
                cosine_table[HALF:-HALF],
                sine_table[HALF:-HALF],
            ),
            rotate(key_pre.reshape(-1, HEADS, HEAD_DIM), cosine_table, sine_table),
        )

    (query_turned, key_turned), turn_pull = jax.vjp(rotate_pair, query_pre, key_pre)
    queries = query_turned.astype(low)
    key_rows = key_turned.astype(low)
    attended_heads, log_totals = attend_forward(queries, key_rows, values, allowed)
    attended = attended_heads.reshape(row_count, D).astype(low)
    middle = hidden + dot(attended, proj_full, (1,), (0,))
    normed_two, norm_pull_two = jax.vjp(layer_norm, middle, gains_full[1])
    rows_two = normed_two.astype(low)
    gate_in = dot(rows_two, in_full[0], (1,), (1,))
    gate_up = dot(rows_two, in_full[1], (1,), (1,))
    active_full, geglu_pull = jax.vjp(geglu, gate_in, gate_up)
    active = active_full.astype(low)
    output = middle + dot(active, down_full, (1,), (0,))

    grad_active = dot(cot_low, down_full, (1,), (1,))
    down_sum = scatter(split([dot(active, cot_low, (0,), (0,))]), True).T
    grad_gate_in, grad_gate_up = geglu_pull(grad_active)
    grad_gate_in = grad_gate_in.astype(low)
    grad_gate_up = grad_gate_up.astype(low)
    in_sum = scatter(
        split(
            [
                dot(grad_gate_in, rows_two, (0,), (0,)),
                dot(grad_gate_up, rows_two, (0,), (0,)),
            ]
        ),
        False,
    ).T.reshape(w_in.shape)
    grad_normed_two = dot(grad_gate_in, in_full[0], (1,), (0,)) + dot(
        grad_gate_up, in_full[1], (1,), (0,)
    )
    grad_middle_norm, grad_gain_two = norm_pull_two(grad_normed_two)
    grad_middle = cot_low.astype(jnp.float32) + grad_middle_norm
    grad_middle_low = grad_middle.astype(low)
    grad_attended = dot(grad_middle_low, proj_full, (1,), (1,)).astype(low)
    grad_proj = dot(attended, grad_middle_low, (0,), (0,))
    grad_queries, grad_keys, grad_values = attend_backward(
        queries,
        key_rows,
        values,
        allowed,
        log_totals,
        grad_attended.reshape(row_count, HEADS, HEAD_DIM),
    )
    grad_query_pre, grad_key_pre = turn_pull((grad_queries, grad_keys))
    grad_pair = jnp.stack([grad_key_pre, grad_values.reshape(-1, D)])
    from_after = shift(grad_pair[:, :HALF].astype(low), -1).astype(jnp.float32)
    from_before = shift(grad_pair[:, -HALF:].astype(low), 1).astype(jnp.float32)
    from_after = jnp.roll(from_after, -head_wide, axis=-1)
    from_before = jnp.roll(from_before, head_wide, axis=-1)
    grad_pair = grad_pair[:, HALF:-HALF]
    grad_pair = grad_pair.at[:, :HALF].add(from_before).at[:, -HALF:].add(from_after)
    grad_mixed = jnp.concatenate([grad_query_pre[None], grad_pair]).astype(low)
    heads_sum = scatter(
        split([dot(grad_mixed[c], rows_one, (0,), (0,)) for c in range(3)] + [grad_proj]), True
    ).T
    qkv_sum = heads_sum[:, :qkv_wide].reshape(w_qkv.shape)
    proj_sum = heads_sum[:, qkv_wide:]
    grad_normed_one = sum(dot(grad_mixed[c], qkv_full[c], (1,), (0,)) for c in range(3))
    grad_hidden_norm, grad_gain_one = norm_pull_one(grad_normed_one)
    grad_input = grad_middle + grad_hidden_norm
    gain_total = lax.psum(
        to_relative(jnp.stack([grad_gain_one, grad_gain_two]), back=True), ("dp", "tensor")
    )
    chunk = norm_gains.shape[1]
    gain_sum = lax.dynamic_slice_in_dim(gain_total, lax.axis_index("dp") * chunk, chunk, axis=1)
    qkv_one, qkv_two, qkv_new = adam_update(w_qkv, qkv_sum, qkv_first, qkv_second, D ** (-0.5))
    proj_one, proj_two, proj_new = adam_update(
        w_proj, proj_sum, proj_first, proj_second, (D // HALF) ** (-0.5)
    )
    in_one, in_two, in_new = adam_update(w_in, in_sum, in_first, in_second, D ** (-0.5))
    down_one, down_two, down_new = adam_update(
        w_down, down_sum, down_first, down_second, (FF // 2) ** (-0.5)
    )
    gain_one, gain_two, gains_new = adam_update(
        norm_gains, gain_sum, gain_first, gain_second, GAIN_RATE
    )
    return (
        to_relative(output.astype(low), back=True),
        to_relative(grad_input, back=True),
        qkv_one,
        qkv_two,
        qkv_new,
        proj_one,
        proj_two,
        proj_new,
        in_one,
        in_two,
        in_new,
        down_one,
        down_two,
        down_new,
        gain_one,
        gain_two,
        gains_new,
    )


def solution(mesh):
    placed = (
        P(("dp", "tensor"), None),
        P("dp", None),
        P(("dp", "tensor"), None),
        P("dp", None, "tensor"),
        P("dp", "tensor"),
        P("dp", None, "tensor"),
        P("dp", "tensor"),
        P(None, "dp"),
        P("dp", None, "tensor"),
        P("dp", None, "tensor"),
        P("dp", "tensor"),
        P("dp", "tensor"),
        P("dp", None, "tensor"),
        P("dp", None, "tensor"),
        P("dp", "tensor"),
        P("dp", "tensor"),
        P(None, "dp"),
        P(None, "dp"),
    )
    return jax.shard_map(
        local,
        mesh=mesh,
        in_specs=placed,
        out_specs=(
            P(("dp", "tensor"), None),
            P(("dp", "tensor"), None),
            P("dp", None, "tensor"),
            P("dp", None, "tensor"),
            P("dp", None, "tensor"),
            P("dp", "tensor"),
            P("dp", "tensor"),
            P("dp", "tensor"),
            P("dp", None, "tensor"),
            P("dp", None, "tensor"),
            P("dp", None, "tensor"),
            P("dp", "tensor"),
            P("dp", "tensor"),
            P("dp", "tensor"),
            P(None, "dp"),
            P(None, "dp"),
            P(None, "dp"),
        ),
        check_vma=False,
    )
```

```python
import functools
import math

import jax
import jax.numpy as jnp
from jax import lax
from jax.experimental import pallas as pl
from jax.experimental.pallas import tpu as pltpu
from jax.sharding import PartitionSpec as P

D = 1024
HEADS = 16
HEAD_DIM = 64
FF = 2624
HALF = 64
BLOCK = 128
STEP = 10

NORM_EPS = 1e-05
THETA_BASE = 10000.0
BETA_ONE = 0.9
BETA_TWO = 0.98
ADAM_EPS = 1e-06
WEIGHT_DECAY = 0.01
GAIN_RATE = 0.5
MASKED = -1e30


LANES = 128
PIECES = 8
SLAB_PAD = 16
VMEM_BYTES = 52 * 1024 * 1024


def layout(lengths, token_index, group_rows):
    seq_ends = jnp.cumsum(lengths)
    seq_starts = seq_ends - lengths
    segment = jnp.sum((token_index[:, None] >= seq_ends[None, :]).astype(jnp.int32), axis=1)
    member = segment[:, None] == jnp.arange(lengths.shape[0])[None, :]
    position = token_index - jnp.sum(jnp.where(member, seq_starts[None, :], 0), axis=1)
    inside = (token_index >= 0) & (token_index < group_rows)
    return (jnp.where(inside, segment, -1), jnp.where(inside, position, 0))


def rotary_tables(position):
    half_dim = HEAD_DIM // 2
    exponent = jnp.arange(half_dim).astype(jnp.float32) * (2.0 / HEAD_DIM)
    inverse = jnp.power(jnp.float32(THETA_BASE), -exponent)
    angle_table = position.astype(jnp.float32)[:, None] * inverse[None, :]
    copies = LANES // half_dim
    return (jnp.tile(jnp.cos(angle_table), (1, copies)), jnp.tile(jnp.sin(angle_table), (1, copies)))


def windows(rows):
    count = (rows.shape[0] - 2 * HALF) // BLOCK
    return jnp.stack([rows[n * BLOCK : n * BLOCK + BLOCK + 2 * HALF] for n in range(count)])


def allowed_pairs(segment):
    key_seg = windows(segment)
    query_seg = segment[HALF:-HALF].reshape(-1, BLOCK)
    offset = jnp.arange(BLOCK)[:, None] + HALF - jnp.arange(BLOCK + 2 * HALF)[None, :]
    return (query_seg[:, :, None] == key_seg[:, None, :]) & (jnp.abs(offset) <= HALF)[None]


def adam_update(master, gradient, moment_one, moment_two, step_rate):
    one_new = BETA_ONE * moment_one + (1.0 - BETA_ONE) * gradient
    two_new = BETA_TWO * moment_two + (1.0 - BETA_TWO) * gradient * gradient
    one_hat = one_new / (1.0 - BETA_ONE**STEP)
    two_hat = two_new / (1.0 - BETA_TWO**STEP)
    master_new = master - step_rate * (
        one_hat / (jnp.sqrt(two_hat) + ADAM_EPS) + WEIGHT_DECAY * master
    )
    return (one_new, two_new, master_new)


def line_gather(slab):
    size = lax.axis_size("tensor")
    place = lax.axis_index("tensor")
    from_before, from_after = [slab], [slab]
    for step in range(1, size):
        from_before.append(
            lax.ppermute(from_before[-1], "tensor", [(n, n + 1) for n in range(step - 1, size - 1)])
        )
        from_after.append(
            lax.ppermute(from_after[-1], "tensor", [(n, n - 1) for n in range(1, size - step + 1)])
        )
    return jnp.stack(
        [slab]
        + [
            jnp.where(place >= step, from_before[step], from_after[size - step])
            for step in range(1, size)
        ]
    )


def line_scatter(parts):
    size = lax.axis_size("tensor")
    up, down = 0.0, 0.0
    for step in range(size - 1, 0, -1):
        to_after = (parts[size - step].astype(jnp.float32) + up).astype(parts.dtype)
        to_before = (parts[step].astype(jnp.float32) + down).astype(parts.dtype)
        up = lax.ppermute(to_after, "tensor", [(n, n + 1) for n in range(size - step)])
        down = lax.ppermute(to_before, "tensor", [(n, n - 1) for n in range(step, size)])
        up, down = up.astype(jnp.float32), down.astype(jnp.float32)
    return parts[0].astype(jnp.float32) + up + down


def flip(rows, mask):
    return lax.ppermute(rows, "dp", [(n, n ^ mask) for n in range(lax.axis_size("dp"))])


def far_bits():
    size = lax.axis_size("dp")
    return [1 << n for n in range(3, size.bit_length() - 1)]


def gather(slab, x_first):
    piece = line_gather(slab)
    piece = piece.reshape(-1, piece.shape[-1])
    for mask in far_bits():
        piece = jnp.concatenate([piece, flip(piece, mask)], axis=1)
    by_x, by_y = flip(piece, 2), flip(piece, 4)
    far = flip(by_x, 4) if x_first else flip(by_y, 2)
    mine = [piece, by_x, by_y, far]
    return (mine + [flip(part, 1) for part in mine], piece)


def add_low(left, right):
    return (left.astype(jnp.float32) + right.astype(jnp.float32)).astype(left.dtype)


def scatter(own, partner, x_first):
    received = flip(partner, 1)
    own, by_x, by_y, far = [add_low(mine, received[n]) for n, mine in enumerate(own)]
    if x_first:
        passed = flip(far, 2)
        by_y = add_low(by_y, passed)
    else:
        passed = flip(far, 4)
        by_x = add_low(by_x, passed)
    from_x, from_y = flip(by_x, 2), flip(by_y, 4)
    total = (
        own.astype(jnp.float32) + from_x.astype(jnp.float32) + from_y.astype(jnp.float32)
    ).astype(own.dtype)
    for mask in reversed(far_bits()):
        half = total.shape[1] // 2
        total = add_low(total[:, :half], flip(total[:, half:], mask))
    size = lax.axis_size("tensor")
    total = total.reshape(size, total.shape[0] // size, total.shape[1])
    return (total, (received, passed, from_x, from_y))


def to_relative(rows, back=False):
    size = lax.axis_size("dp")
    place = lax.axis_index("dp")
    bits = size.bit_length() - 1
    lead = rows.shape[:-1]
    axes = len(lead)
    chunk = rows.shape[-1] // size
    wanted = [bits - 1, bits - 3, bits - 2] + list(range(bits - 3))
    order = list(range(axes)) + [axes + n for n in wanted] + [axes + bits]
    cube = rows.reshape(lead + (2,) * bits + (chunk,))
    if back:
        cube = jnp.transpose(cube, [order.index(n) for n in range(len(order))])
    for n in range(bits):
        cube = jnp.where((place >> (bits - 1 - n)) & 1 == 1, jnp.flip(cube, axes + n), cube)
    if not back:
        cube = jnp.transpose(cube, order)
    return cube.reshape(rows.shape)


def shift(rows, step):
    size = lax.axis_size("tensor")
    pairs = [(n, n + step) for n in range(size) if 0 <= n + step < size]
    return lax.ppermute(rows, "tensor", pairs)


NN = ((1,), (0,))
NT = ((1,), (1,))
TN = ((0,), (0,))


def dot(left, right, dims):
    return lax.dot_general(left, right, (dims, ((), ())), preferred_element_type=jnp.float32)


def wide(pieces, rows):
    return jnp.concatenate([piece[0, rows, :] for piece in pieces], axis=1)


def relative(order, ref, rows):
    return jnp.concatenate(
        [
            ref[rows, pl.ds(pl.multiple_of(order[n] * LANES, LANES), LANES)]
            for n in range(PIECES)
        ],
        axis=1,
    )


def normed(values):
    centered = values - jnp.mean(values, axis=-1, keepdims=True)
    scale = lax.rsqrt(jnp.mean(centered * centered, axis=-1, keepdims=True) + NORM_EPS)
    return (centered * scale, scale)


def norm_pull(hat, scale, gain, grad):
    scaled = grad * gain
    return scale * (
        scaled
        - jnp.mean(scaled, axis=-1, keepdims=True)
        - hat * jnp.mean(scaled * hat, axis=-1, keepdims=True)
    )


def row_steps(count, size, body):
    def step(n, carried):
        body(pl.ds(pl.multiple_of(n * size, size), size))
        return carried

    lax.fori_loop(0, count // size, step, 0)


def whole_spec(array):
    return pl.BlockSpec(array.shape, lambda *_: (0,) * len(array.shape))


def run(kernel, name, operands, outs, scratch, flops, after=()):
    order, operands = operands[0], operands[1:]
    specs = [spec if spec is not None else whole_spec(array) for array, spec in operands]
    out_specs = [
        spec if spec is not None else pl.BlockSpec(shape, lambda *_, n=len(shape): (0,) * n)
        for shape, dtype, spec in outs
    ]
    moved = sum(array.size * array.dtype.itemsize for array, _ in operands)
    moved += sum(math.prod(shape) * jnp.dtype(dtype).itemsize for shape, dtype, _ in outs)
    kept = len(operands)

    def body(order_ref, *refs):
        kernel(order_ref, *refs[:kept], *refs[kept + len(after) :])

    return pl.pallas_call(
        body,
        grid_spec=pltpu.PrefetchScalarGridSpec(
            num_scalar_prefetch=1,
            grid=(lax.axis_size("tensor"),),
            in_specs=specs + [pl.BlockSpec(memory_space=pl.ANY)] * len(after),
            out_specs=out_specs,
            scratch_shapes=scratch,
        ),
        out_shape=[jax.ShapeDtypeStruct(shape, dtype) for shape, dtype, _ in outs],
        compiler_params=pltpu.CompilerParams(
            dimension_semantics=("arbitrary",), vmem_limit_bytes=VMEM_BYTES
        ),
        cost_estimate=pl.CostEstimate(flops=flops, bytes_accessed=moved, transcendentals=0),
        name=name,
    )(order, *[array for array, _ in operands], *after)


def slabs(piece, rows, first=0):
    return (piece, pl.BlockSpec((1, rows, LANES), lambda n, *_: (n, first, 0)))


def lead(array):
    shape = (1,) + array.shape[1:]
    return (array, pl.BlockSpec(shape, lambda n, *_: (n,) + (0,) * (len(shape) - 1)))


def lead_out(shape, dtype):
    return (shape, dtype, pl.BlockSpec((1,) + shape[1:], lambda n, *_: (n,) + (0,) * (len(shape) - 1)))


def piece_outs(parts, rows):
    low = jnp.bfloat16
    own = pl.BlockSpec((1, rows, LANES), lambda n, *_: (n, 0, 0))
    other = pl.BlockSpec((4, 1, rows, LANES), lambda n, *_: (0, n, 0, 0))
    return [((parts, rows, LANES), low, own)] * 4 + [((4, parts, rows, LANES), low, other)]


def store_pieces(refs, rows, values):
    values = values.astype(jnp.bfloat16)
    for n in range(4):
        refs[n][0, rows, :] = values[:, n * LANES : (n + 1) * LANES]
        refs[4][n, 0, rows, :] = values[:, (n + 4) * LANES : (n + 5) * LANES]


def heads_kernel(order, hidden, before, after, gains, cosine, sine, *refs):
    pieces, (q_out, k_out, v_out, rows_out, rows_wide) = refs[:PIECES], refs[PIECES:]
    row_count = hidden.shape[0]
    gain = gains[0:1, :]

    def norm_rows(source, rows, first):
        values = relative(order, source, rows).astype(jnp.float32)
        return (normed(values)[0] * gain).astype(jnp.bfloat16)

    @pl.when(pl.program_id(0) == 0)
    def _():
        rows_wide[0:HALF, :] = norm_rows(before, slice(0, HALF), 0)
        rows_wide[HALF + row_count :, :] = norm_rows(after, slice(0, HALF), 0)

        def one(rows):
            values = norm_rows(hidden, rows, 0)
            rows_out[rows, :] = values
            rows_wide[pl.ds(pl.multiple_of(rows.start + HALF, HALF), HALF), :] = values

        row_steps(row_count, HALF, one)

    width = 2 * LANES

    def turned(mixed, rows):
        front, back = mixed[:, :LANES], mixed[:, LANES:]
        cos, sin = cosine[rows, :], sine[rows, :]
        return (front * cos - back * sin, back * cos + front * sin)

    inner = slice(HALF, HALF + row_count)
    scale = HEAD_DIM ** (-0.5)
    front, back = turned(dot(rows_out[...], wide(pieces, slice(0, width)), NT), inner)
    q_out[0, :, :LANES] = (front.astype(jnp.bfloat16) * scale).astype(jnp.bfloat16)
    q_out[0, :, LANES:] = (back.astype(jnp.bfloat16) * scale).astype(jnp.bfloat16)
    front, back = turned(
        dot(rows_wide[...], wide(pieces, slice(width, 2 * width)), NT), slice(None)
    )
    k_out[0, :, :LANES] = front.astype(jnp.bfloat16)
    k_out[0, :, LANES:] = back.astype(jnp.bfloat16)
    v_out[0] = dot(rows_wide[...], wide(pieces, slice(2 * width, 3 * width)), NT).astype(
        jnp.bfloat16
    )


def head_masks():
    lane = lax.broadcasted_iota(jnp.int32, (1, 2 * LANES), 1)
    turned = [((lane % LANES) // 32 == n).astype(jnp.float32).astype(jnp.bfloat16) for n in range(4)]
    plain = [(lane // HEAD_DIM == n).astype(jnp.float32).astype(jnp.bfloat16) for n in range(4)]
    return (turned, plain)


def attend_kernel(order, bias, q_in, k_in, v_in, out, log_out):
    turned, plain = head_masks()
    lane = lax.broadcasted_iota(jnp.int32, (BLOCK, LANES), 1)

    def block(n, carried):
        rows = pl.ds(pl.multiple_of(n * BLOCK, BLOCK), BLOCK)
        span = pl.ds(pl.multiple_of(n * BLOCK, BLOCK), BLOCK + 2 * HALF)
        queries, keys, values = q_in[0, rows, :], k_in[0, span, :], v_in[0, span, :]
        masked = bias[n]
        total = jnp.zeros((BLOCK, 2 * LANES), jnp.float32)
        logs = jnp.zeros((BLOCK, LANES), jnp.float32)
        for h in range(4):
            scores = dot(queries * turned[h], keys, NT) + masked
            row_top = jnp.max(scores, axis=-1, keepdims=True)
            lifted = jnp.exp(scores - row_top)
            row_total = jnp.sum(lifted, axis=-1, keepdims=True)
            probs_low = (lifted * (1.0 / row_total)).astype(jnp.bfloat16)
            total = total + dot(probs_low, values * plain[h], NN)
            logs = jnp.where(lane == h, row_top + jnp.log(row_total), logs)
        out[0, rows, :] = total.astype(jnp.bfloat16)
        log_out[0, rows, :] = logs
        return carried

    lax.fori_loop(0, bias.shape[0], block, 0)


def proj_kernel(order, hidden, gains, attended, *refs):
    pieces, (middle, rows_two) = refs[:PIECES], refs[PIECES:]
    step = pl.program_id(0)

    @pl.when(step == 0)
    def _():
        def one(rows):
            middle[rows, :] = relative(order, hidden, rows).astype(jnp.float32)

        row_steps(hidden.shape[0], HALF, one)

    middle[...] += dot(attended[0], wide(pieces, slice(None)), NN)

    @pl.when(step == pl.num_programs(0) - 1)
    def _():
        def one(rows):
            rows_two[rows, :] = (normed(middle[rows, :])[0] * gains[1:2, :]).astype(jnp.bfloat16)

        row_steps(hidden.shape[0], HALF, one)


def gate_kernel(order, rows_two, *refs):
    pieces, (active, gate_side, up_side, rows_turned, gate, up) = refs[:PIECES], refs[PIECES:]

    @pl.when(pl.program_id(0) == 0)
    def _():
        rows_turned[...] = rows_two[...].T

    count = gate.shape[0]
    gate[...] = dot(wide(pieces, slice(0, count)), rows_turned[...], NN)
    up[...] = dot(wide(pieces, slice(count, 2 * count)), rows_turned[...], NN)

    def one(rows):
        x, u = gate[rows, :], up[rows, :]
        below = 0.5 * (1.0 + lax.erf(x * (0.5**0.5)))
        density = jnp.exp(-0.5 * x * x) * ((2.0 * math.pi) ** -0.5)
        lifted = x * below
        active[rows, :] = (lifted * u).astype(jnp.bfloat16)
        gate_side[rows, :] = (u * (below + x * density)).astype(jnp.bfloat16)
        up_side[rows, :] = lifted.astype(jnp.bfloat16)

    row_steps(count, 16, one)


def down_kernel(order, middle, active, *refs):
    pieces, (out, total) = refs[:PIECES], refs[PIECES:]
    step = pl.program_id(0)

    @pl.when(step == 0)
    def _():
        total[...] = middle[...]

    total[...] += dot(active[...], wide(pieces, slice(None)), TN)

    @pl.when(step == pl.num_programs(0) - 1)
    def _():
        for n in range(PIECES):
            lanes = pl.ds(pl.multiple_of(order[n] * LANES, LANES), LANES)
            out[:, lanes] = total[:, n * LANES : (n + 1) * LANES].astype(jnp.bfloat16)


def down_grad_kernel(order, cotangent, active, *refs):
    pieces, (cot_out,) = refs[:5], refs[5:]

    @pl.when(pl.program_id(0) == 0)
    def _():
        def one(rows):
            cot_out[rows, :] = relative(order, cotangent, rows)

        row_steps(cotangent.shape[0], HALF, one)

    store_pieces(pieces, slice(None), dot(active[...], cot_out[...], NN))


def in_grad_kernel(order, cot, rows_two, gate_side, up_side, *refs):
    pieces, grads = refs[:PIECES], refs[PIECES : PIECES + 5]
    gate_out, up_out, cot_turned, grad_active = refs[PIECES + 5 :]

    @pl.when(pl.program_id(0) == 0)
    def _():
        cot_turned[...] = cot[...].T

    count = grad_active.shape[0]
    grad_active[...] = dot(wide(pieces, slice(None)), cot_turned[...], NN)

    def one(rows):
        grad = grad_active[rows, :]
        gate_out[rows, :] = (grad * gate_side[rows, :].astype(jnp.float32)).astype(jnp.bfloat16)
        up_out[rows, :] = (grad * up_side[rows, :].astype(jnp.float32)).astype(jnp.bfloat16)

    row_steps(count, 16, one)
    store_pieces(grads, slice(0, count), dot(gate_out[...], rows_two[...], NN))
    store_pieces(grads, slice(count, 2 * count), dot(up_out[...], rows_two[...], NN))


def middle_grad_kernel(order, middle, cot, gains, gate_grad, up_grad, *refs):
    pieces, (grad_middle, grad_low, gain_out, total) = refs[:PIECES], refs[PIECES:]
    step = pl.program_id(0)
    count = gate_grad.shape[0]

    @pl.when(step == 0)
    def _():
        total[...] = jnp.zeros_like(total)
        gain_out[...] = jnp.zeros_like(gain_out)

    total[...] += dot(gate_grad[...], wide(pieces, slice(0, count)), TN)
    total[...] += dot(up_grad[...], wide(pieces, slice(count, 2 * count)), TN)

    @pl.when(step == pl.num_programs(0) - 1)
    def _():
        def one(rows):
            grad = total[rows, :]
            hat, scale = normed(middle[rows, :])
            result = cot[rows, :].astype(jnp.float32) + norm_pull(hat, scale, gains[1:2, :], grad)
            grad_middle[rows, :] = result
            grad_low[rows, :] = result.astype(jnp.bfloat16)
            gain_out[0:1, :] += jnp.sum(grad * hat, axis=0, keepdims=True)

        row_steps(middle.shape[0], HALF, one)


def attend_grad_kernel(order, bias, cosine, sine, grad_low, q_in, k_in, v_in, logs, *refs):
    pieces, (grads, edges, grad_keys, grad_values, grad_out) = refs[:PIECES], refs[PIECES:]
    turned, plain = head_masks()
    row_count = grad_low.shape[0]
    low = jnp.bfloat16
    grad_out[...] = dot(grad_low[...], wide(pieces, slice(None)), NT).astype(low)
    grad_keys[...] = jnp.zeros_like(grad_keys)
    grad_values[...] = jnp.zeros_like(grad_values)

    def back(values, rows):
        front, rear = values[:, :LANES], values[:, LANES:]
        cos, sin = cosine[rows, :], sine[rows, :]
        return (front * cos + rear * sin, rear * cos - front * sin)

    def block(n, carried):
        rows = pl.ds(pl.multiple_of(n * BLOCK, BLOCK), BLOCK)
        span = pl.ds(pl.multiple_of(n * BLOCK, BLOCK), BLOCK + 2 * HALF)
        queries, keys, values = q_in[0, rows, :], k_in[0, span, :], v_in[0, span, :]
        grad_rows = grad_out[rows, :]
        masked = bias[n]
        log_rows = logs[0, rows, :]
        grad_query = jnp.zeros((BLOCK, 2 * LANES), jnp.float32)
        grad_key = jnp.zeros((BLOCK + 2 * HALF, 2 * LANES), jnp.float32)
        grad_value = jnp.zeros((BLOCK + 2 * HALF, 2 * LANES), jnp.float32)
        for h in range(4):
            query_head, grad_head = queries * turned[h], grad_rows * plain[h]
            scores = dot(query_head, keys, NT) + masked
            probs = jnp.exp(scores - log_rows[:, h : h + 1])
            grad_probs = dot(grad_head, values, NT)
            row_delta = jnp.sum(probs * grad_probs, axis=-1, keepdims=True)
            grad_scores = (probs * (grad_probs - row_delta)).astype(low)
            grad_query = grad_query + dot(grad_scores, keys * turned[h], NN)
            grad_key = grad_key + dot(grad_scores, query_head, TN)
            grad_value = grad_value + dot(probs.astype(low), grad_head, TN)
        place = pl.ds(pl.multiple_of(n * BLOCK + HALF, HALF), BLOCK)
        front, rear = back(grad_query * HEAD_DIM ** (-0.5), place)
        grads[0, 0, rows, :LANES] = front.astype(low)
        grads[0, 0, rows, LANES:] = rear.astype(low)
        grad_keys[span, :] += grad_key
        grad_values[span, :] += grad_value
        return carried

    lax.fori_loop(0, bias.shape[0], block, 0)
    inner = slice(HALF, HALF + row_count)
    for rows, out in (
        (inner, lambda n: grads.at[0, 1 + n]),
        (slice(0, HALF), lambda n: edges.at[0, 0, n]),
        (slice(HALF + row_count, None), lambda n: edges.at[0, 1, n]),
    ):
        front, rear = back(grad_keys[rows, :], rows)
        out(0)[:, :LANES] = front.astype(low)
        out(0)[:, LANES:] = rear.astype(low)
        out(1)[...] = grad_values[rows, :].astype(low)


def heads_grad_kernel(
    order, hidden, gains, gain_two, grad_middle, grad_low, rows_one, attended, grads, before, after, *refs
):
    pieces, outs = refs[:PIECES], refs[PIECES : PIECES + 5]
    grad_input, mixed, total, gain_one = refs[PIECES + 5 :]
    step = pl.program_id(0)
    row_count = hidden.shape[0]
    width = 2 * LANES
    last = row_count - HALF

    @pl.when(step == 0)
    def _():
        total[...] = jnp.zeros_like(total)
        gain_one[...] = jnp.zeros_like(gain_one)

    def add_low(left, right):
        return (left.astype(jnp.float32) + right.astype(jnp.float32)).astype(jnp.bfloat16)

    mixed[...] = grads[0]
    for c in range(2):
        mixed[1 + c, 0:HALF, :] = add_low(grads[0, 1 + c, 0:HALF, :], before[0, c])
        mixed[1 + c, last:, :] = add_low(grads[0, 1 + c, last:, :], after[0, c])
    for c in range(3):
        rows = slice(c * width, (c + 1) * width)
        total[...] += dot(mixed[c], wide(pieces, rows), NN)
        store_pieces(outs, rows, dot(mixed[c], rows_one[...], TN))
    store_pieces(outs, slice(3 * width, 4 * width), dot(attended[0], grad_low[...], TN))
    tail = slice(4 * width, 4 * width + SLAB_PAD)
    store_pieces(outs, tail, jnp.zeros((SLAB_PAD, PIECES * LANES), jnp.float32))

    @pl.when(step == pl.num_programs(0) - 1)
    def _():
        def one(rows):
            grad = total[rows, :]
            hat, scale = normed(relative(order, hidden, rows).astype(jnp.float32))
            result = grad_middle[rows, :] + norm_pull(hat, scale, gains[0:1, :], grad)
            for n in range(PIECES):
                lanes = pl.ds(pl.multiple_of(order[n] * LANES, LANES), LANES)
                grad_input[rows, lanes] = result[:, n * LANES : (n + 1) * LANES]
            gain_one[0:1, :] += jnp.sum(grad * hat, axis=0, keepdims=True)

        row_steps(row_count, HALF, one)
        both = jnp.concatenate(
            [gain_one[0:1, :], gain_two[0:1, :], jnp.zeros((SLAB_PAD - 2, PIECES * LANES), jnp.float32)],
            axis=0,
        )
        store_pieces(outs, tail, both)


def local(
    hidden_in,
    seq_lengths,
    cotangent,
    w_qkv,
    w_proj,
    w_in,
    w_down,
    norm_gains,
    qkv_first,
    qkv_second,
    proj_first,
    proj_second,
    in_first,
    in_second,
    down_first,
    down_second,
    gain_first,
    gain_second,
):
    row_count = hidden_in.shape[0]
    wide_count = row_count + 2 * HALF
    size = lax.axis_size("tensor")
    dp_size = lax.axis_size("dp")
    group_rows = row_count * size
    low, full = jnp.bfloat16, jnp.float32
    chunk = norm_gains.shape[1]
    head_wide = w_proj.shape[1]
    head_rows = 4 * head_wide
    slab_rows = head_rows + SLAB_PAD
    hidden_wide = w_down.shape[1]
    head_count, half_dim = head_wide // HEAD_DIM, HEAD_DIM // 2

    def halves_first(weight):
        split = weight.reshape(chunk, 2, head_count, 2, half_dim)
        return jnp.transpose(split, (0, 1, 3, 2, 4)).reshape(chunk, 2 * head_wide)

    def heads_first(weight):
        split = weight.reshape(chunk, 2, 2, head_count, half_dim)
        return jnp.transpose(split, (0, 1, 3, 2, 4)).reshape(chunk, 2, head_wide)

    heads_slab = jnp.concatenate(
        [
            jnp.concatenate(
                [halves_first(w_qkv[:, :2].astype(low)), w_qkv[:, 2].astype(low), w_proj.astype(low)],
                axis=1,
            ).T,
            jnp.pad(norm_gains.astype(low), ((0, SLAB_PAD - 2), (0, 0))),
        ]
    )
    in_slab = w_in.astype(low).reshape(chunk, 2 * hidden_wide).T
    down_slab = w_down.astype(low).T
    if dp_size == PIECES:
        place = jnp.array([0, 2, 4, 6, 1, 3, 5, 7], jnp.int32)
        order = lax.axis_index("dp").astype(jnp.int32) ^ place
        hidden, cot_in = hidden_in, cotangent
    else:
        order = jnp.arange(PIECES, dtype=jnp.int32)
        hidden, cot_in = to_relative(hidden_in), to_relative(cotangent)

    edges = (shift(hidden[-HALF:], 1), shift(hidden[:HALF], -1))
    heads_pieces, heads_line = gather(heads_slab, True)
    in_pieces, in_line = gather(in_slab, False)
    down_pieces, down_line = gather(down_slab, True)
    heads_pieces = [piece.reshape(size, -1, LANES) for piece in heads_pieces]
    in_pieces = [piece.reshape(size, -1, LANES) for piece in in_pieces]
    down_pieces = [piece.reshape(size, -1, LANES) for piece in down_pieces]
    gains = jnp.concatenate(
        [piece[0, head_rows : head_rows + 8] for piece in heads_pieces], axis=1
    ).astype(full)

    first_row = lax.axis_index("tensor") * row_count
    segment, position = layout(
        seq_lengths[0], first_row - HALF + jnp.arange(wide_count), group_rows
    )
    cosine, sine = rotary_tables(position)
    bias = jnp.where(allowed_pairs(segment), 0.0, MASKED).astype(full)

    head_block = (size, row_count, head_wide)
    wide_block = (size, wide_count, head_wide)
    tokens = (row_count, D)
    turned = (size * hidden_wide, row_count)
    turned_spec = pl.BlockSpec((hidden_wide, row_count), lambda n, *_: (n, 0))
    matmul = 2 * row_count * D

    queries, keys, values, rows_one = run(
        heads_kernel,
        "heads",
        [order, (hidden, None), (edges[0], None), (edges[1], None), (gains, None)]
        + [(cosine, None), (sine, None)]
        + [slabs(piece, 3 * head_wide) for piece in heads_pieces],
        [lead_out(head_block, low), lead_out(wide_block, low), lead_out(wide_block, low)]
        + [(tokens, low, None)],
        [pltpu.VMEM((wide_count, D), low)],
        3 * matmul * D,
        after=(in_line, down_line),
    )
    attended, logs = run(
        attend_kernel,
        "attend",
        [order, (bias, None), lead(queries), lead(keys), lead(values)],
        [lead_out(head_block, low), lead_out((size, row_count, LANES), full)],
        [],
        2 * matmul * D,
    )
    middle, rows_two = run(
        proj_kernel,
        "proj",
        [order, (hidden, None), (gains, None), lead(attended)]
        + [slabs(piece, head_wide, 3) for piece in heads_pieces],
        [(tokens, full, None), (tokens, low, None)],
        [],
        matmul * D,
    )
    active, gate_side, up_side = run(
        gate_kernel,
        "gate",
        [order, (rows_two, None)] + [slabs(piece, 2 * hidden_wide) for piece in in_pieces],
        [(turned, low, turned_spec)] * 3,
        [
            pltpu.VMEM((D, row_count), low),
            pltpu.VMEM((hidden_wide, row_count), full),
            pltpu.VMEM((hidden_wide, row_count), full),
        ],
        2 * matmul * FF,
    )

    *down_own, down_partner, cot = run(
        down_grad_kernel,
        "down_grad",
        [order, (cot_in, None), (active, turned_spec)],
        piece_outs(size, hidden_wide) + [(tokens, low, None)],
        [],
        matmul * FF,
    )
    flat = lambda part: part.reshape(-1, LANES)
    flat_four = lambda part: part.reshape(4, -1, LANES)
    down_total, down_steps = scatter([flat(p) for p in down_own], flat_four(down_partner), True)
    *in_own, in_partner, gate_grad, up_grad = run(
        in_grad_kernel,
        "in_grad",
        [order, (cot, None), (rows_two, None), (gate_side, turned_spec), (up_side, turned_spec)]
        + [slabs(piece, hidden_wide) for piece in down_pieces],
        piece_outs(size, 2 * hidden_wide) + [(turned, low, turned_spec)] * 2,
        [pltpu.VMEM((D, row_count), low), pltpu.VMEM((hidden_wide, row_count), full)],
        3 * matmul * FF,
    )
    in_total, in_steps = scatter([flat(p) for p in in_own], flat_four(in_partner), False)
    grad_middle, grad_low, gain_two = run(
        middle_grad_kernel,
        "middle_grad",
        [order, (middle, None), (cot, None), (gains, None)]
        + [(gate_grad, turned_spec), (up_grad, turned_spec)]
        + [slabs(piece, 2 * hidden_wide) for piece in in_pieces],
        [(tokens, full, None), (tokens, low, None), ((8, D), full, None)],
        [pltpu.VMEM(tokens, full)],
        2 * matmul * FF,
        after=down_steps[:1],
    )
    grads, edge_grads = run(
        attend_grad_kernel,
        "attend_grad",
        [order, (bias, None), (cosine, None), (sine, None), (grad_low, None)]
        + [lead(queries), lead(keys), lead(values), lead(logs)]
        + [slabs(piece, head_wide, 3) for piece in heads_pieces],
        [
            lead_out((size, 3, row_count, head_wide), low),
            lead_out((size, 2, 2, HALF, head_wide), low),
        ],
        [
            pltpu.VMEM((wide_count, head_wide), full),
            pltpu.VMEM((wide_count, head_wide), full),
            pltpu.VMEM((row_count, head_wide), low),
        ],
        5 * matmul * D,
        after=(down_steps[1], in_steps[0]),
    )
    grads_before = jnp.roll(shift(edge_grads[:, 1], 1), 1, axis=0)
    grads_after = jnp.roll(shift(edge_grads[:, 0], -1), -1, axis=0)
    *heads_own, heads_partner, grad_input = run(
        heads_grad_kernel,
        "heads_grad",
        [order, (hidden, None), (gains, None), (gain_two, None), (grad_middle, None)]
        + [(grad_low, None), (rows_one, None), lead(attended), lead(grads)]
        + [lead(grads_before), lead(grads_after)]
        + [slabs(piece, 3 * head_wide) for piece in heads_pieces],
        piece_outs(size, slab_rows) + [(tokens, full, None)],
        [
            pltpu.VMEM((3, row_count, head_wide), low),
            pltpu.VMEM(tokens, full),
            pltpu.VMEM((8, D), full),
        ],
        7 * matmul * D,
        after=down_steps[2:] + in_steps[1:2],
    )
    heads_total, heads_steps = scatter([flat(p) for p in heads_own], flat_four(heads_partner), True)
    (hidden_out,) = run(
        down_kernel,
        "down",
        [order, (middle, None), (active, turned_spec)]
        + [slabs(piece, hidden_wide) for piece in down_pieces],
        [(tokens, low, None)],
        [pltpu.VMEM(tokens, full)],
        matmul * FF,
        after=heads_steps[:1],
    )
    if dp_size != PIECES:
        hidden_out, grad_input = to_relative(hidden_out, True), to_relative(grad_input, True)

    down_sum = line_scatter(down_total).T
    in_sum = line_scatter(in_total).T.reshape(w_in.shape)
    gain_sum = heads_total[size - 1, head_rows : head_rows + 2].astype(full)
    for mask in (1 << n for n in range(size.bit_length() - 1)):
        gain_sum = gain_sum + lax.ppermute(
            gain_sum, "tensor", [(n, n ^ mask) for n in range(size)]
        )
    heads_sum = line_scatter(heads_total[:, :head_rows]).T
    qkv_sum = jnp.concatenate(
        [
            heads_first(heads_sum[:, : 2 * head_wide]),
            heads_sum[:, None, 2 * head_wide : 3 * head_wide],
        ],
        axis=1,
    )
    proj_sum = heads_sum[:, 3 * head_wide :]
    qkv_one, qkv_two, qkv_new = adam_update(w_qkv, qkv_sum, qkv_first, qkv_second, D ** (-0.5))
    proj_one, proj_two, proj_new = adam_update(
        w_proj, proj_sum, proj_first, proj_second, (D // HALF) ** (-0.5)
    )
    in_one, in_two, in_new = adam_update(w_in, in_sum, in_first, in_second, D ** (-0.5))
    down_one, down_two, down_new = adam_update(
        w_down, down_sum, down_first, down_second, (FF // 2) ** (-0.5)
    )
    gain_one, gain_two, gains_new = adam_update(
        norm_gains, gain_sum, gain_first, gain_second, GAIN_RATE
    )
    return (
        hidden_out,
        grad_input,
        qkv_one,
        qkv_two,
        qkv_new,
        proj_one,
        proj_two,
        proj_new,
        in_one,
        in_two,
        in_new,
        down_one,
        down_two,
        down_new,
        gain_one,
        gain_two,
        gains_new,
    )


def solution(mesh):
    placed = (
        P(("dp", "tensor"), None),
        P("dp", None),
        P(("dp", "tensor"), None),
        P("dp", None, "tensor"),
        P("dp", "tensor"),
        P("dp", None, "tensor"),
        P("dp", "tensor"),
        P(None, "dp"),
        P("dp", None, "tensor"),
        P("dp", None, "tensor"),
        P("dp", "tensor"),
        P("dp", "tensor"),
        P("dp", None, "tensor"),
        P("dp", None, "tensor"),
        P("dp", "tensor"),
        P("dp", "tensor"),
        P(None, "dp"),
        P(None, "dp"),
    )
    return jax.shard_map(
        local,
        mesh=mesh,
        in_specs=placed,
        out_specs=(
            P(("dp", "tensor"), None),
            P(("dp", "tensor"), None),
            P("dp", None, "tensor"),
            P("dp", None, "tensor"),
            P("dp", None, "tensor"),
            P("dp", "tensor"),
            P("dp", "tensor"),
            P("dp", "tensor"),
            P("dp", None, "tensor"),
            P("dp", None, "tensor"),
            P("dp", None, "tensor"),
            P("dp", "tensor"),
            P("dp", "tensor"),
            P("dp", "tensor"),
            P(None, "dp"),
            P(None, "dp"),
            P(None, "dp"),
        ),
        check_vma=False,
    )
```

```python
import functools
import math

import jax
import jax.numpy as jnp
from jax import lax
from jax.experimental import pallas as pl
from jax.experimental.pallas import tpu as pltpu
from jax.sharding import PartitionSpec as P

D = 1024
HEADS = 16
HEAD_DIM = 64
FF = 2624
HALF = 64
BLOCK = 128
STEP = 10

NORM_EPS = 1e-05
THETA_BASE = 10000.0
BETA_ONE = 0.9
BETA_TWO = 0.98
ADAM_EPS = 1e-06
WEIGHT_DECAY = 0.01
GAIN_RATE = 0.5
MASKED = -1e30


LANES = 128
PIECES = 8
SLAB_PAD = 16
VMEM_BYTES = 52 * 1024 * 1024
COST_FACTOR = 100


def layout(lengths, token_index, group_rows):
    seq_ends = jnp.cumsum(lengths)
    seq_starts = seq_ends - lengths
    segment = jnp.sum((token_index[:, None] >= seq_ends[None, :]).astype(jnp.int32), axis=1)
    member = segment[:, None] == jnp.arange(lengths.shape[0])[None, :]
    position = token_index - jnp.sum(jnp.where(member, seq_starts[None, :], 0), axis=1)
    inside = (token_index >= 0) & (token_index < group_rows)
    return (jnp.where(inside, segment, -1), jnp.where(inside, position, 0))


def rotary_tables(position):
    half_dim = HEAD_DIM // 2
    exponent = jnp.arange(half_dim).astype(jnp.float32) * (2.0 / HEAD_DIM)
    inverse = jnp.power(jnp.float32(THETA_BASE), -exponent)
    angle_table = position.astype(jnp.float32)[:, None] * inverse[None, :]
    copies = LANES // half_dim
    return (jnp.tile(jnp.cos(angle_table), (1, copies)), jnp.tile(jnp.sin(angle_table), (1, copies)))


def windows(rows):
    count = (rows.shape[0] - 2 * HALF) // BLOCK
    return jnp.stack([rows[n * BLOCK : n * BLOCK + BLOCK + 2 * HALF] for n in range(count)])


def allowed_pairs(segment):
    key_seg = windows(segment)
    query_seg = segment[HALF:-HALF].reshape(-1, BLOCK)
    offset = jnp.arange(BLOCK)[:, None] + HALF - jnp.arange(BLOCK + 2 * HALF)[None, :]
    return (query_seg[:, :, None] == key_seg[:, None, :]) & (jnp.abs(offset) <= HALF)[None]


def adam_update(master, gradient, moment_one, moment_two, step_rate):
    one_new = BETA_ONE * moment_one + (1.0 - BETA_ONE) * gradient
    two_new = BETA_TWO * moment_two + (1.0 - BETA_TWO) * gradient * gradient
    one_hat = one_new / (1.0 - BETA_ONE**STEP)
    two_hat = two_new / (1.0 - BETA_TWO**STEP)
    master_new = master - step_rate * (
        one_hat / (jnp.sqrt(two_hat) + ADAM_EPS) + WEIGHT_DECAY * master
    )
    return (one_new, two_new, master_new)


def line_gather(slab, place):
    size = lax.axis_size("tensor")
    from_before, from_after = [slab], [slab]
    for step in range(1, size):
        from_before.append(
            lax.ppermute(from_before[-1], "tensor", [(n, n + 1) for n in range(step - 1, size - 1)])
        )
        from_after.append(
            lax.ppermute(from_after[-1], "tensor", [(n, n - 1) for n in range(1, size - step + 1)])
        )
    return jnp.stack(
        [slab]
        + [
            jnp.where(place >= step, from_before[step], from_after[size - step])
            for step in range(1, size)
        ]
    )


def tied(values, token):
    return values if token is None else jnp.where(token[0, 0] == 0, values, 0.0 * values)


def line_hop(to_after, to_before, step):
    size = lax.axis_size("tensor")
    return (
        lax.ppermute(to_after, "tensor", [(n, n + 1) for n in range(size - step)]),
        lax.ppermute(to_before, "tensor", [(n, n - 1) for n in range(step, size)]),
    )


def line_end(own, arrived):
    return sum((part.astype(jnp.float32) for part in arrived), own.astype(jnp.float32))


def gain_scatter(gains):
    for mask in [1, 4, 2] + far_bits()[::-1]:
        half = gains.shape[1] // 2
        gains = gains[:, :half] + flip(gains[:, half:], mask)
    size = lax.axis_size("tensor")
    for mask in (1 << n for n in range(size.bit_length() - 1)):
        gains = gains + lax.ppermute(gains, "tensor", [(n, n ^ mask) for n in range(size)])
    return gains


def flip(rows, mask):
    return lax.ppermute(rows, "dp", [(n, n ^ mask) for n in range(lax.axis_size("dp"))])


def far_bits():
    size = lax.axis_size("dp")
    return [1 << n for n in range(3, size.bit_length() - 1)]


def gather_near(slab, place):
    piece = line_gather(slab, place)
    piece = piece.reshape(-1, piece.shape[-1])
    for mask in far_bits():
        piece = jnp.concatenate([piece, flip(piece, mask)], axis=1)
    return (piece, flip(piece, 2), flip(piece, 4))


def gather_far(near, x_first, token=None, core_token=None):
    piece, by_x, by_y = near
    far = flip(tied(by_x, token), 4) if x_first else flip(tied(by_y, token), 2)
    mine = [piece, by_x, by_y, tied(far, core_token)]
    return mine + [flip(part, 1) for part in mine]


def add_low(left, right):
    return (left.astype(jnp.float32) + right.astype(jnp.float32)).astype(left.dtype)


def far_scatter(part):
    for mask in reversed(far_bits()):
        half = part.shape[1] // 2
        part = add_low(part[:, :half], flip(part[:, half:], mask))
    return part


def to_relative(rows, back=False):
    size = lax.axis_size("dp")
    place = lax.axis_index("dp")
    bits = size.bit_length() - 1
    lead = rows.shape[:-1]
    axes = len(lead)
    chunk = rows.shape[-1] // size
    wanted = [bits - 1, bits - 3, bits - 2] + list(range(bits - 3))
    order = list(range(axes)) + [axes + n for n in wanted] + [axes + bits]
    cube = rows.reshape(lead + (2,) * bits + (chunk,))
    if back:
        cube = jnp.transpose(cube, [order.index(n) for n in range(len(order))])
    for n in range(bits):
        cube = jnp.where((place >> (bits - 1 - n)) & 1 == 1, jnp.flip(cube, axes + n), cube)
    if not back:
        cube = jnp.transpose(cube, order)
    return cube.reshape(rows.shape)


def shift(rows, step):
    size = lax.axis_size("tensor")
    pairs = [(n, n + step) for n in range(size) if 0 <= n + step < size]
    return lax.ppermute(rows, "tensor", pairs)


NN = ((1,), (0,))
NT = ((1,), (1,))
TN = ((0,), (0,))


def dot(left, right, dims):
    return lax.dot_general(left, right, (dims, ((), ())), preferred_element_type=jnp.float32)


def wide(pieces, rows, slab=0):
    return jnp.concatenate([piece[slab, rows, :] for piece in pieces], axis=1)


def relative(order, ref, rows):
    return jnp.concatenate(
        [
            ref[rows, pl.ds(pl.multiple_of(order[n] * LANES, LANES), LANES)]
            for n in range(PIECES)
        ],
        axis=1,
    )


def normed(values):
    centered = values - jnp.mean(values, axis=-1, keepdims=True)
    scale = lax.rsqrt(jnp.mean(centered * centered, axis=-1, keepdims=True) + NORM_EPS)
    return (centered * scale, scale)


def norm_pull(hat, scale, gain, grad):
    scaled = grad * gain
    return scale * (
        scaled
        - jnp.mean(scaled, axis=-1, keepdims=True)
        - hat * jnp.mean(scaled * hat, axis=-1, keepdims=True)
    )


def row_steps(count, size, body):
    def step(n, carried):
        body(pl.ds(pl.multiple_of(n * size, size), size))
        return carried

    lax.fori_loop(0, count // size, step, 0)


def whole_spec(array):
    return pl.BlockSpec(array.shape, lambda *_: (0,) * len(array.shape))


def run(kernel, name, operands, outs, scratch, flops, after=(), steps=None):
    order, operands = operands[0], operands[1:]
    specs = [spec if spec is not None else whole_spec(array) for array, spec in operands]
    out_specs = [
        spec if spec is not None else pl.BlockSpec(shape, lambda *_, n=len(shape): (0,) * n)
        for shape, dtype, spec in outs
    ]
    moved = sum(array.size * array.dtype.itemsize for array, _ in operands)
    moved += sum(math.prod(shape) * jnp.dtype(dtype).itemsize for shape, dtype, _ in outs)
    kept, made = len(operands), len(outs)

    def body(order_ref, *refs):
        refs = refs[:kept] + refs[kept + len(after) :]
        token = refs[kept + made]
        token[...] = jnp.zeros_like(token)
        kernel(order_ref, *refs[: kept + made], *refs[kept + made + 1 :])

    return pl.pallas_call(
        body,
        grid_spec=pltpu.PrefetchScalarGridSpec(
            num_scalar_prefetch=1,
            grid=(steps or lax.axis_size("tensor"),),
            in_specs=specs + [pl.BlockSpec(memory_space=pl.ANY)] * len(after),
            out_specs=out_specs + [pl.BlockSpec((8, LANES), lambda *_: (0, 0))],
            scratch_shapes=scratch,
        ),
        out_shape=[jax.ShapeDtypeStruct(shape, dtype) for shape, dtype, _ in outs]
        + [jax.ShapeDtypeStruct((8, LANES), jnp.int32)],
        compiler_params=pltpu.CompilerParams(
            dimension_semantics=("arbitrary",), vmem_limit_bytes=VMEM_BYTES
        ),
        cost_estimate=pl.CostEstimate(
            flops=COST_FACTOR * flops, bytes_accessed=moved, transcendentals=0
        ),
        name=name,
    )(order, *[array for array, _ in operands], *after)


def held_back(value, after):
    def body(value_ref, *refs):
        refs[-1][...] = value_ref[...]

    return pl.pallas_call(
        body,
        in_specs=[pl.BlockSpec(memory_space=pltpu.VMEM)]
        + [pl.BlockSpec(memory_space=pl.ANY)] * len(after),
        out_specs=pl.BlockSpec(memory_space=pltpu.VMEM),
        out_shape=jax.ShapeDtypeStruct(value.shape, value.dtype),
        name="held_back",
    )(value, *after)


def blend(name, jobs, after):
    halves = 2
    operands, specs, out_specs, shapes, counts, cut = [], [], [], [], [], []
    for terms in jobs:
        rows, lanes = terms[0][0].shape[-2:]
        small = rows % (16 * halves) != 0 or rows < 512
        height = rows if small else rows // halves
        for term in terms:
            operands.append(term[0])
            if len(term) == 1:
                specs.append(pl.BlockSpec((height, lanes), lambda i, s=small: (0 if s else i, 0)))
            else:
                specs.append(
                    pl.BlockSpec(
                        (None, height, lanes),
                        lambda i, s=small, n=term[1]: (n, 0 if s else i, 0),
                    )
                )
        out_specs.append(pl.BlockSpec((height, lanes), lambda i, s=small: (0 if s else i, 0)))
        shapes.append(jax.ShapeDtypeStruct((rows, lanes), jnp.bfloat16))
        counts.append(len(terms))
        cut.append(small)

    def body(*refs):
        ins = refs[: len(operands)]
        outs = refs[len(operands) + len(after) :]
        outs[-1][...] = jnp.zeros_like(outs[-1])
        first = 0
        for n, count in enumerate(counts):
            terms = ins[first : first + count]
            first += count

            def add(out=outs[n], terms=terms):
                out[...] = sum(
                    (term[...].astype(jnp.float32) for term in terms[1:]),
                    terms[0][...].astype(jnp.float32),
                ).astype(jnp.bfloat16)

            pl.when((pl.program_id(0) == 0) | (not cut[n]))(add)

    *sums, token = pl.pallas_call(
        body,
        grid=(halves,),
        in_specs=specs + [pl.BlockSpec(memory_space=pl.ANY)] * len(after),
        out_specs=out_specs + [pl.BlockSpec((8, LANES), lambda i: (0, 0))],
        out_shape=shapes + [jax.ShapeDtypeStruct((8, LANES), jnp.int32)],
        compiler_params=pltpu.CompilerParams(
            dimension_semantics=("arbitrary",), vmem_limit_bytes=VMEM_BYTES
        ),
        name=name,
    )(*operands, *after)
    return (sums, token)


ALL, ODD, EVEN, SECOND, OWN = (0, 1), (1, 2), (0, 2), (2, 1), (0, 1)


def slabs(piece, rows, part=ALL, first=0, count=1):
    return (
        piece,
        pl.BlockSpec((count, rows, LANES), lambda n, *_: (part[0] + part[1] * n, first, 0)),
    )


def lead(array, part=ALL, count=1):
    shape = (count,) + array.shape[1:]
    return (
        array,
        pl.BlockSpec(shape, lambda n, *_: (part[0] + part[1] * n,) + (0,) * (len(shape) - 1)),
    )


def turned_block(array, rows, part=ALL):
    return (array, pl.BlockSpec((rows, array.shape[1]), lambda n, *_: (part[0] + part[1] * n, 0)))


def lead_out(shape, dtype):
    return (shape, dtype, pl.BlockSpec((1,) + shape[1:], lambda n, *_: (n,) + (0,) * (len(shape) - 1)))


def piece_outs(parts, rows):
    low = jnp.bfloat16
    own = pl.BlockSpec((1, rows, LANES), lambda n, *_: (n, 0, 0))
    other = pl.BlockSpec((4, 1, rows, LANES), lambda n, *_: (0, n, 0, 0))
    return [((parts, rows, LANES), low, own)] * 4 + [((4, parts, rows, LANES), low, other)]


def store_pieces(refs, rows, values):
    values = values.astype(jnp.bfloat16)
    for n in range(4):
        refs[n][0, rows, :] = values[:, n * LANES : (n + 1) * LANES]
        refs[4][n, 0, rows, :] = values[:, (n + 4) * LANES : (n + 5) * LANES]


def heads_kernel(order, hidden, before, after, gains, cosine, sine, *refs):
    pieces, (q_out, k_out, v_out, rows_wide) = refs[:PIECES], refs[PIECES:]
    row_count = hidden.shape[0]
    gain = gains[0:1, :]

    def norm_rows(source, rows, first):
        values = relative(order, source, rows).astype(jnp.float32)
        return (normed(values)[0] * gain).astype(jnp.bfloat16)

    @pl.when(pl.program_id(0) == 0)
    def _():
        rows_wide[0:HALF, :] = norm_rows(before, slice(0, HALF), 0)
        rows_wide[HALF + row_count :, :] = norm_rows(after, slice(0, HALF), 0)

        def one(rows):
            values = norm_rows(hidden, rows, 0)
            rows_wide[pl.ds(pl.multiple_of(rows.start + HALF, HALF), HALF), :] = values

        row_steps(row_count, HALF, one)

    width = 2 * LANES

    def turned(mixed, rows):
        front, back = mixed[:, :LANES], mixed[:, LANES:]
        cos, sin = cosine[rows, :], sine[rows, :]
        return (front * cos - back * sin, back * cos + front * sin)

    inner = slice(HALF, HALF + row_count)
    scale = HEAD_DIM ** (-0.5)
    front, back = turned(dot(rows_wide[inner, :], wide(pieces, slice(0, width)), NT), inner)
    q_out[0, :, :LANES] = (front.astype(jnp.bfloat16) * scale).astype(jnp.bfloat16)
    q_out[0, :, LANES:] = (back.astype(jnp.bfloat16) * scale).astype(jnp.bfloat16)
    front, back = turned(
        dot(rows_wide[...], wide(pieces, slice(width, 2 * width)), NT), slice(None)
    )
    k_out[0, :, :LANES] = front.astype(jnp.bfloat16)
    k_out[0, :, LANES:] = back.astype(jnp.bfloat16)
    v_out[0] = dot(rows_wide[...], wide(pieces, slice(2 * width, 3 * width)), NT).astype(
        jnp.bfloat16
    )


def head_masks():
    lane = lax.broadcasted_iota(jnp.int32, (1, 2 * LANES), 1)
    turned = [((lane % LANES) // 32 == n).astype(jnp.float32).astype(jnp.bfloat16) for n in range(4)]
    plain = [(lane // HEAD_DIM == n).astype(jnp.float32).astype(jnp.bfloat16) for n in range(4)]
    return (turned, plain)


def attend_kernel(order, bias, q_in, k_in, v_in, out, log_out):
    turned, plain = head_masks()
    lane = lax.broadcasted_iota(jnp.int32, (BLOCK, LANES), 1)

    def block(n, carried):
        rows = pl.ds(pl.multiple_of(n * BLOCK, BLOCK), BLOCK)
        span = pl.ds(pl.multiple_of(n * BLOCK, BLOCK), BLOCK + 2 * HALF)
        queries, keys, values = q_in[0, rows, :], k_in[0, span, :], v_in[0, span, :]
        masked = bias[n]
        total = jnp.zeros((BLOCK, 2 * LANES), jnp.float32)
        logs = jnp.zeros((BLOCK, LANES), jnp.float32)
        for h in range(4):
            scores = dot(queries * turned[h], keys, NT) + masked
            row_top = jnp.max(scores, axis=-1, keepdims=True)
            lifted = jnp.exp(scores - row_top)
            row_total = jnp.sum(lifted, axis=-1, keepdims=True)
            probs_low = (lifted * (1.0 / row_total)).astype(jnp.bfloat16)
            total = total + dot(probs_low, values * plain[h], NN)
            logs = jnp.where(lane == h, row_top + jnp.log(row_total), logs)
        out[0, rows, :] = total.astype(jnp.bfloat16)
        log_out[0, rows, :] = logs
        return carried

    lax.fori_loop(0, bias.shape[0], block, 0)


def proj_kernel(order, hidden, gains, attended, *refs):
    pieces, (middle, rows_two) = refs[:PIECES], refs[PIECES:]
    step = pl.program_id(0)

    @pl.when(step == 0)
    def _():
        def one(rows):
            middle[rows, :] = relative(order, hidden, rows).astype(jnp.float32)

        row_steps(hidden.shape[0], HALF, one)

    middle[...] += dot(attended[0], wide(pieces, slice(None)), NN)

    @pl.when(step == pl.num_programs(0) - 1)
    def _():
        def one(rows):
            rows_two[rows, :] = (normed(middle[rows, :])[0] * gains[1:2, :]).astype(jnp.bfloat16)

        row_steps(hidden.shape[0], HALF, one)


def gate_kernel(order, rows_two, *refs):
    pieces, (active, gate_side, up_side, rows_turned, gate, up) = refs[:PIECES], refs[PIECES:]

    @pl.when(pl.program_id(0) == 0)
    def _():
        rows_turned[...] = rows_two[...].T

    count = gate.shape[0]
    gate[...] = dot(wide(pieces, slice(0, count)), rows_turned[...], NN)
    up[...] = dot(wide(pieces, slice(count, 2 * count)), rows_turned[...], NN)

    def one(rows):
        x, u = gate[rows, :], up[rows, :]
        below = 0.5 * (1.0 + lax.erf(x * (0.5**0.5)))
        density = jnp.exp(-0.5 * x * x) * ((2.0 * math.pi) ** -0.5)
        lifted = x * below
        active[rows, :] = (lifted * u).astype(jnp.bfloat16)
        gate_side[rows, :] = (u * (below + x * density)).astype(jnp.bfloat16)
        up_side[rows, :] = lifted.astype(jnp.bfloat16)

    row_steps(count, 16, one)


def down_kernel(order, middle, active, *refs):
    pieces, (out, total) = refs[:PIECES], refs[PIECES:]
    step = pl.program_id(0)

    @pl.when(step == 0)
    def _():
        total[...] = middle[...]

    total[...] += dot(active[...], wide(pieces, slice(None)), TN)

    @pl.when(step == pl.num_programs(0) - 1)
    def _():
        for n in range(PIECES):
            lanes = pl.ds(pl.multiple_of(order[n] * LANES, LANES), LANES)
            out[:, lanes] = total[:, n * LANES : (n + 1) * LANES].astype(jnp.bfloat16)


def down_grad_kernel(order, cotangent, active, *refs):
    pieces, (cot_out,) = refs[:5], refs[5:]

    @pl.when(pl.program_id(0) == 0)
    def _():
        def one(rows):
            cot_out[rows, :] = relative(order, cotangent, rows)

        row_steps(cotangent.shape[0], HALF, one)

    store_pieces(pieces, slice(None), dot(active[...], cot_out[...], NN))


def in_grad_kernel(order, cot, rows_two, gate_side, up_side, *refs):
    pieces, grads = refs[:PIECES], refs[PIECES : PIECES + 5]
    gate_out, up_out, cot_turned, grad_active = refs[PIECES + 5 :]

    @pl.when(pl.program_id(0) == 0)
    def _():
        cot_turned[...] = cot[...].T

    count = grad_active.shape[0]
    grad_active[...] = dot(wide(pieces, slice(None)), cot_turned[...], NN)

    def one(rows):
        grad = grad_active[rows, :]
        gate_out[rows, :] = (grad * gate_side[rows, :].astype(jnp.float32)).astype(jnp.bfloat16)
        up_out[rows, :] = (grad * up_side[rows, :].astype(jnp.float32)).astype(jnp.bfloat16)

    row_steps(count, 16, one)
    store_pieces(grads, slice(0, count), dot(gate_out[...], rows_two[...], NN))
    store_pieces(grads, slice(count, 2 * count), dot(up_out[...], rows_two[...], NN))


def middle_grad_kernel(order, middle, cot, gains, *refs):
    sides, pieces, refs = refs[:4], refs[4 : 4 + PIECES], refs[4 + PIECES :]
    grad_middle, grad_low, gain_out, total = refs
    step = pl.program_id(0)
    count = sides[0].shape[0]

    @pl.when(step == 0)
    def _():
        total[...] = jnp.zeros_like(total)
        gain_out[...] = jnp.zeros_like(gain_out)

    for n, side in enumerate(sides):
        rows = slice((n % 2) * count, (n % 2 + 1) * count)
        total[...] += dot(side[...], wide(pieces, rows, n // 2), TN)

    @pl.when(step == pl.num_programs(0) - 1)
    def _():
        def one(rows):
            grad = total[rows, :]
            hat, scale = normed(middle[rows, :])
            result = cot[rows, :].astype(jnp.float32) + norm_pull(hat, scale, gains[1:2, :], grad)
            grad_middle[rows, :] = result
            grad_low[rows, :] = result.astype(jnp.bfloat16)
            gain_out[0:1, :] += jnp.sum(grad * hat, axis=0, keepdims=True)

        row_steps(middle.shape[0], HALF, one)


def attend_grad_kernel(
    order, bias, cosine, sine, grad_low, rows_wide, q_in, k_in, v_in, attended, logs, *refs
):
    pieces, refs = refs[:PIECES], refs[PIECES:]
    weight_grads, (query_out, pair_out, grad_keys, grad_values, grad_out) = refs[:5], refs[5:]
    turned, plain = head_masks()
    row_count = grad_low.shape[0]
    low = jnp.bfloat16
    width = 2 * LANES
    grad_out[...] = dot(grad_low[...], wide(pieces, slice(None)), NT).astype(low)
    grad_keys[...] = jnp.zeros_like(grad_keys)
    grad_values[...] = jnp.zeros_like(grad_values)

    def back(values, rows):
        front, rear = values[:, :LANES], values[:, LANES:]
        cos, sin = cosine[rows, :], sine[rows, :]
        return (front * cos + rear * sin, rear * cos - front * sin)

    def block(n, carried):
        rows = pl.ds(pl.multiple_of(n * BLOCK, BLOCK), BLOCK)
        span = pl.ds(pl.multiple_of(n * BLOCK, BLOCK), BLOCK + 2 * HALF)
        queries, keys, values = q_in[0, rows, :], k_in[0, span, :], v_in[0, span, :]
        grad_rows = grad_out[rows, :]
        masked = bias[n]
        log_rows = logs[0, rows, :]
        grad_query = jnp.zeros((BLOCK, width), jnp.float32)
        grad_key = jnp.zeros((BLOCK + 2 * HALF, width), jnp.float32)
        grad_value = jnp.zeros((BLOCK + 2 * HALF, width), jnp.float32)
        for h in range(4):
            query_head, grad_head = queries * turned[h], grad_rows * plain[h]
            scores = dot(query_head, keys, NT) + masked
            probs = jnp.exp(scores - log_rows[:, h : h + 1])
            grad_probs = dot(grad_head, values, NT)
            row_delta = jnp.sum(probs * grad_probs, axis=-1, keepdims=True)
            grad_scores = (probs * (grad_probs - row_delta)).astype(low)
            grad_query = grad_query + dot(grad_scores, keys * turned[h], NN)
            grad_key = grad_key + dot(grad_scores, query_head, TN)
            grad_value = grad_value + dot(probs.astype(low), grad_head, TN)
        place = pl.ds(pl.multiple_of(n * BLOCK + HALF, HALF), BLOCK)
        front, rear = back(grad_query * HEAD_DIM ** (-0.5), place)
        query_out[0, rows, :LANES] = front.astype(low)
        query_out[0, rows, LANES:] = rear.astype(low)
        grad_keys[span, :] += grad_key
        grad_values[span, :] += grad_value
        return carried

    lax.fori_loop(0, bias.shape[0], block, 0)
    front, rear = back(grad_keys[...], slice(None))
    pair_out[0, 0, :, :LANES] = front.astype(low)
    pair_out[0, 0, :, LANES:] = rear.astype(low)
    pair_out[0, 1] = grad_values[...].astype(low)
    inner = slice(HALF, HALF + row_count)
    store_pieces(weight_grads, slice(0, width), dot(query_out[0], rows_wide[inner, :], TN))
    for c in range(2):
        rows = slice((1 + c) * width, (2 + c) * width)
        store_pieces(weight_grads, rows, dot(pair_out[0, c], rows_wide[...], TN))
    store_pieces(weight_grads, slice(3 * width, 4 * width), dot(attended[0], grad_low[...], TN))


def input_grad_kernel(order, hidden, gains, grad_middle, *refs):
    own, second, odd, (before, after), refs = refs[:2], refs[2:4], refs[4:6], refs[6:8], refs[8:]
    pieces, (grad_input, gain_out, mixed, total) = refs[:PIECES], refs[PIECES:]
    step = pl.program_id(0)
    row_count = hidden.shape[0]
    width = 2 * LANES
    last = row_count - HALF

    @pl.when(step == 0)
    def _():
        total[...] = jnp.zeros_like(total)
        gain_out[...] = jnp.zeros_like(gain_out)

    def sum_low(left, right):
        return (left.astype(jnp.float32) + right.astype(jnp.float32)).astype(jnp.bfloat16)

    def add(slab, queries, pairs):
        total[...] += dot(queries[0], wide(pieces, slice(0, width), slab), NN)
        for c in range(2):
            mixed[...] = pairs[0, c, HALF : HALF + row_count, :]
            mixed[0:HALF, :] = sum_low(mixed[0:HALF, :], before[slab, c])
            mixed[last:, :] = sum_low(mixed[last:, :], after[slab, c])
            rows = slice((1 + c) * width, (2 + c) * width)
            total[...] += dot(mixed[...], wide(pieces, rows, slab), NN)

    pl.when(step == 0)(functools.partial(add, 0, *own))
    pl.when(step == 1)(functools.partial(add, 0, *second))
    add(1, *odd)

    @pl.when(step == pl.num_programs(0) - 1)
    def _():
        def one(rows):
            grad = total[rows, :]
            hat, scale = normed(relative(order, hidden, rows).astype(jnp.float32))
            result = grad_middle[rows, :] + norm_pull(hat, scale, gains[0:1, :], grad)
            for n in range(PIECES):
                lanes = pl.ds(pl.multiple_of(order[n] * LANES, LANES), LANES)
                grad_input[rows, lanes] = result[:, n * LANES : (n + 1) * LANES]
            gain_out[0:1, :] += jnp.sum(grad * hat, axis=0, keepdims=True)

        row_steps(row_count, HALF, one)


def local(
    hidden_in,
    seq_lengths,
    cotangent,
    w_qkv,
    w_proj,
    w_in,
    w_down,
    norm_gains,
    qkv_first,
    qkv_second,
    proj_first,
    proj_second,
    in_first,
    in_second,
    down_first,
    down_second,
    gain_first,
    gain_second,
):
    row_count = hidden_in.shape[0]
    wide_count = row_count + 2 * HALF
    size = lax.axis_size("tensor")
    dp_size = lax.axis_size("dp")
    group_rows = row_count * size
    low, full = jnp.bfloat16, jnp.float32
    chunk = norm_gains.shape[1]
    head_wide = w_proj.shape[1]
    head_rows = 4 * head_wide
    slab_rows = head_rows + SLAB_PAD
    hidden_wide = w_down.shape[1]
    head_count, half_dim = head_wide // HEAD_DIM, HEAD_DIM // 2

    def halves_first(weight):
        split = weight.reshape(chunk, 2, head_count, 2, half_dim)
        return jnp.transpose(split, (0, 1, 3, 2, 4)).reshape(chunk, 2 * head_wide)

    def heads_first(weight):
        split = weight.reshape(chunk, 2, 2, head_count, half_dim)
        return jnp.transpose(split, (0, 1, 3, 2, 4)).reshape(chunk, 2, head_wide)

    heads_slab = jnp.concatenate(
        [
            jnp.concatenate(
                [halves_first(w_qkv[:, :2].astype(low)), w_qkv[:, 2].astype(low), w_proj.astype(low)],
                axis=1,
            ).T,
            jnp.pad(norm_gains.astype(low), ((0, SLAB_PAD - 2), (0, 0))),
        ]
    )
    in_slab = w_in.astype(low).reshape(chunk, 2 * hidden_wide).T
    down_slab = w_down.astype(low).T
    if dp_size == PIECES:
        apart = jnp.array([0, 2, 4, 6, 1, 3, 5, 7], jnp.int32)
        order = lax.axis_index("dp").astype(jnp.int32) ^ apart
        hidden, cot_in = hidden_in, cotangent
    else:
        order = jnp.arange(PIECES, dtype=jnp.int32)
        hidden, cot_in = to_relative(hidden_in), to_relative(cotangent)

    edges = (shift(hidden[-HALF:], 1), shift(hidden[:HALF], -1))
    place = lax.axis_index("tensor").astype(jnp.int32)
    place_rows = jnp.full((8, LANES), place)
    heads_near = gather_near(heads_slab, place)
    heads_pieces = gather_far(heads_near, True)
    line_token = held_back(place_rows * 0, heads_near[:1])
    in_near = gather_near(
        tied(in_slab, line_token), held_back(place_rows, heads_pieces[3:4])[0, 0]
    )
    heads_pieces = [piece.reshape(size, -1, LANES) for piece in heads_pieces]
    gains = jnp.concatenate(
        [piece[0, head_rows : head_rows + 8] for piece in heads_pieces], axis=1
    ).astype(full)

    first_row = lax.axis_index("tensor") * row_count
    segment, position = layout(
        seq_lengths[0], first_row - HALF + jnp.arange(wide_count), group_rows
    )
    cosine, sine = rotary_tables(position)
    bias = jnp.where(allowed_pairs(segment), 0.0, MASKED).astype(full)

    head_block = (size, row_count, head_wide)
    wide_block = (size, wide_count, head_wide)
    tokens = (row_count, D)
    turned = (size * hidden_wide, row_count)
    turned_spec = pl.BlockSpec((hidden_wide, row_count), lambda n, *_: (n, 0))
    matmul = 2 * row_count * D

    queries, keys, values, rows_wide, token = run(
        heads_kernel,
        "heads",
        [order, (hidden, None), (edges[0], None), (edges[1], None), (gains, None)]
        + [(cosine, None), (sine, None)]
        + [slabs(piece, 3 * head_wide) for piece in heads_pieces],
        [lead_out(head_block, low), lead_out(wide_block, low), lead_out(wide_block, low)]
        + [((wide_count, D), low, None)],
        [],
        3 * matmul * D,
        after=in_near[:1],
    )
    in_pieces = gather_far(in_near, False, token)
    attended, logs, token = run(
        attend_kernel,
        "attend",
        [order, (bias, None), lead(queries), lead(keys), lead(values)],
        [lead_out(head_block, low), lead_out((size, row_count, LANES), full)],
        [],
        2 * matmul * D,
        after=in_near[1:],
    )
    down_near = gather_near(tied(down_slab, line_token), place + token[0, 0])
    middle, rows_two, proj_token = run(
        proj_kernel,
        "proj",
        [order, (hidden, None), (gains, None), lead(attended)]
        + [slabs(piece, head_wide, first=3) for piece in heads_pieces],
        [(tokens, full, None), (tokens, low, None)],
        [],
        matmul * D,
        after=in_pieces[3:4],
    )
    in_pieces = [piece.reshape(size, -1, LANES) for piece in in_pieces]
    _, proj_token = blend("arrived", [], (proj_token, *down_near[1:]))
    active, gate_side, up_side, token = run(
        gate_kernel,
        "gate",
        [order, (rows_two, None)] + [slabs(piece, 2 * hidden_wide) for piece in in_pieces],
        [(turned, low, turned_spec)] * 3,
        [
            pltpu.VMEM((D, row_count), low),
            pltpu.VMEM((hidden_wide, row_count), full),
            pltpu.VMEM((hidden_wide, row_count), full),
        ],
        2 * matmul * FF,
        after=(proj_token,),
    )
    down_pieces = gather_far(down_near, True, proj_token, token)

    *down_own, down_partner, cot, token = run(
        down_grad_kernel,
        "down_grad",
        [order, (cot_in, None), turned_block(active, hidden_wide)],
        piece_outs(size, hidden_wide) + [(tokens, low, None)],
        [],
        matmul * FF,
        after=down_pieces[3:4],
    )
    down_pieces = [piece.reshape(size, -1, LANES) for piece in down_pieces]

    half = size // 2
    half_turned = (half * hidden_wide, row_count)

    def core_hop(outs):
        own = [part.reshape(-1, LANES) for part in outs[:4]]
        return (own, flip(outs[4].reshape(4, -1, LANES), 1))

    def core_sums(own, received):
        return [[(part,), (received, n)] for n, part in enumerate(own)]

    def near_sums(own, arrived, entries):
        terms = [part.reshape(entries, -1, LANES) for part in (own, *arrived)]
        return [[(term, n) for term in terms] for n in range(entries)]

    def line_sums(to_after, to_before, arrived):
        return [[(to_after,), (arrived[0],)], [(to_before,), (arrived[1],)]]

    down_core = core_hop([*down_own, down_partner])

    def in_grad(part, name, after):
        return run(
            in_grad_kernel,
            name,
            [order, (cot, None), (rows_two, None)]
            + [turned_block(gate_side, hidden_wide, part), turned_block(up_side, hidden_wide, part)]
            + [slabs(piece, hidden_wide, part) for piece in down_pieces],
            piece_outs(half, 2 * hidden_wide) + [(half_turned, low, turned_spec)] * 2,
            [pltpu.VMEM((D, row_count), low), pltpu.VMEM((hidden_wide, row_count), full)],
            3 * matmul * FF // 2,
            after=after,
            steps=half,
        )

    *odd_outs, odd_gate, odd_up, token = in_grad(ODD, "in_grad_odd", ())
    odd_core = core_hop(odd_outs)
    down_sums, token = blend("sums_one", core_sums(*down_core), (token,))
    down_far = flip(down_sums[3], 2)
    *even_outs, even_gate, even_up, token = in_grad(EVEN, "in_grad_even", (token,))
    even_core = core_hop(even_outs)
    (*odd_sums, down_y), token = blend(
        "sums_two", core_sums(*odd_core) + [[(down_sums[2],), (down_far,)]], (token,)
    )
    odd_far = flip(odd_sums[3], 4)
    down_near = (flip(down_sums[1], 2), flip(down_y, 4))
    grad_middle, grad_low, gain_two, token = run(
        middle_grad_kernel,
        "middle_grad",
        [order, (middle, None), (cot, None), (gains, None)]
        + [turned_block(side, hidden_wide) for side in (even_gate, even_up, odd_gate, odd_up)]
        + [slabs(piece, 2 * hidden_wide, count=2) for piece in in_pieces],
        [(tokens, full, None), (tokens, low, None), ((8, D), full, None)],
        [pltpu.VMEM(tokens, full)],
        2 * matmul * FF,
        after=(token,),
        steps=half,
    )
    sums, token = blend(
        "sums_three",
        core_sums(*even_core)
        + [[(odd_sums[1],), (odd_far,)]]
        + near_sums(down_sums[0], down_near, size),
        (token,),
    )
    even_sums, odd_x, down_parts = sums[:4], sums[4], [far_scatter(part) for part in sums[5:]]
    even_far = flip(even_sums[3], 4)
    odd_near = (flip(odd_x, 2), flip(odd_sums[2], 4))
    down_line = line_hop(down_parts[1], down_parts[3], 3)

    def attend_grad(part, count, name, after):
        return run(
            attend_grad_kernel,
            name,
            [order, (bias, None), (cosine, None), (sine, None), (grad_low, None), (rows_wide, None)]
            + [lead(array, part) for array in (queries, keys, values, attended, logs)]
            + [slabs(piece, head_wide, part, first=3) for piece in heads_pieces],
            piece_outs(count, head_rows)
            + [
                lead_out((count, row_count, head_wide), low),
                lead_out((count, 2, wide_count, head_wide), low),
            ],
            [
                pltpu.VMEM((wide_count, head_wide), full),
                pltpu.VMEM((wide_count, head_wide), full),
                pltpu.VMEM((row_count, head_wide), low),
            ],
            3 * count * matmul * D,
            after=after,
            steps=count,
        )

    *odd_outs, odd_queries, odd_pairs, token = attend_grad(ODD, half, "attend_grad_odd", (token,))
    heads_odd_core = core_hop(odd_outs)
    sums, token = blend(
        "sums_four",
        [[(even_sums[1],), (even_far,)]]
        + near_sums(odd_sums[0], odd_near, half)
        + line_sums(down_parts[2], down_parts[2], down_line),
        (token,),
    )
    even_near = (flip(sums[0], 2), flip(even_sums[2], 4))
    odd_parts = [far_scatter(part) for part in sums[1:3]]
    down_line = line_hop(sums[3], sums[4], 2)
    *second_outs, second_queries, second_pairs, token = attend_grad(
        SECOND, 1, "attend_grad_second", (token,)
    )
    heads_second_core = core_hop(second_outs)
    sums, token = blend(
        "sums_five",
        core_sums(*heads_odd_core)
        + near_sums(even_sums[0], even_near, half)
        + line_sums(down_parts[3], down_parts[1], down_line),
        (token,),
    )
    heads_odd_sums, even_parts = sums[:4], [far_scatter(part) for part in sums[4:6]]
    heads_odd_far = flip(heads_odd_sums[3], 2)
    down_line = line_hop(sums[6], sums[7], 1)
    in_line = line_hop(odd_parts[0], odd_parts[1], 3)
    *own_outs, own_queries, own_pairs, token = attend_grad(OWN, 1, "attend_grad_own", (token,))
    heads_own_core = core_hop(own_outs)
    sums, token = blend(
        "sums_six",
        core_sums(*heads_second_core)
        + [[(heads_odd_sums[2],), (heads_odd_far,)]]
        + line_sums(even_parts[1], even_parts[1], in_line),
        (token, *down_line),
    )
    heads_second_sums = sums[:4]
    heads_second_far = flip(heads_second_sums[3], 4)
    heads_odd_near = (flip(heads_odd_sums[1], 2), flip(sums[4], 4))
    in_line = line_hop(sums[5], sums[6], 2)
    pairs = [own_pairs[0], odd_pairs[0], second_pairs[0], odd_pairs[1]]
    edge_after = jnp.stack([pair[:, -HALF:] for pair in pairs[-1:] + pairs[:-1]])
    edge_before = jnp.stack([pair[:, :HALF] for pair in pairs[1:] + pairs[:1]])
    edges = (shift(edge_after, 1), shift(edge_before, -1))
    hidden_out, token = run(
        down_kernel,
        "down",
        [order, (middle, None), turned_block(active, hidden_wide)]
        + [slabs(piece, hidden_wide) for piece in down_pieces],
        [(tokens, low, None)],
        [pltpu.VMEM(tokens, full)],
        matmul * FF,
        after=(token,),
    )
    sums, token = blend(
        "sums_seven",
        core_sums(*heads_own_core)
        + [[(heads_second_sums[1],), (heads_second_far,)]]
        + near_sums(heads_odd_sums[0], heads_odd_near, half)
        + line_sums(odd_parts[1], odd_parts[0], in_line),
        (token,),
    )
    heads_own_sums, heads_odd_parts = sums[:4], [far_scatter(part) for part in sums[5:7]]
    heads_own_far = flip(heads_own_sums[3], 2)
    heads_second_near = (flip(sums[4], 2), flip(heads_second_sums[2], 4))
    in_line = line_hop(sums[7], sums[8], 1)
    heads_line = line_hop(heads_odd_parts[0], heads_odd_parts[1], 3)
    grad_input, gain_one, token = run(
        input_grad_kernel,
        "input_grad",
        [order, (hidden, None), (gains, None), (grad_middle, None)]
        + [(own_queries, None), (own_pairs, None), (second_queries, None), (second_pairs, None)]
        + [lead(odd_queries), lead(odd_pairs)]
        + [lead(array, count=2) for array in edges]
        + [slabs(piece, 3 * head_wide, count=2) for piece in heads_pieces],
        [(tokens, full, None), ((8, D), full, None)],
        [pltpu.VMEM((row_count, head_wide), low), pltpu.VMEM(tokens, full)],
        3 * matmul * D,
        after=(token,),
        steps=half,
    )
    sums, token = blend(
        "sums_eight",
        near_sums(heads_second_sums[0], heads_second_near, 1)
        + [[(heads_own_sums[2],), (heads_own_far,)]],
        (token, *heads_line),
    )
    heads_second_part = far_scatter(sums[0])
    heads_own_near = (flip(heads_own_sums[1], 2), flip(sums[1], 4))
    heads_line = line_hop(*[add_low(heads_second_part, part) for part in heads_line], 2)
    heads_line = line_hop(
        add_low(heads_odd_parts[1], heads_line[0]), add_low(heads_odd_parts[0], heads_line[1]), 1
    )
    heads_own_part = far_scatter(line_end(heads_own_sums[0], heads_own_near).astype(low))
    gain_sum = gain_scatter(tied(jnp.concatenate([gain_one[:1], gain_two[:1]]), token))
    if dp_size != PIECES:
        hidden_out, grad_input = to_relative(hidden_out, True), to_relative(grad_input, True)

    down_sum = line_end(down_parts[0], down_line).T
    in_sum = line_end(even_parts[0], in_line).T.reshape(w_in.shape)
    heads_sum = line_end(heads_own_part, heads_line).T
    qkv_sum = jnp.concatenate(
        [
            heads_first(heads_sum[:, : 2 * head_wide]),
            heads_sum[:, None, 2 * head_wide : 3 * head_wide],
        ],
        axis=1,
    )
    proj_sum = heads_sum[:, 3 * head_wide :]
    qkv_one, qkv_two, qkv_new = adam_update(w_qkv, qkv_sum, qkv_first, qkv_second, D ** (-0.5))
    proj_one, proj_two, proj_new = adam_update(
        w_proj, proj_sum, proj_first, proj_second, (D // HALF) ** (-0.5)
    )
    in_one, in_two, in_new = adam_update(w_in, in_sum, in_first, in_second, D ** (-0.5))
    down_one, down_two, down_new = adam_update(
        w_down, down_sum, down_first, down_second, (FF // 2) ** (-0.5)
    )
    gain_one, gain_two, gains_new = adam_update(
        norm_gains, gain_sum, gain_first, gain_second, GAIN_RATE
    )
    return (
        hidden_out,
        grad_input,
        qkv_one,
        qkv_two,
        qkv_new,
        proj_one,
        proj_two,
        proj_new,
        in_one,
        in_two,
        in_new,
        down_one,
        down_two,
        down_new,
        gain_one,
        gain_two,
        gains_new,
    )


def solution(mesh):
    placed = (
        P(("dp", "tensor"), None),
        P("dp", None),
        P(("dp", "tensor"), None),
        P("dp", None, "tensor"),
        P("dp", "tensor"),
        P("dp", None, "tensor"),
        P("dp", "tensor"),
        P(None, "dp"),
        P("dp", None, "tensor"),
        P("dp", None, "tensor"),
        P("dp", "tensor"),
        P("dp", "tensor"),
        P("dp", None, "tensor"),
        P("dp", None, "tensor"),
        P("dp", "tensor"),
        P("dp", "tensor"),
        P(None, "dp"),
        P(None, "dp"),
    )
    return jax.shard_map(
        local,
        mesh=mesh,
        in_specs=placed,
        out_specs=(
            P(("dp", "tensor"), None),
            P(("dp", "tensor"), None),
            P("dp", None, "tensor"),
            P("dp", None, "tensor"),
            P("dp", None, "tensor"),
            P("dp", "tensor"),
            P("dp", "tensor"),
            P("dp", "tensor"),
            P("dp", None, "tensor"),
            P("dp", None, "tensor"),
            P("dp", None, "tensor"),
            P("dp", "tensor"),
            P("dp", "tensor"),
            P("dp", "tensor"),
            P(None, "dp"),
            P(None, "dp"),
            P(None, "dp"),
        ),
        check_vma=False,
    )
```

```python
import functools
import math

import jax
import jax.numpy as jnp
from jax import lax
from jax.experimental import pallas as pl
from jax.experimental.pallas import tpu as pltpu
from jax.sharding import PartitionSpec as P

D = 1024
HEADS = 16
HEAD_DIM = 64
FF = 2624
HALF = 64
BLOCK = 128
STEP = 10

NORM_EPS = 1e-05
THETA_BASE = 10000.0
BETA_ONE = 0.9
BETA_TWO = 0.98
ADAM_EPS = 1e-06
WEIGHT_DECAY = 0.01
GAIN_RATE = 0.5
MASKED = -1e30


LANES = 128
PIECES = 8
SLAB_PAD = 16
VMEM_BYTES = 52 * 1024 * 1024
COST_FACTOR = 1e-3


def layout(lengths, token_index, group_rows):
    seq_ends = jnp.cumsum(lengths)
    seq_starts = seq_ends - lengths
    segment = jnp.sum((token_index[:, None] >= seq_ends[None, :]).astype(jnp.int32), axis=1)
    member = segment[:, None] == jnp.arange(lengths.shape[0])[None, :]
    position = token_index - jnp.sum(jnp.where(member, seq_starts[None, :], 0), axis=1)
    inside = (token_index >= 0) & (token_index < group_rows)
    return (jnp.where(inside, segment, -1), jnp.where(inside, position, 0))


def rotary_tables(position):
    half_dim = HEAD_DIM // 2
    exponent = jnp.arange(half_dim).astype(jnp.float32) * (2.0 / HEAD_DIM)
    inverse = jnp.power(jnp.float32(THETA_BASE), -exponent)
    angle_table = position.astype(jnp.float32)[:, None] * inverse[None, :]
    copies = LANES // half_dim
    return (jnp.tile(jnp.cos(angle_table), (1, copies)), jnp.tile(jnp.sin(angle_table), (1, copies)))


def windows(rows):
    count = (rows.shape[0] - 2 * HALF) // BLOCK
    return jnp.stack([rows[n * BLOCK : n * BLOCK + BLOCK + 2 * HALF] for n in range(count)])


def allowed_pairs(segment):
    key_seg = windows(segment)
    query_seg = segment[HALF:-HALF].reshape(-1, BLOCK)
    offset = jnp.arange(BLOCK)[:, None] + HALF - jnp.arange(BLOCK + 2 * HALF)[None, :]
    return (query_seg[:, :, None] == key_seg[:, None, :]) & (jnp.abs(offset) <= HALF)[None]


def adam_update(master, gradient, moment_one, moment_two, step_rate):
    one_new = BETA_ONE * moment_one + (1.0 - BETA_ONE) * gradient
    two_new = BETA_TWO * moment_two + (1.0 - BETA_TWO) * gradient * gradient
    one_hat = one_new / (1.0 - BETA_ONE**STEP)
    two_hat = two_new / (1.0 - BETA_TWO**STEP)
    master_new = master - step_rate * (
        one_hat / (jnp.sqrt(two_hat) + ADAM_EPS) + WEIGHT_DECAY * master
    )
    return (one_new, two_new, master_new)


def line_gather(slab, place):
    size = lax.axis_size("tensor")
    from_before, from_after = [slab], [slab]
    for step in range(1, size):
        from_before.append(
            lax.ppermute(from_before[-1], "tensor", [(n, n + 1) for n in range(step - 1, size - 1)])
        )
        from_after.append(
            lax.ppermute(from_after[-1], "tensor", [(n, n - 1) for n in range(1, size - step + 1)])
        )
    return jnp.stack(
        [slab]
        + [
            jnp.where(place >= step, from_before[step], from_after[size - step])
            for step in range(1, size)
        ]
    )


def tied(values, token):
    return values if token is None else jnp.where(token[0, 0] == 0, values, 0.0 * values)


def line_hop(to_after, to_before, step):
    size = lax.axis_size("tensor")
    return (
        lax.ppermute(to_after, "tensor", [(n, n + 1) for n in range(size - step)]),
        lax.ppermute(to_before, "tensor", [(n, n - 1) for n in range(step, size)]),
    )


def line_end(own, arrived):
    return sum((part.astype(jnp.float32) for part in arrived), own.astype(jnp.float32))


def gain_scatter(gains):
    for mask in [1, 4, 2] + far_bits()[::-1]:
        half = gains.shape[1] // 2
        gains = gains[:, :half] + flip(gains[:, half:], mask)
    size = lax.axis_size("tensor")
    for mask in (1 << n for n in range(size.bit_length() - 1)):
        gains = gains + lax.ppermute(gains, "tensor", [(n, n ^ mask) for n in range(size)])
    return gains


def flip(rows, mask):
    return lax.ppermute(rows, "dp", [(n, n ^ mask) for n in range(lax.axis_size("dp"))])


def far_bits():
    size = lax.axis_size("dp")
    return [1 << n for n in range(3, size.bit_length() - 1)]


def gather_near(slab, place):
    piece = line_gather(slab, place)
    piece = piece.reshape(-1, piece.shape[-1])
    for mask in far_bits():
        piece = jnp.concatenate([piece, flip(piece, mask)], axis=1)
    return (piece, flip(piece, 2), flip(piece, 4))


def gather_far(near):
    piece, by_x, by_y = near
    half = piece.shape[0] // 2
    far = jnp.concatenate([flip(by_x[:half], 4), flip(by_y[half:], 2)])
    mine = [piece, by_x, by_y, far]
    return mine + [flip(part, 1) for part in mine]


def add_low(left, right):
    return (left.astype(jnp.float32) + right.astype(jnp.float32)).astype(left.dtype)


def far_scatter(part):
    for mask in reversed(far_bits()):
        half = part.shape[1] // 2
        part = add_low(part[:, :half], flip(part[:, half:], mask))
    return part


def gather_dp(piece):
    if lax.axis_size("dp") == PIECES:
        return lax.all_gather(piece, "dp", axis=0)
    flat = piece.reshape(-1, piece.shape[-1])
    for mask in far_bits():
        flat = jnp.concatenate([flat, flip(flat, mask)], axis=1)
    pieces = gather_far((flat, flip(flat, 2), flip(flat, 4)))
    return jnp.stack(pieces).reshape((PIECES,) + piece.shape[:-1] + (LANES,))


def scatter_dp(grads):
    if lax.axis_size("dp") == PIECES:
        return lax.psum_scatter(grads, "dp", scatter_dimension=0, tiled=False)
    flat = grads.reshape(PIECES, -1, LANES)
    own, by_x, by_y, far = add_low(flat[:4], flip(flat[4:], 1))
    by_y = add_low(by_y, flip(far, 2))
    total = add_low(add_low(own, flip(by_x, 2)), flip(by_y, 4))
    return far_scatter(total).reshape(grads.shape[1:3] + (-1,))


def to_relative(rows, back=False):
    size = lax.axis_size("dp")
    place = lax.axis_index("dp")
    bits = size.bit_length() - 1
    lead = rows.shape[:-1]
    axes = len(lead)
    chunk = rows.shape[-1] // size
    wanted = [bits - 1, bits - 3, bits - 2] + list(range(bits - 3))
    order = list(range(axes)) + [axes + n for n in wanted] + [axes + bits]
    cube = rows.reshape(lead + (2,) * bits + (chunk,))
    if back:
        cube = jnp.transpose(cube, [order.index(n) for n in range(len(order))])
    for n in range(bits):
        cube = jnp.where((place >> (bits - 1 - n)) & 1 == 1, jnp.flip(cube, axes + n), cube)
    if not back:
        cube = jnp.transpose(cube, order)
    return cube.reshape(rows.shape)


def shift(rows, step):
    size = lax.axis_size("tensor")
    pairs = [(n, n + step) for n in range(size) if 0 <= n + step < size]
    return lax.ppermute(rows, "tensor", pairs)


NN = ((1,), (0,))
NT = ((1,), (1,))
TN = ((0,), (0,))


def dot(left, right, dims):
    return lax.dot_general(left, right, (dims, ((), ())), preferred_element_type=jnp.float32)


def wide(pieces, rows, slab=0):
    return jnp.concatenate([piece[slab, rows, :] for piece in pieces], axis=1)


def relative(order, ref, rows):
    return jnp.concatenate(
        [
            ref[rows, pl.ds(pl.multiple_of(order[n] * LANES, LANES), LANES)]
            for n in range(PIECES)
        ],
        axis=1,
    )


def normed(values):
    centered = values - jnp.mean(values, axis=-1, keepdims=True)
    scale = lax.rsqrt(jnp.mean(centered * centered, axis=-1, keepdims=True) + NORM_EPS)
    return (centered * scale, scale)


def norm_pull(hat, scale, gain, grad):
    scaled = grad * gain
    return scale * (
        scaled
        - jnp.mean(scaled, axis=-1, keepdims=True)
        - hat * jnp.mean(scaled * hat, axis=-1, keepdims=True)
    )


def row_steps(count, size, body):
    def step(n, carried):
        body(pl.ds(pl.multiple_of(n * size, size), size))
        return carried

    lax.fori_loop(0, count // size, step, 0)


def whole_spec(array):
    return pl.BlockSpec(array.shape, lambda *_: (0,) * len(array.shape))


def run(kernel, name, operands, outs, scratch, flops, after=(), steps=None):
    order, operands = operands[0], operands[1:]
    specs = [spec if spec is not None else whole_spec(array) for array, spec in operands]
    out_specs = [
        spec if spec is not None else pl.BlockSpec(shape, lambda *_, n=len(shape): (0,) * n)
        for shape, dtype, spec in outs
    ]
    moved = sum(array.size * array.dtype.itemsize for array, _ in operands)
    moved += sum(math.prod(shape) * jnp.dtype(dtype).itemsize for shape, dtype, _ in outs)
    kept, made = len(operands), len(outs)

    def body(order_ref, *refs):
        refs = refs[:kept] + refs[kept + len(after) :]
        token = refs[kept + made]
        token[...] = jnp.zeros_like(token)
        kernel(order_ref, *refs[: kept + made], *refs[kept + made + 1 :])

    return pl.pallas_call(
        body,
        grid_spec=pltpu.PrefetchScalarGridSpec(
            num_scalar_prefetch=1,
            grid=(steps or lax.axis_size("tensor"),),
            in_specs=specs + [pl.BlockSpec(memory_space=pl.ANY)] * len(after),
            out_specs=out_specs + [pl.BlockSpec((8, LANES), lambda *_: (0, 0))],
            scratch_shapes=scratch,
        ),
        out_shape=[jax.ShapeDtypeStruct(shape, dtype) for shape, dtype, _ in outs]
        + [jax.ShapeDtypeStruct((8, LANES), jnp.int32)],
        compiler_params=pltpu.CompilerParams(
            dimension_semantics=("arbitrary",), vmem_limit_bytes=VMEM_BYTES
        ),
        cost_estimate=pl.CostEstimate(
            flops=int(COST_FACTOR * flops), bytes_accessed=LANES, transcendentals=0
        ),
        name=name,
    )(order, *[array for array, _ in operands], *after)


def held_back(value, after):
    def body(value_ref, *refs):
        refs[-1][...] = value_ref[...]

    return pl.pallas_call(
        body,
        in_specs=[pl.BlockSpec(memory_space=pltpu.VMEM)]
        + [pl.BlockSpec(memory_space=pl.ANY)] * len(after),
        out_specs=pl.BlockSpec(memory_space=pltpu.VMEM),
        out_shape=jax.ShapeDtypeStruct(value.shape, value.dtype),
        name="held_back",
    )(value, *after)


def blend(name, jobs, after):
    halves = 2
    operands, specs, out_specs, shapes, counts, cut = [], [], [], [], [], []
    for terms in jobs:
        rows, lanes = terms[0][0].shape[-2:]
        small = rows % (16 * halves) != 0 or rows < 512
        height = rows if small else rows // halves
        for term in terms:
            operands.append(term[0])
            if len(term) == 1:
                specs.append(pl.BlockSpec((height, lanes), lambda i, s=small: (0 if s else i, 0)))
            else:
                specs.append(
                    pl.BlockSpec(
                        (None, height, lanes),
                        lambda i, s=small, n=term[1]: (n, 0 if s else i, 0),
                    )
                )
        out_specs.append(pl.BlockSpec((height, lanes), lambda i, s=small: (0 if s else i, 0)))
        shapes.append(jax.ShapeDtypeStruct((rows, lanes), jnp.bfloat16))
        counts.append(len(terms))
        cut.append(small)

    def body(*refs):
        ins = refs[: len(operands)]
        outs = refs[len(operands) + len(after) :]
        outs[-1][...] = jnp.zeros_like(outs[-1])
        first = 0
        for n, count in enumerate(counts):
            terms = ins[first : first + count]
            first += count

            def add(out=outs[n], terms=terms):
                out[...] = sum(
                    (term[...].astype(jnp.float32) for term in terms[1:]),
                    terms[0][...].astype(jnp.float32),
                ).astype(jnp.bfloat16)

            pl.when((pl.program_id(0) == 0) | (not cut[n]))(add)

    *sums, token = pl.pallas_call(
        body,
        grid=(halves,),
        in_specs=specs + [pl.BlockSpec(memory_space=pl.ANY)] * len(after),
        out_specs=out_specs + [pl.BlockSpec((8, LANES), lambda i: (0, 0))],
        out_shape=shapes + [jax.ShapeDtypeStruct((8, LANES), jnp.int32)],
        compiler_params=pltpu.CompilerParams(
            dimension_semantics=("arbitrary",), vmem_limit_bytes=VMEM_BYTES
        ),
        name=name,
    )(*operands, *after)
    return (sums, token)


ALL, ODD, EVEN = (0, 1), (1, 2), (0, 2)


def slabs(piece, rows, part=ALL, first=0, count=1):
    return (
        piece,
        pl.BlockSpec((count, rows, LANES), lambda n, *_: (part[0] + part[1] * n, first, 0)),
    )


def gathered(array, rows, part=ALL, count=1):
    return [
        (
            array,
            pl.BlockSpec(
                (None, count, rows, LANES),
                lambda n, order, p=p: (order[p], part[0] + part[1] * n, 0, 0),
            ),
        )
        for p in range(PIECES)
    ]


def gathered_out(parts, rows):
    return (
        (PIECES, parts, rows, LANES),
        jnp.bfloat16,
        pl.BlockSpec((PIECES, 1, rows, LANES), lambda n, *_: (0, n, 0, 0)),
    )


def store_gathered(order, ref, rows, values):
    values = values.astype(jnp.bfloat16)
    for n in range(PIECES):
        ref[order[n], 0, rows, :] = values[:, n * LANES : (n + 1) * LANES]


def lead(array, part=ALL, count=1):
    shape = (count,) + array.shape[1:]
    return (
        array,
        pl.BlockSpec(shape, lambda n, *_: (part[0] + part[1] * n,) + (0,) * (len(shape) - 1)),
    )


def turned_block(array, rows, part=ALL):
    return (array, pl.BlockSpec((rows, array.shape[1]), lambda n, *_: (part[0] + part[1] * n, 0)))


def lead_out(shape, dtype):
    return (shape, dtype, pl.BlockSpec((1,) + shape[1:], lambda n, *_: (n,) + (0,) * (len(shape) - 1)))


def piece_outs(parts, rows):
    low = jnp.bfloat16
    own = pl.BlockSpec((1, rows, LANES), lambda n, *_: (n, 0, 0))
    other = pl.BlockSpec((4, 1, rows, LANES), lambda n, *_: (0, n, 0, 0))
    return [((parts, rows, LANES), low, own)] * 4 + [((4, parts, rows, LANES), low, other)]


def store_pieces(refs, rows, values):
    values = values.astype(jnp.bfloat16)
    for n in range(4):
        refs[n][0, rows, :] = values[:, n * LANES : (n + 1) * LANES]
        refs[4][n, 0, rows, :] = values[:, (n + 4) * LANES : (n + 5) * LANES]


def heads_kernel(order, hidden, before, after, gains, cosine, sine, *refs):
    pieces, (q_out, k_out, v_out, rows_wide) = refs[:PIECES], refs[PIECES:]
    row_count = hidden.shape[0]
    gain = gains[0:1, :]

    def norm_rows(source, rows, first):
        values = relative(order, source, rows).astype(jnp.float32)
        return (normed(values)[0] * gain).astype(jnp.bfloat16)

    @pl.when(pl.program_id(0) == 0)
    def _():
        rows_wide[0:HALF, :] = norm_rows(before, slice(0, HALF), 0)
        rows_wide[HALF + row_count :, :] = norm_rows(after, slice(0, HALF), 0)

        def one(rows):
            values = norm_rows(hidden, rows, 0)
            rows_wide[pl.ds(pl.multiple_of(rows.start + HALF, HALF), HALF), :] = values

        row_steps(row_count, HALF, one)

    width = 2 * LANES

    def turned(mixed, rows):
        front, back = mixed[:, :LANES], mixed[:, LANES:]
        cos, sin = cosine[rows, :], sine[rows, :]
        return (front * cos - back * sin, back * cos + front * sin)

    inner = slice(HALF, HALF + row_count)
    scale = HEAD_DIM ** (-0.5)
    front, back = turned(dot(rows_wide[inner, :], wide(pieces, slice(0, width)), NT), inner)
    q_out[0, :, :LANES] = (front.astype(jnp.bfloat16) * scale).astype(jnp.bfloat16)
    q_out[0, :, LANES:] = (back.astype(jnp.bfloat16) * scale).astype(jnp.bfloat16)
    front, back = turned(
        dot(rows_wide[...], wide(pieces, slice(width, 2 * width)), NT), slice(None)
    )
    k_out[0, :, :LANES] = front.astype(jnp.bfloat16)
    k_out[0, :, LANES:] = back.astype(jnp.bfloat16)
    v_out[0] = dot(rows_wide[...], wide(pieces, slice(2 * width, 3 * width)), NT).astype(
        jnp.bfloat16
    )


def head_masks():
    lane = lax.broadcasted_iota(jnp.int32, (1, 2 * LANES), 1)
    turned = [((lane % LANES) // 32 == n).astype(jnp.float32).astype(jnp.bfloat16) for n in range(4)]
    plain = [(lane // HEAD_DIM == n).astype(jnp.float32).astype(jnp.bfloat16) for n in range(4)]
    return (turned, plain)


def attend_kernel(order, bias, q_in, k_in, v_in, out, log_out):
    turned, plain = head_masks()
    lane = lax.broadcasted_iota(jnp.int32, (BLOCK, LANES), 1)

    def block(n, carried):
        rows = pl.ds(pl.multiple_of(n * BLOCK, BLOCK), BLOCK)
        span = pl.ds(pl.multiple_of(n * BLOCK, BLOCK), BLOCK + 2 * HALF)
        queries, keys, values = q_in[0, rows, :], k_in[0, span, :], v_in[0, span, :]
        masked = bias[n]
        total = jnp.zeros((BLOCK, 2 * LANES), jnp.float32)
        logs = jnp.zeros((BLOCK, LANES), jnp.float32)
        for h in range(4):
            scores = dot(queries * turned[h], keys, NT) + masked
            row_top = jnp.max(scores, axis=-1, keepdims=True)
            lifted = jnp.exp(scores - row_top)
            row_total = jnp.sum(lifted, axis=-1, keepdims=True)
            probs_low = (lifted * (1.0 / row_total)).astype(jnp.bfloat16)
            total = total + dot(probs_low, values * plain[h], NN)
            logs = jnp.where(lane == h, row_top + jnp.log(row_total), logs)
        out[0, rows, :] = total.astype(jnp.bfloat16)
        log_out[0, rows, :] = logs
        return carried

    lax.fori_loop(0, bias.shape[0], block, 0)


def proj_kernel(order, hidden, gains, attended, *refs):
    pieces, (middle, rows_two) = refs[:PIECES], refs[PIECES:]
    step = pl.program_id(0)

    @pl.when(step == 0)
    def _():
        def one(rows):
            middle[rows, :] = relative(order, hidden, rows).astype(jnp.float32)

        row_steps(hidden.shape[0], HALF, one)

    middle[...] += dot(attended[0], wide(pieces, slice(None)), NN)

    @pl.when(step == pl.num_programs(0) - 1)
    def _():
        def one(rows):
            rows_two[rows, :] = (normed(middle[rows, :])[0] * gains[1:2, :]).astype(jnp.bfloat16)

        row_steps(hidden.shape[0], HALF, one)


def gate_kernel(order, rows_two, *refs):
    pieces, (active, gate_side, up_side, rows_turned, gate, up) = refs[:PIECES], refs[PIECES:]

    @pl.when(pl.program_id(0) == 0)
    def _():
        rows_turned[...] = rows_two[...].T

    count = gate.shape[0]
    gate[...] = dot(wide(pieces, slice(0, count)), rows_turned[...], NN)
    up[...] = dot(wide(pieces, slice(count, 2 * count)), rows_turned[...], NN)

    def one(rows):
        x, u = gate[rows, :], up[rows, :]
        below = 0.5 * (1.0 + lax.erf(x * (0.5**0.5)))
        density = jnp.exp(-0.5 * x * x) * ((2.0 * math.pi) ** -0.5)
        lifted = x * below
        active[rows, :] = (lifted * u).astype(jnp.bfloat16)
        gate_side[rows, :] = (u * (below + x * density)).astype(jnp.bfloat16)
        up_side[rows, :] = lifted.astype(jnp.bfloat16)

    row_steps(count, 16, one)


def down_kernel(order, middle, active, *refs):
    pieces, (out, total) = refs[:PIECES], refs[PIECES:]
    step = pl.program_id(0)

    @pl.when(step == 0)
    def _():
        total[...] = middle[...]

    total[...] += dot(active[...], wide(pieces, slice(None)), TN)

    @pl.when(step == pl.num_programs(0) - 1)
    def _():
        for n in range(PIECES):
            lanes = pl.ds(pl.multiple_of(order[n] * LANES, LANES), LANES)
            out[:, lanes] = total[:, n * LANES : (n + 1) * LANES].astype(jnp.bfloat16)


def down_grad_kernel(order, cotangent, active, *refs):
    grads, cot_out = refs

    @pl.when(pl.program_id(0) == 0)
    def _():
        def one(rows):
            cot_out[rows, :] = relative(order, cotangent, rows)

        row_steps(cotangent.shape[0], HALF, one)

    store_gathered(order, grads, slice(None), dot(active[...], cot_out[...], NN))


def in_grad_kernel(order, cot, rows_two, gate_side, up_side, *refs):
    pieces, (grads, gate_out, up_out, cot_turned, grad_active) = refs[:PIECES], refs[PIECES:]

    @pl.when(pl.program_id(0) == 0)
    def _():
        cot_turned[...] = cot[...].T

    count = grad_active.shape[0]
    grad_active[...] = dot(wide(pieces, slice(None)), cot_turned[...], NN)

    def one(rows):
        grad = grad_active[rows, :]
        gate_out[rows, :] = (grad * gate_side[rows, :].astype(jnp.float32)).astype(jnp.bfloat16)
        up_out[rows, :] = (grad * up_side[rows, :].astype(jnp.float32)).astype(jnp.bfloat16)

    row_steps(count, 16, one)
    store_gathered(order, grads, slice(0, count), dot(gate_out[...], rows_two[...], NN))
    store_gathered(order, grads, slice(count, 2 * count), dot(up_out[...], rows_two[...], NN))


def middle_grad_kernel(order, middle, cot, gains, *refs):
    sides, pieces, refs = refs[:2], refs[2 : 2 + PIECES], refs[2 + PIECES :]
    grad_middle, grad_low, gain_out, total = refs
    step = pl.program_id(0)
    count = sides[0].shape[0]

    @pl.when(step == 0)
    def _():
        total[...] = jnp.zeros_like(total)
        gain_out[...] = jnp.zeros_like(gain_out)

    for n, side in enumerate(sides):
        total[...] += dot(side[...], wide(pieces, slice(n * count, (n + 1) * count)), TN)

    @pl.when(step == pl.num_programs(0) - 1)
    def _():
        def one(rows):
            grad = total[rows, :]
            hat, scale = normed(middle[rows, :])
            result = cot[rows, :].astype(jnp.float32) + norm_pull(hat, scale, gains[1:2, :], grad)
            grad_middle[rows, :] = result
            grad_low[rows, :] = result.astype(jnp.bfloat16)
            gain_out[0:1, :] += jnp.sum(grad * hat, axis=0, keepdims=True)

        row_steps(middle.shape[0], HALF, one)


def attend_grad_kernel(
    order, bias, cosine, sine, grad_low, rows_wide, q_in, k_in, v_in, attended, logs, *refs
):
    pieces, refs = refs[:PIECES], refs[PIECES:]
    weight_grads, (query_out, pair_out, grad_keys, grad_values, grad_out) = refs[:5], refs[5:]
    turned, plain = head_masks()
    row_count = grad_low.shape[0]
    low = jnp.bfloat16
    width = 2 * LANES
    grad_out[...] = dot(grad_low[...], wide(pieces, slice(None)), NT).astype(low)
    grad_keys[...] = jnp.zeros_like(grad_keys)
    grad_values[...] = jnp.zeros_like(grad_values)

    def back(values, rows):
        front, rear = values[:, :LANES], values[:, LANES:]
        cos, sin = cosine[rows, :], sine[rows, :]
        return (front * cos + rear * sin, rear * cos - front * sin)

    def block(n, carried):
        rows = pl.ds(pl.multiple_of(n * BLOCK, BLOCK), BLOCK)
        span = pl.ds(pl.multiple_of(n * BLOCK, BLOCK), BLOCK + 2 * HALF)
        queries, keys, values = q_in[0, rows, :], k_in[0, span, :], v_in[0, span, :]
        grad_rows = grad_out[rows, :]
        masked = bias[n]
        log_rows = logs[0, rows, :]
        grad_query = jnp.zeros((BLOCK, width), jnp.float32)
        grad_key = jnp.zeros((BLOCK + 2 * HALF, width), jnp.float32)
        grad_value = jnp.zeros((BLOCK + 2 * HALF, width), jnp.float32)
        for h in range(4):
            query_head, grad_head = queries * turned[h], grad_rows * plain[h]
            scores = dot(query_head, keys, NT) + masked
            probs = jnp.exp(scores - log_rows[:, h : h + 1])
            grad_probs = dot(grad_head, values, NT)
            row_delta = jnp.sum(probs * grad_probs, axis=-1, keepdims=True)
            grad_scores = (probs * (grad_probs - row_delta)).astype(low)
            grad_query = grad_query + dot(grad_scores, keys * turned[h], NN)
            grad_key = grad_key + dot(grad_scores, query_head, TN)
            grad_value = grad_value + dot(probs.astype(low), grad_head, TN)
        place = pl.ds(pl.multiple_of(n * BLOCK + HALF, HALF), BLOCK)
        front, rear = back(grad_query * HEAD_DIM ** (-0.5), place)
        query_out[0, rows, :LANES] = front.astype(low)
        query_out[0, rows, LANES:] = rear.astype(low)
        grad_keys[span, :] += grad_key
        grad_values[span, :] += grad_value
        return carried

    lax.fori_loop(0, bias.shape[0], block, 0)
    front, rear = back(grad_keys[...], slice(None))
    pair_out[0, 0, :, :LANES] = front.astype(low)
    pair_out[0, 0, :, LANES:] = rear.astype(low)
    pair_out[0, 1] = grad_values[...].astype(low)
    inner = slice(HALF, HALF + row_count)
    store_pieces(weight_grads, slice(0, width), dot(query_out[0], rows_wide[inner, :], TN))
    for c in range(2):
        rows = slice((1 + c) * width, (2 + c) * width)
        store_pieces(weight_grads, rows, dot(pair_out[0, c], rows_wide[...], TN))
    store_pieces(weight_grads, slice(3 * width, 4 * width), dot(attended[0], grad_low[...], TN))


def input_grad_kernel(order, hidden, gains, grad_middle, *refs):
    even, odd, (before, after), refs = refs[:2], refs[2:4], refs[4:6], refs[6:]
    pieces, (grad_input, gain_out, mixed, total) = refs[:PIECES], refs[PIECES:]
    step = pl.program_id(0)
    row_count = hidden.shape[0]
    width = 2 * LANES
    last = row_count - HALF

    @pl.when(step == 0)
    def _():
        total[...] = jnp.zeros_like(total)
        gain_out[...] = jnp.zeros_like(gain_out)

    def sum_low(left, right):
        return (left.astype(jnp.float32) + right.astype(jnp.float32)).astype(jnp.bfloat16)

    def add(slab, queries, pairs):
        total[...] += dot(queries[0], wide(pieces, slice(0, width), slab), NN)
        for c in range(2):
            mixed[...] = pairs[0, c, HALF : HALF + row_count, :]
            mixed[0:HALF, :] = sum_low(mixed[0:HALF, :], before[slab, c])
            mixed[last:, :] = sum_low(mixed[last:, :], after[slab, c])
            rows = slice((1 + c) * width, (2 + c) * width)
            total[...] += dot(mixed[...], wide(pieces, rows, slab), NN)

    add(0, *even)
    add(1, *odd)

    @pl.when(step == pl.num_programs(0) - 1)
    def _():
        def one(rows):
            grad = total[rows, :]
            hat, scale = normed(relative(order, hidden, rows).astype(jnp.float32))
            result = grad_middle[rows, :] + norm_pull(hat, scale, gains[0:1, :], grad)
            for n in range(PIECES):
                lanes = pl.ds(pl.multiple_of(order[n] * LANES, LANES), LANES)
                grad_input[rows, lanes] = result[:, n * LANES : (n + 1) * LANES]
            gain_out[0:1, :] += jnp.sum(grad * hat, axis=0, keepdims=True)

        row_steps(row_count, HALF, one)


def local(
    hidden_in,
    seq_lengths,
    cotangent,
    w_qkv,
    w_proj,
    w_in,
    w_down,
    norm_gains,
    qkv_first,
    qkv_second,
    proj_first,
    proj_second,
    in_first,
    in_second,
    down_first,
    down_second,
    gain_first,
    gain_second,
):
    row_count = hidden_in.shape[0]
    wide_count = row_count + 2 * HALF
    size = lax.axis_size("tensor")
    dp_size = lax.axis_size("dp")
    group_rows = row_count * size
    low, full = jnp.bfloat16, jnp.float32
    chunk = norm_gains.shape[1]
    head_wide = w_proj.shape[1]
    head_rows = 4 * head_wide
    slab_rows = head_rows + SLAB_PAD
    hidden_wide = w_down.shape[1]
    head_count, half_dim = head_wide // HEAD_DIM, HEAD_DIM // 2

    def halves_first(weight):
        split = weight.reshape(chunk, 2, head_count, 2, half_dim)
        return jnp.transpose(split, (0, 1, 3, 2, 4)).reshape(chunk, 2 * head_wide)

    def heads_first(weight):
        split = weight.reshape(chunk, 2, 2, head_count, half_dim)
        return jnp.transpose(split, (0, 1, 3, 2, 4)).reshape(chunk, 2, head_wide)

    heads_slab = jnp.concatenate(
        [
            jnp.concatenate(
                [halves_first(w_qkv[:, :2].astype(low)), w_qkv[:, 2].astype(low), w_proj.astype(low)],
                axis=1,
            ).T,
            jnp.pad(norm_gains.astype(low), ((0, SLAB_PAD - 2), (0, 0))),
        ]
    )
    ffn_slab = jnp.concatenate(
        [w_in.astype(low).reshape(chunk, 2 * hidden_wide), w_down.astype(low)], axis=1
    ).T
    if dp_size == PIECES:
        apart = jnp.array([0, 2, 4, 6, 1, 3, 5, 7], jnp.int32)
        order = lax.axis_index("dp").astype(jnp.int32) ^ apart
        hidden, cot_in = hidden_in, cotangent
    else:
        order = jnp.arange(PIECES, dtype=jnp.int32)
        hidden, cot_in = to_relative(hidden_in), to_relative(cotangent)

    edges = (shift(hidden[-HALF:], 1), shift(hidden[:HALF], -1))
    place = lax.axis_index("tensor").astype(jnp.int32)
    place_rows = jnp.full((8, LANES), place)
    heads_near = gather_near(heads_slab, place)
    line_token = held_back(place_rows * 0, heads_near[:1])
    ffn_line = line_gather(tied(ffn_slab, line_token), place)
    in_all = gather_dp(ffn_line[:, : 2 * hidden_wide])
    heads_pieces = [piece.reshape(size, -1, LANES) for piece in gather_far(heads_near)]
    gains = jnp.concatenate(
        [piece[0, head_rows : head_rows + 8] for piece in heads_pieces], axis=1
    ).astype(full)

    first_row = lax.axis_index("tensor") * row_count
    segment, position = layout(
        seq_lengths[0], first_row - HALF + jnp.arange(wide_count), group_rows
    )
    cosine, sine = rotary_tables(position)
    bias = jnp.where(allowed_pairs(segment), 0.0, MASKED).astype(full)

    head_block = (size, row_count, head_wide)
    wide_block = (size, wide_count, head_wide)
    tokens = (row_count, D)
    turned = (size * hidden_wide, row_count)
    turned_spec = pl.BlockSpec((hidden_wide, row_count), lambda n, *_: (n, 0))
    matmul = 2 * row_count * D

    queries, keys, values, rows_wide, token = run(
        heads_kernel,
        "heads",
        [order, (hidden, None), (edges[0], None), (edges[1], None), (gains, None)]
        + [(cosine, None), (sine, None)]
        + [slabs(piece, 3 * head_wide) for piece in heads_pieces],
        [lead_out(head_block, low), lead_out(wide_block, low), lead_out(wide_block, low)]
        + [((wide_count, D), low, None)],
        [],
        3 * matmul * D,
    )
    down_all = gather_dp(tied(ffn_line[:, 2 * hidden_wide :], token))
    attended, logs, token = run(
        attend_kernel,
        "attend",
        [order, (bias, None), lead(queries), lead(keys), lead(values)],
        [lead_out(head_block, low), lead_out((size, row_count, LANES), full)],
        [],
        2 * matmul * D,
    )
    middle, rows_two, token = run(
        proj_kernel,
        "proj",
        [order, (hidden, None), (gains, None), lead(attended)]
        + [slabs(piece, head_wide, first=3) for piece in heads_pieces],
        [(tokens, full, None), (tokens, low, None)],
        [],
        matmul * D,
    )
    active, gate_side, up_side, token = run(
        gate_kernel,
        "gate",
        [order, (rows_two, None)] + gathered(in_all, 2 * hidden_wide),
        [(turned, low, turned_spec)] * 3,
        [
            pltpu.VMEM((D, row_count), low),
            pltpu.VMEM((hidden_wide, row_count), full),
            pltpu.VMEM((hidden_wide, row_count), full),
        ],
        2 * matmul * FF,
    )

    down_grads, cot, token = run(
        down_grad_kernel,
        "down_grad",
        [order, (cot_in, None), turned_block(active, hidden_wide)],
        [gathered_out(size, hidden_wide), (tokens, low, None)],
        [],
        matmul * FF,
    )
    down_sum = scatter_dp(down_grads)
    half = size // 2
    in_grads, gate_grad, up_grad, token = run(
        in_grad_kernel,
        "in_grad",
        [order, (cot, None), (rows_two, None)]
        + [turned_block(gate_side, hidden_wide), turned_block(up_side, hidden_wide)]
        + gathered(down_all, hidden_wide),
        [gathered_out(size, 2 * hidden_wide)] + [(turned, low, turned_spec)] * 2,
        [pltpu.VMEM((D, row_count), low), pltpu.VMEM((hidden_wide, row_count), full)],
        3 * matmul * FF,
    )
    in_sum = scatter_dp(in_grads)
    grad_middle, grad_low, gain_two, token = run(
        middle_grad_kernel,
        "middle_grad",
        [order, (middle, None), (cot, None), (gains, None)]
        + [turned_block(side, hidden_wide) for side in (gate_grad, up_grad)]
        + gathered(in_all, 2 * hidden_wide),
        [(tokens, full, None), (tokens, low, None), ((8, D), full, None)],
        [pltpu.VMEM(tokens, full)],
        2 * matmul * FF,
    )

    def core_hop(outs):
        return (outs[:4], flip(outs[4], 1))

    def core_sums(own, received):
        entries = own[0].shape[0]
        received = received.reshape((-1,) + received.shape[2:])
        return [
            [(part, e), (received, n * entries + e)]
            for n, part in enumerate(own)
            for e in range(entries)
        ]

    def far_hop(sums):
        return (flip(sums[6], 2), flip(sums[7], 4))

    def far_sums(sums, arrived):
        return [[(sums[4],), (arrived[0],)], [(sums[3],), (arrived[1],)]]

    def near_hop(sums, added):
        return (flip(sums[2], 2), flip(added[0], 4), flip(added[1], 2), flip(sums[5], 4))

    def near_sums(sums, arrived):
        return [
            [(sums[0],), (arrived[0],), (arrived[1],)],
            [(sums[1],), (arrived[2],), (arrived[3],)],
        ]

    def attend_grad(part, count, name, after):
        return run(
            attend_grad_kernel,
            name,
            [order, (bias, None), (cosine, None), (sine, None), (grad_low, None), (rows_wide, None)]
            + [lead(array, part) for array in (queries, keys, values, attended, logs)]
            + [slabs(piece, head_wide, part, first=3) for piece in heads_pieces],
            piece_outs(count, head_rows)
            + [
                lead_out((count, row_count, head_wide), low),
                lead_out((count, 2, wide_count, head_wide), low),
            ],
            [
                pltpu.VMEM((wide_count, head_wide), full),
                pltpu.VMEM((wide_count, head_wide), full),
                pltpu.VMEM((row_count, head_wide), low),
            ],
            3 * count * matmul * D,
            after=after,
            steps=count,
        )

    *odd_outs, odd_queries, odd_pairs, token = attend_grad(ODD, half, "attend_grad_odd", ())
    odd_core = core_hop(odd_outs)
    *even_outs, even_queries, even_pairs, token = attend_grad(
        EVEN, half, "attend_grad_even", (token,)
    )
    even_core = core_hop(even_outs)
    odd, token = blend("sums_one", core_sums(*odd_core), (token,))
    odd_far = far_hop(odd)
    pairs = [even_pairs[0], odd_pairs[0], even_pairs[1], odd_pairs[1]]
    edge_after = jnp.stack([pair[:, -HALF:] for pair in pairs[-1:] + pairs[:-1]])
    edge_before = jnp.stack([pair[:, :HALF] for pair in pairs[1:] + pairs[:1]])
    edges = (shift(edge_after, 1), shift(edge_before, -1))
    hidden_out, token = run(
        down_kernel,
        "down",
        [order, (middle, None), turned_block(active, hidden_wide)]
        + gathered(down_all, hidden_wide),
        [(tokens, low, None)],
        [pltpu.VMEM(tokens, full)],
        matmul * FF,
        after=(token,),
    )
    (*even, odd_y, odd_x), token = blend(
        "sums_two", core_sums(*even_core) + far_sums(odd, odd_far), (token,)
    )
    even_far = far_hop(even)
    odd_near = near_hop(odd, (odd_y, odd_x))
    ffn_parts = tied(jnp.concatenate([in_sum, down_sum], axis=1), token)
    ffn_arrived = line_hop(ffn_parts[1], ffn_parts[size - 1], size - 1)
    grad_input, gain_one, token = run(
        input_grad_kernel,
        "input_grad",
        [order, (hidden, None), (gains, None), (grad_middle, None)]
        + [lead(array) for array in (even_queries, even_pairs, odd_queries, odd_pairs)]
        + [lead(array, count=2) for array in edges]
        + [slabs(piece, 3 * head_wide, count=2) for piece in heads_pieces],
        [(tokens, full, None), ((8, D), full, None)],
        [pltpu.VMEM((row_count, head_wide), low), pltpu.VMEM(tokens, full)],
        3 * matmul * D,
        after=(token,),
        steps=half,
    )
    (*odd_parts, even_y, even_x), token = blend(
        "sums_three",
        near_sums(odd, odd_near) + far_sums(even, even_far),
        (token, *ffn_arrived),
    )
    even_near = near_hop(even, (even_y, even_x))
    odd_parts = [far_scatter(part) for part in odd_parts]

    def line_round(parts, step, arrived=None):
        to_after, to_before = parts[size - step], parts[step]
        if arrived is not None:
            to_after, to_before = add_low(to_after, arrived[0]), add_low(to_before, arrived[1])
        return line_hop(to_after, to_before, step)

    ffn_arrived = line_round(ffn_parts, 2, ffn_arrived)
    three_token = token
    even_parts, token = blend("sums_four", near_sums(even, even_near), (token, *ffn_arrived))
    ffn_total = line_end(ffn_parts[0], line_round(ffn_parts, 1, ffn_arrived))
    even_parts = [far_scatter(part) for part in even_parts]
    heads_parts = [even_parts[0], odd_parts[0], even_parts[1], odd_parts[1]]
    heads_arrived = None
    for step in range(size - 1, 0, -1):
        heads_arrived = line_round(heads_parts, step, heads_arrived)
    heads_total = line_end(heads_parts[0], heads_arrived)
    gain_sum = gain_scatter(tied(jnp.concatenate([gain_one[:1], gain_two[:1]]), three_token))
    if dp_size != PIECES:
        hidden_out, grad_input = to_relative(hidden_out, True), to_relative(grad_input, True)

    ffn_total = ffn_total.T
    in_sum = ffn_total[:, : 2 * hidden_wide].reshape(w_in.shape)
    down_sum = ffn_total[:, 2 * hidden_wide :]
    heads_sum = heads_total.T
    qkv_sum = jnp.concatenate(
        [
            heads_first(heads_sum[:, : 2 * head_wide]),
            heads_sum[:, None, 2 * head_wide : 3 * head_wide],
        ],
        axis=1,
    )
    proj_sum = heads_sum[:, 3 * head_wide :]
    qkv_one, qkv_two, qkv_new = adam_update(w_qkv, qkv_sum, qkv_first, qkv_second, D ** (-0.5))
    proj_one, proj_two, proj_new = adam_update(
        w_proj, proj_sum, proj_first, proj_second, (D // HALF) ** (-0.5)
    )
    in_one, in_two, in_new = adam_update(w_in, in_sum, in_first, in_second, D ** (-0.5))
    down_one, down_two, down_new = adam_update(
        w_down, down_sum, down_first, down_second, (FF // 2) ** (-0.5)
    )
    gain_one, gain_two, gains_new = adam_update(
        norm_gains, gain_sum, gain_first, gain_second, GAIN_RATE
    )
    return (
        hidden_out,
        grad_input,
        qkv_one,
        qkv_two,
        qkv_new,
        proj_one,
        proj_two,
        proj_new,
        in_one,
        in_two,
        in_new,
        down_one,
        down_two,
        down_new,
        gain_one,
        gain_two,
        gains_new,
    )


def solution(mesh):
    placed = (
        P(("dp", "tensor"), None),
        P("dp", None),
        P(("dp", "tensor"), None),
        P("dp", None, "tensor"),
        P("dp", "tensor"),
        P("dp", None, "tensor"),
        P("dp", "tensor"),
        P(None, "dp"),
        P("dp", None, "tensor"),
        P("dp", None, "tensor"),
        P("dp", "tensor"),
        P("dp", "tensor"),
        P("dp", None, "tensor"),
        P("dp", None, "tensor"),
        P("dp", "tensor"),
        P("dp", "tensor"),
        P(None, "dp"),
        P(None, "dp"),
    )
    return jax.shard_map(
        local,
        mesh=mesh,
        in_specs=placed,
        out_specs=(
            P(("dp", "tensor"), None),
            P(("dp", "tensor"), None),
            P("dp", None, "tensor"),
            P("dp", None, "tensor"),
            P("dp", None, "tensor"),
            P("dp", "tensor"),
            P("dp", "tensor"),
            P("dp", "tensor"),
            P("dp", None, "tensor"),
            P("dp", None, "tensor"),
            P("dp", None, "tensor"),
            P("dp", "tensor"),
            P("dp", "tensor"),
            P("dp", "tensor"),
            P(None, "dp"),
            P(None, "dp"),
            P(None, "dp"),
        ),
        check_vma=False,
    )
```

```python
import functools
import math

import jax
import jax.numpy as jnp
from jax import lax
from jax.experimental import pallas as pl
from jax.experimental.pallas import tpu as pltpu
from jax.sharding import PartitionSpec as P

D = 1024
HEADS = 16
HEAD_DIM = 64
FF = 2624
HALF = 64
BLOCK = 128
STEP = 10

NORM_EPS = 1e-05
THETA_BASE = 10000.0
BETA_ONE = 0.9
BETA_TWO = 0.98
ADAM_EPS = 1e-06
WEIGHT_DECAY = 0.01
GAIN_RATE = 0.5
MASKED = -1e30


LANES = 128
PIECES = 8
SLAB_PAD = 16
VMEM_BYTES = 52 * 1024 * 1024
COST_FACTOR = 1e-3


def layout(lengths, token_index, group_rows):
    seq_ends = jnp.cumsum(lengths)
    seq_starts = seq_ends - lengths
    segment = jnp.sum((token_index[:, None] >= seq_ends[None, :]).astype(jnp.int32), axis=1)
    member = segment[:, None] == jnp.arange(lengths.shape[0])[None, :]
    position = token_index - jnp.sum(jnp.where(member, seq_starts[None, :], 0), axis=1)
    inside = (token_index >= 0) & (token_index < group_rows)
    return (jnp.where(inside, segment, -1), jnp.where(inside, position, 0))


def rotary_tables(position):
    half_dim = HEAD_DIM // 2
    exponent = jnp.arange(half_dim).astype(jnp.float32) * (2.0 / HEAD_DIM)
    inverse = jnp.power(jnp.float32(THETA_BASE), -exponent)
    angle_table = position.astype(jnp.float32)[:, None] * inverse[None, :]
    copies = LANES // half_dim
    return (jnp.tile(jnp.cos(angle_table), (1, copies)), jnp.tile(jnp.sin(angle_table), (1, copies)))


def windows(rows):
    count = (rows.shape[0] - 2 * HALF) // BLOCK
    return jnp.stack([rows[n * BLOCK : n * BLOCK + BLOCK + 2 * HALF] for n in range(count)])


def allowed_pairs(segment):
    key_seg = windows(segment)
    query_seg = segment[HALF:-HALF].reshape(-1, BLOCK)
    offset = jnp.arange(BLOCK)[:, None] + HALF - jnp.arange(BLOCK + 2 * HALF)[None, :]
    return (query_seg[:, :, None] == key_seg[:, None, :]) & (jnp.abs(offset) <= HALF)[None]


def adam_update(master, gradient, moment_one, moment_two, step_rate):
    one_new = BETA_ONE * moment_one + (1.0 - BETA_ONE) * gradient
    two_new = BETA_TWO * moment_two + (1.0 - BETA_TWO) * gradient * gradient
    one_hat = one_new / (1.0 - BETA_ONE**STEP)
    two_hat = two_new / (1.0 - BETA_TWO**STEP)
    master_new = master - step_rate * (
        one_hat / (jnp.sqrt(two_hat) + ADAM_EPS) + WEIGHT_DECAY * master
    )
    return (one_new, two_new, master_new)


def line_gather(slab, place):
    size = lax.axis_size("tensor")
    from_before, from_after = [slab], [slab]
    for step in range(1, size):
        from_before.append(
            lax.ppermute(from_before[-1], "tensor", [(n, n + 1) for n in range(step - 1, size - 1)])
        )
        from_after.append(
            lax.ppermute(from_after[-1], "tensor", [(n, n - 1) for n in range(1, size - step + 1)])
        )
    return jnp.stack(
        [slab]
        + [
            jnp.where(place >= step, from_before[step], from_after[size - step])
            for step in range(1, size)
        ]
    )


def tied(values, token):
    return values if token is None else jnp.where(token[0, 0] == 0, values, 0.0 * values)


def gather_hop(from_before, from_after, step):
    size = lax.axis_size("tensor")
    return (
        lax.ppermute(from_before, "tensor", [(n, n + 1) for n in range(step - 1, size - 1)]),
        lax.ppermute(from_after, "tensor", [(n, n - 1) for n in range(1, size - step + 1)]),
    )


def line_hop(to_after, to_before, step):
    size = lax.axis_size("tensor")
    return (
        lax.ppermute(to_after, "tensor", [(n, n + 1) for n in range(size - step)]),
        lax.ppermute(to_before, "tensor", [(n, n - 1) for n in range(step, size)]),
    )


def line_end(own, arrived):
    return sum((part.astype(jnp.float32) for part in arrived), own.astype(jnp.float32))


def gain_scatter(gains):
    steps = []
    for mask in [1, 4, 2] + far_bits()[::-1]:
        half = gains.shape[1] // 2
        steps.append(flip(gains[:, half:], mask))
        gains = gains[:, :half] + steps[-1]
    size = lax.axis_size("tensor")
    for mask in (1 << n for n in range(size.bit_length() - 1)):
        steps.append(lax.ppermute(gains, "tensor", [(n, n ^ mask) for n in range(size)]))
        gains = gains + steps[-1]
    return (gains, steps)


def flip(rows, mask):
    return lax.ppermute(rows, "dp", [(n, n ^ mask) for n in range(lax.axis_size("dp"))])


def far_bits():
    size = lax.axis_size("dp")
    return [1 << n for n in range(3, size.bit_length() - 1)]


def gather_near(slab, place):
    piece = line_gather(slab, place)
    piece = piece.reshape(-1, piece.shape[-1])
    for mask in far_bits():
        piece = jnp.concatenate([piece, flip(piece, mask)], axis=1)
    return (piece, flip(piece, 2), flip(piece, 4))


def gather_far_hop(near, token=None):
    piece, by_x, by_y = near
    half = piece.shape[0] // 2
    return (flip(tied(by_x[:half], token), 4), flip(tied(by_y[half:], token), 2))


def gather_far(near, arrived=None, token=None):
    piece, by_x, by_y = near
    if arrived is None:
        arrived = gather_far_hop(near)
    far = tied(jnp.concatenate(arrived), token)
    mine = [piece, by_x, by_y, far]
    return mine + [flip(part, 1) for part in mine]


def add_low(left, right):
    return (left.astype(jnp.float32) + right.astype(jnp.float32)).astype(left.dtype)


def far_scatter(part):
    for mask in reversed(far_bits()):
        half = part.shape[1] // 2
        part = add_low(part[:, :half], flip(part[:, half:], mask))
    return part


def gather_dp(piece):
    if lax.axis_size("dp") == PIECES:
        return lax.all_gather(piece, "dp", axis=0)
    flat = piece.reshape(-1, piece.shape[-1])
    for mask in far_bits():
        flat = jnp.concatenate([flat, flip(flat, mask)], axis=1)
    pieces = gather_far((flat, flip(flat, 2), flip(flat, 4)))
    return jnp.stack(pieces).reshape((PIECES,) + piece.shape[:-1] + (LANES,))


def scatter_dp(grads):
    if lax.axis_size("dp") == PIECES:
        return lax.psum_scatter(grads, "dp", scatter_dimension=0, tiled=False)
    flat = grads.reshape(PIECES, -1, LANES)
    own, by_x, by_y, far = add_low(flat[:4], flip(flat[4:], 1))
    by_y = add_low(by_y, flip(far, 2))
    total = add_low(add_low(own, flip(by_x, 2)), flip(by_y, 4))
    return far_scatter(total).reshape(grads.shape[1:3] + (-1,))


def to_relative(rows, back=False):
    size = lax.axis_size("dp")
    place = lax.axis_index("dp")
    bits = size.bit_length() - 1
    lead = rows.shape[:-1]
    axes = len(lead)
    chunk = rows.shape[-1] // size
    wanted = [bits - 1, bits - 3, bits - 2] + list(range(bits - 3))
    order = list(range(axes)) + [axes + n for n in wanted] + [axes + bits]
    cube = rows.reshape(lead + (2,) * bits + (chunk,))
    if back:
        cube = jnp.transpose(cube, [order.index(n) for n in range(len(order))])
    for n in range(bits):
        cube = jnp.where((place >> (bits - 1 - n)) & 1 == 1, jnp.flip(cube, axes + n), cube)
    if not back:
        cube = jnp.transpose(cube, order)
    return cube.reshape(rows.shape)


def shift(rows, step):
    size = lax.axis_size("tensor")
    pairs = [(n, n + step) for n in range(size) if 0 <= n + step < size]
    return lax.ppermute(rows, "tensor", pairs)


NN = ((1,), (0,))
NT = ((1,), (1,))
TN = ((0,), (0,))


def dot(left, right, dims):
    return lax.dot_general(left, right, (dims, ((), ())), preferred_element_type=jnp.float32)


def wide(pieces, rows, slab=0):
    return jnp.concatenate([piece[slab, rows, :] for piece in pieces], axis=1)


def relative(order, ref, rows):
    return jnp.concatenate(
        [
            ref[rows, pl.ds(pl.multiple_of(order[n] * LANES, LANES), LANES)]
            for n in range(PIECES)
        ],
        axis=1,
    )


def normed(values):
    centered = values - jnp.mean(values, axis=-1, keepdims=True)
    scale = lax.rsqrt(jnp.mean(centered * centered, axis=-1, keepdims=True) + NORM_EPS)
    return (centered * scale, scale)


def norm_pull(hat, scale, gain, grad):
    scaled = grad * gain
    return scale * (
        scaled
        - jnp.mean(scaled, axis=-1, keepdims=True)
        - hat * jnp.mean(scaled * hat, axis=-1, keepdims=True)
    )


def row_steps(count, size, body):
    def step(n, carried):
        body(pl.ds(pl.multiple_of(n * size, size), size))
        return carried

    lax.fori_loop(0, count // size, step, 0)


def whole_spec(array):
    return pl.BlockSpec(array.shape, lambda *_: (0,) * len(array.shape))


def run(kernel, name, operands, outs, scratch, flops, after=(), steps=None):
    order, operands = operands[0], operands[1:]
    specs = [spec if spec is not None else whole_spec(array) for array, spec in operands]
    out_specs = [
        spec if spec is not None else pl.BlockSpec(shape, lambda *_, n=len(shape): (0,) * n)
        for shape, dtype, spec in outs
    ]
    moved = sum(array.size * array.dtype.itemsize for array, _ in operands)
    moved += sum(math.prod(shape) * jnp.dtype(dtype).itemsize for shape, dtype, _ in outs)
    kept, made = len(operands), len(outs)

    def body(order_ref, *refs):
        refs = refs[:kept] + refs[kept + len(after) :]
        token = refs[kept + made]
        token[...] = jnp.zeros_like(token)
        kernel(order_ref, *refs[: kept + made], *refs[kept + made + 1 :])

    return pl.pallas_call(
        body,
        grid_spec=pltpu.PrefetchScalarGridSpec(
            num_scalar_prefetch=1,
            grid=(steps or lax.axis_size("tensor"),),
            in_specs=specs + [pl.BlockSpec(memory_space=pl.ANY)] * len(after),
            out_specs=out_specs + [pl.BlockSpec((8, LANES), lambda *_: (0, 0))],
            scratch_shapes=scratch,
        ),
        out_shape=[jax.ShapeDtypeStruct(shape, dtype) for shape, dtype, _ in outs]
        + [jax.ShapeDtypeStruct((8, LANES), jnp.int32)],
        compiler_params=pltpu.CompilerParams(
            dimension_semantics=("arbitrary",), vmem_limit_bytes=VMEM_BYTES
        ),
        cost_estimate=pl.CostEstimate(
            flops=int(COST_FACTOR * flops), bytes_accessed=LANES, transcendentals=0
        ),
        name=name,
    )(order, *[array for array, _ in operands], *after)


def held_back(value, after):
    def body(value_ref, *refs):
        refs[-1][...] = value_ref[...]

    return pl.pallas_call(
        body,
        in_specs=[pl.BlockSpec(memory_space=pltpu.VMEM)]
        + [pl.BlockSpec(memory_space=pl.ANY)] * len(after),
        out_specs=pl.BlockSpec(memory_space=pltpu.VMEM),
        out_shape=jax.ShapeDtypeStruct(value.shape, value.dtype),
        name="held_back",
    )(value, *after)


def blend(name, jobs, after):
    halves = 2
    operands, specs, out_specs, shapes, counts, cut = [], [], [], [], [], []
    for terms in jobs:
        rows, lanes = terms[0][0].shape[-2:]
        small = rows % (16 * halves) != 0 or rows < 512
        height = rows if small else rows // halves
        for term in terms:
            operands.append(term[0])
            if len(term) == 1:
                specs.append(pl.BlockSpec((height, lanes), lambda i, s=small: (0 if s else i, 0)))
            else:
                specs.append(
                    pl.BlockSpec(
                        (None, height, lanes),
                        lambda i, s=small, n=term[1]: (n, 0 if s else i, 0),
                    )
                )
        out_specs.append(pl.BlockSpec((height, lanes), lambda i, s=small: (0 if s else i, 0)))
        shapes.append(jax.ShapeDtypeStruct((rows, lanes), jnp.bfloat16))
        counts.append(len(terms))
        cut.append(small)

    def body(*refs):
        ins = refs[: len(operands)]
        outs = refs[len(operands) + len(after) :]
        outs[-1][...] = jnp.zeros_like(outs[-1])
        first = 0
        for n, count in enumerate(counts):
            terms = ins[first : first + count]
            first += count

            def add(out=outs[n], terms=terms):
                out[...] = sum(
                    (term[...].astype(jnp.float32) for term in terms[1:]),
                    terms[0][...].astype(jnp.float32),
                ).astype(jnp.bfloat16)

            pl.when((pl.program_id(0) == 0) | (not cut[n]))(add)

    *sums, token = pl.pallas_call(
        body,
        grid=(halves,),
        in_specs=specs + [pl.BlockSpec(memory_space=pl.ANY)] * len(after),
        out_specs=out_specs + [pl.BlockSpec((8, LANES), lambda i: (0, 0))],
        out_shape=shapes + [jax.ShapeDtypeStruct((8, LANES), jnp.int32)],
        compiler_params=pltpu.CompilerParams(
            dimension_semantics=("arbitrary",), vmem_limit_bytes=VMEM_BYTES
        ),
        name=name,
    )(*operands, *after)
    return (sums, token)


ALL, ODD, EVEN = (0, 1), (1, 2), (0, 2)


def slabs(piece, rows, part=ALL, first=0, count=1):
    return (
        piece,
        pl.BlockSpec((count, rows, LANES), lambda n, *_: (part[0] + part[1] * n, first, 0)),
    )


def gathered(array, rows, part=ALL, count=1):
    return [
        (
            array,
            pl.BlockSpec(
                (None, count, rows, LANES),
                lambda n, order, p=p: (order[p], part[0] + part[1] * n, 0, 0),
            ),
        )
        for p in range(PIECES)
    ]


def gathered_out(parts, rows):
    return (
        (PIECES, parts, rows, LANES),
        jnp.bfloat16,
        pl.BlockSpec((PIECES, 1, rows, LANES), lambda n, order: (0, order[PIECES + n], 0, 0)),
    )


def store_gathered(order, ref, rows, values):
    values = values.astype(jnp.bfloat16)
    for n in range(PIECES):
        ref[order[n], 0, rows, :] = values[:, n * LANES : (n + 1) * LANES]


def lead(array, part=ALL, count=1):
    shape = (count,) + array.shape[1:]
    return (
        array,
        pl.BlockSpec(shape, lambda n, *_: (part[0] + part[1] * n,) + (0,) * (len(shape) - 1)),
    )


def turned_block(array, rows, part=ALL):
    return (array, pl.BlockSpec((rows, array.shape[1]), lambda n, *_: (part[0] + part[1] * n, 0)))


def lead_out(shape, dtype):
    return (shape, dtype, pl.BlockSpec((1,) + shape[1:], lambda n, *_: (n,) + (0,) * (len(shape) - 1)))


def piece_outs(parts, rows):
    low = jnp.bfloat16
    own = pl.BlockSpec((1, rows, LANES), lambda n, *_: (n, 0, 0))
    other = pl.BlockSpec((4, 1, rows, LANES), lambda n, *_: (0, n, 0, 0))
    return [((parts, rows, LANES), low, own)] * 4 + [((4, parts, rows, LANES), low, other)]


def store_pieces(refs, rows, values):
    values = values.astype(jnp.bfloat16)
    for n in range(4):
        refs[n][0, rows, :] = values[:, n * LANES : (n + 1) * LANES]
        refs[4][n, 0, rows, :] = values[:, (n + 4) * LANES : (n + 5) * LANES]


def heads_kernel(order, hidden, before, after, gains, cosine, sine, *refs):
    pieces, (q_out, k_out, v_out, rows_wide) = refs[:PIECES], refs[PIECES:]
    row_count = hidden.shape[0]
    gain = gains[0:1, :]

    def norm_rows(source, rows, first):
        values = relative(order, source, rows).astype(jnp.float32)
        return (normed(values)[0] * gain).astype(jnp.bfloat16)

    @pl.when(pl.program_id(0) == 0)
    def _():
        rows_wide[0:HALF, :] = norm_rows(before, slice(0, HALF), 0)
        rows_wide[HALF + row_count :, :] = norm_rows(after, slice(0, HALF), 0)

        def one(rows):
            values = norm_rows(hidden, rows, 0)
            rows_wide[pl.ds(pl.multiple_of(rows.start + HALF, HALF), HALF), :] = values

        row_steps(row_count, HALF, one)

    width = 2 * LANES

    def turned(mixed, rows):
        front, back = mixed[:, :LANES], mixed[:, LANES:]
        cos, sin = cosine[rows, :], sine[rows, :]
        return (front * cos - back * sin, back * cos + front * sin)

    inner = slice(HALF, HALF + row_count)
    scale = HEAD_DIM ** (-0.5)
    front, back = turned(dot(rows_wide[inner, :], wide(pieces, slice(0, width)), NT), inner)
    q_out[0, :, :LANES] = (front.astype(jnp.bfloat16) * scale).astype(jnp.bfloat16)
    q_out[0, :, LANES:] = (back.astype(jnp.bfloat16) * scale).astype(jnp.bfloat16)
    front, back = turned(
        dot(rows_wide[...], wide(pieces, slice(width, 2 * width)), NT), slice(None)
    )
    k_out[0, :, :LANES] = front.astype(jnp.bfloat16)
    k_out[0, :, LANES:] = back.astype(jnp.bfloat16)
    v_out[0] = dot(rows_wide[...], wide(pieces, slice(2 * width, 3 * width)), NT).astype(
        jnp.bfloat16
    )


def head_masks():
    lane = lax.broadcasted_iota(jnp.int32, (1, 2 * LANES), 1)
    turned = [((lane % LANES) // 32 == n).astype(jnp.float32).astype(jnp.bfloat16) for n in range(4)]
    plain = [(lane // HEAD_DIM == n).astype(jnp.float32).astype(jnp.bfloat16) for n in range(4)]
    return (turned, plain)


def attend_kernel(order, bias, q_in, k_in, v_in, out, log_out):
    turned, plain = head_masks()
    lane = lax.broadcasted_iota(jnp.int32, (BLOCK, LANES), 1)

    def block(n, carried):
        rows = pl.ds(pl.multiple_of(n * BLOCK, BLOCK), BLOCK)
        span = pl.ds(pl.multiple_of(n * BLOCK, BLOCK), BLOCK + 2 * HALF)
        queries, keys, values = q_in[0, rows, :], k_in[0, span, :], v_in[0, span, :]
        masked = bias[n]
        total = jnp.zeros((BLOCK, 2 * LANES), jnp.float32)
        logs = jnp.zeros((BLOCK, LANES), jnp.float32)
        for h in range(4):
            scores = dot(queries * turned[h], keys, NT) + masked
            row_top = jnp.max(scores, axis=-1, keepdims=True)
            lifted = jnp.exp(scores - row_top)
            row_total = jnp.sum(lifted, axis=-1, keepdims=True)
            probs_low = (lifted * (1.0 / row_total)).astype(jnp.bfloat16)
            total = total + dot(probs_low, values * plain[h], NN)
            logs = jnp.where(lane == h, row_top + jnp.log(row_total), logs)
        out[0, rows, :] = total.astype(jnp.bfloat16)
        log_out[0, rows, :] = logs
        return carried

    lax.fori_loop(0, bias.shape[0], block, 0)


def proj_kernel(order, hidden, gains, attended, *refs):
    pieces, (middle, rows_two) = refs[:PIECES], refs[PIECES:]
    step = pl.program_id(0)

    @pl.when(step == 0)
    def _():
        def one(rows):
            middle[rows, :] = relative(order, hidden, rows).astype(jnp.float32)

        row_steps(hidden.shape[0], HALF, one)

    middle[...] += dot(attended[0], wide(pieces, slice(None)), NN)

    @pl.when(step == pl.num_programs(0) - 1)
    def _():
        def one(rows):
            rows_two[rows, :] = (normed(middle[rows, :])[0] * gains[1:2, :]).astype(jnp.bfloat16)

        row_steps(hidden.shape[0], HALF, one)


def gate_kernel(order, rows_two, *refs):
    pieces, (active, gate_side, up_side, rows_turned, gate, up) = refs[:PIECES], refs[PIECES:]

    @pl.when(pl.program_id(0) == 0)
    def _():
        rows_turned[...] = rows_two[...].T

    count = gate.shape[0]
    gate[...] = dot(wide(pieces, slice(0, count)), rows_turned[...], NN)
    up[...] = dot(wide(pieces, slice(count, 2 * count)), rows_turned[...], NN)

    def one(rows):
        x, u = gate[rows, :], up[rows, :]
        below = 0.5 * (1.0 + lax.erf(x * (0.5**0.5)))
        density = jnp.exp(-0.5 * x * x) * ((2.0 * math.pi) ** -0.5)
        lifted = x * below
        active[rows, :] = (lifted * u).astype(jnp.bfloat16)
        gate_side[rows, :] = (u * (below + x * density)).astype(jnp.bfloat16)
        up_side[rows, :] = lifted.astype(jnp.bfloat16)

    row_steps(count, 16, one)


def down_kernel(order, middle, active, *refs):
    pieces, (out, total) = refs[:PIECES], refs[PIECES:]
    step = pl.program_id(0)

    @pl.when(step == 0)
    def _():
        total[...] = middle[...]

    total[...] += dot(active[...], wide(pieces, slice(None)), TN)

    @pl.when(step == pl.num_programs(0) - 1)
    def _():
        for n in range(PIECES):
            lanes = pl.ds(pl.multiple_of(order[n] * LANES, LANES), LANES)
            out[:, lanes] = total[:, n * LANES : (n + 1) * LANES].astype(jnp.bfloat16)


def down_grad_kernel(order, cotangent, active, *refs):
    grads, cot_out = refs

    @pl.when(pl.program_id(0) == 0)
    def _():
        def one(rows):
            cot_out[rows, :] = relative(order, cotangent, rows)

        row_steps(cotangent.shape[0], HALF, one)

    store_gathered(order, grads, slice(None), dot(active[...], cot_out[...], NN))


def in_grad_kernel(order, cot, rows_two, gate_side, up_side, *refs):
    pieces, (grads, gate_out, up_out, cot_turned, grad_active) = refs[:PIECES], refs[PIECES:]

    @pl.when(pl.program_id(0) == 0)
    def _():
        cot_turned[...] = cot[...].T

    count = grad_active.shape[0]
    grad_active[...] = dot(wide(pieces, slice(None)), cot_turned[...], NN)

    def one(rows):
        grad = grad_active[rows, :]
        gate_out[rows, :] = (grad * gate_side[rows, :].astype(jnp.float32)).astype(jnp.bfloat16)
        up_out[rows, :] = (grad * up_side[rows, :].astype(jnp.float32)).astype(jnp.bfloat16)

    row_steps(count, 16, one)
    store_gathered(order, grads, slice(0, count), dot(gate_out[...], rows_two[...], NN))
    store_gathered(order, grads, slice(count, 2 * count), dot(up_out[...], rows_two[...], NN))


def middle_grad_kernel(order, middle, cot, gains, *refs):
    sides, pieces, refs = refs[:2], refs[2 : 2 + PIECES], refs[2 + PIECES :]
    grad_middle, grad_low, gain_out, total = refs
    step = pl.program_id(0)
    count = sides[0].shape[0]

    @pl.when(step == 0)
    def _():
        total[...] = jnp.zeros_like(total)
        gain_out[...] = jnp.zeros_like(gain_out)

    for n, side in enumerate(sides):
        total[...] += dot(side[...], wide(pieces, slice(n * count, (n + 1) * count)), TN)

    @pl.when(step == pl.num_programs(0) - 1)
    def _():
        def one(rows):
            grad = total[rows, :]
            hat, scale = normed(middle[rows, :])
            result = cot[rows, :].astype(jnp.float32) + norm_pull(hat, scale, gains[1:2, :], grad)
            grad_middle[rows, :] = result
            grad_low[rows, :] = result.astype(jnp.bfloat16)
            gain_out[0:1, :] += jnp.sum(grad * hat, axis=0, keepdims=True)

        row_steps(middle.shape[0], HALF, one)


def attend_grad_kernel(
    order, bias, cosine, sine, grad_low, rows_wide, q_in, k_in, v_in, attended, logs, *refs
):
    pieces, refs = refs[:PIECES], refs[PIECES:]
    weight_grads, (query_out, pair_out, grad_keys, grad_values, grad_out) = refs[:5], refs[5:]
    turned, plain = head_masks()
    row_count = grad_low.shape[0]
    low = jnp.bfloat16
    width = 2 * LANES
    grad_out[...] = dot(grad_low[...], wide(pieces, slice(None)), NT).astype(low)
    grad_keys[...] = jnp.zeros_like(grad_keys)
    grad_values[...] = jnp.zeros_like(grad_values)

    def back(values, rows):
        front, rear = values[:, :LANES], values[:, LANES:]
        cos, sin = cosine[rows, :], sine[rows, :]
        return (front * cos + rear * sin, rear * cos - front * sin)

    def block(n, carried):
        rows = pl.ds(pl.multiple_of(n * BLOCK, BLOCK), BLOCK)
        span = pl.ds(pl.multiple_of(n * BLOCK, BLOCK), BLOCK + 2 * HALF)
        queries, keys, values = q_in[0, rows, :], k_in[0, span, :], v_in[0, span, :]
        grad_rows = grad_out[rows, :]
        masked = bias[n]
        log_rows = logs[0, rows, :]
        grad_query = jnp.zeros((BLOCK, width), jnp.float32)
        grad_key = jnp.zeros((BLOCK + 2 * HALF, width), jnp.float32)
        grad_value = jnp.zeros((BLOCK + 2 * HALF, width), jnp.float32)
        for h in range(4):
            query_head, grad_head = queries * turned[h], grad_rows * plain[h]
            scores = dot(query_head, keys, NT) + masked
            probs = jnp.exp(scores - log_rows[:, h : h + 1])
            grad_probs = dot(grad_head, values, NT)
            row_delta = jnp.sum(probs * grad_probs, axis=-1, keepdims=True)
            grad_scores = (probs * (grad_probs - row_delta)).astype(low)
            grad_query = grad_query + dot(grad_scores, keys * turned[h], NN)
            grad_key = grad_key + dot(grad_scores, query_head, TN)
            grad_value = grad_value + dot(probs.astype(low), grad_head, TN)
        place = pl.ds(pl.multiple_of(n * BLOCK + HALF, HALF), BLOCK)
        front, rear = back(grad_query * HEAD_DIM ** (-0.5), place)
        query_out[0, rows, :LANES] = front.astype(low)
        query_out[0, rows, LANES:] = rear.astype(low)
        grad_keys[span, :] += grad_key
        grad_values[span, :] += grad_value
        return carried

    lax.fori_loop(0, bias.shape[0], block, 0)
    front, rear = back(grad_keys[...], slice(None))
    pair_out[0, 0, :, :LANES] = front.astype(low)
    pair_out[0, 0, :, LANES:] = rear.astype(low)
    pair_out[0, 1] = grad_values[...].astype(low)
    inner = slice(HALF, HALF + row_count)
    store_pieces(weight_grads, slice(0, width), dot(query_out[0], rows_wide[inner, :], TN))
    for c in range(2):
        rows = slice((1 + c) * width, (2 + c) * width)
        store_pieces(weight_grads, rows, dot(pair_out[0, c], rows_wide[...], TN))
    store_pieces(weight_grads, slice(3 * width, 4 * width), dot(attended[0], grad_low[...], TN))


def input_grad_kernel(order, hidden, gains, grad_middle, *refs):
    even, odd, (before, after), refs = refs[:2], refs[2:4], refs[4:6], refs[6:]
    pieces, (grad_input, gain_out, mixed, total) = refs[:PIECES], refs[PIECES:]
    step = pl.program_id(0)
    row_count = hidden.shape[0]
    width = 2 * LANES
    last = row_count - HALF

    @pl.when(step == 0)
    def _():
        total[...] = jnp.zeros_like(total)
        gain_out[...] = jnp.zeros_like(gain_out)

    def sum_low(left, right):
        return (left.astype(jnp.float32) + right.astype(jnp.float32)).astype(jnp.bfloat16)

    def add(slab, queries, pairs):
        total[...] += dot(queries[0], wide(pieces, slice(0, width), slab), NN)
        for c in range(2):
            mixed[...] = pairs[0, c, HALF : HALF + row_count, :]
            mixed[0:HALF, :] = sum_low(mixed[0:HALF, :], before[slab, c])
            mixed[last:, :] = sum_low(mixed[last:, :], after[slab, c])
            rows = slice((1 + c) * width, (2 + c) * width)
            total[...] += dot(mixed[...], wide(pieces, rows, slab), NN)

    add(0, *even)
    add(1, *odd)

    @pl.when(step == pl.num_programs(0) - 1)
    def _():
        def one(rows):
            grad = total[rows, :]
            hat, scale = normed(relative(order, hidden, rows).astype(jnp.float32))
            result = grad_middle[rows, :] + norm_pull(hat, scale, gains[0:1, :], grad)
            for n in range(PIECES):
                lanes = pl.ds(pl.multiple_of(order[n] * LANES, LANES), LANES)
                grad_input[rows, lanes] = result[:, n * LANES : (n + 1) * LANES]
            gain_out[0:1, :] += jnp.sum(grad * hat, axis=0, keepdims=True)

        row_steps(row_count, HALF, one)


def local(
    hidden_in,
    seq_lengths,
    cotangent,
    w_qkv,
    w_proj,
    w_in,
    w_down,
    norm_gains,
    qkv_first,
    qkv_second,
    proj_first,
    proj_second,
    in_first,
    in_second,
    down_first,
    down_second,
    gain_first,
    gain_second,
):
    row_count = hidden_in.shape[0]
    wide_count = row_count + 2 * HALF
    size = lax.axis_size("tensor")
    dp_size = lax.axis_size("dp")
    group_rows = row_count * size
    low, full = jnp.bfloat16, jnp.float32
    chunk = norm_gains.shape[1]
    head_wide = w_proj.shape[1]
    head_rows = 4 * head_wide
    slab_rows = head_rows + SLAB_PAD
    hidden_wide = w_down.shape[1]
    head_count, half_dim = head_wide // HEAD_DIM, HEAD_DIM // 2

    def halves_first(weight):
        split = weight.reshape(chunk, 2, head_count, 2, half_dim)
        return jnp.transpose(split, (0, 1, 3, 2, 4)).reshape(chunk, 2 * head_wide)

    def heads_first(weight):
        split = weight.reshape(chunk, 2, 2, head_count, half_dim)
        return jnp.transpose(split, (0, 1, 3, 2, 4)).reshape(chunk, 2, head_wide)

    heads_slab = jnp.concatenate(
        [
            jnp.concatenate(
                [halves_first(w_qkv[:, :2].astype(low)), w_qkv[:, 2].astype(low), w_proj.astype(low)],
                axis=1,
            ).T,
            jnp.pad(norm_gains.astype(low), ((0, SLAB_PAD - 2), (0, 0))),
        ]
    )
    ffn_slab = jnp.concatenate(
        [w_in.astype(low).reshape(chunk, 2 * hidden_wide), w_down.astype(low)], axis=1
    ).T
    if dp_size == PIECES:
        apart = jnp.array([0, 2, 4, 6, 1, 3, 5, 7], jnp.int32)
        order = lax.axis_index("dp").astype(jnp.int32) ^ apart
        hidden, cot_in = hidden_in, cotangent
    else:
        order = jnp.arange(PIECES, dtype=jnp.int32)
        hidden, cot_in = to_relative(hidden_in), to_relative(cotangent)

    place = lax.axis_index("tensor").astype(jnp.int32)
    owners = (place + size - jnp.arange(size, dtype=jnp.int32)) % size
    order = jnp.concatenate([order, owners])
    edges = (shift(hidden[-HALF:], 1), shift(hidden[:HALF], -1))
    zeros = jnp.zeros((8, LANES), jnp.int32)
    heads_near = gather_near(heads_slab, place)
    ffn_slab = tied(ffn_slab, held_back(zeros, heads_near[:1]))
    first = gather_hop(ffn_slab, ffn_slab, 1)
    token = held_back(zeros, (*heads_near[1:], *first))
    heads_far = gather_far_hop(heads_near, token)
    second = gather_hop(tied(first[0], token), tied(first[1], token), 2)
    token = held_back(zeros, (*heads_far, *second))
    third = gather_hop(tied(second[0], token), tied(second[1], token), 3)
    ffn_line = jnp.stack(
        [
            ffn_slab,
            jnp.where(place >= 1, first[0], third[1]),
            jnp.where(place >= 2, second[0], second[1]),
            jnp.where(place >= 3, third[0], first[1]),
        ]
    )
    in_all = gather_dp(ffn_line[:, : 2 * hidden_wide])
    heads_pieces = [
        piece.reshape(size, -1, LANES) for piece in gather_far(heads_near, heads_far, token)
    ]
    gains = jnp.concatenate(
        [piece[0, head_rows : head_rows + 8] for piece in heads_pieces], axis=1
    ).astype(full)

    first_row = lax.axis_index("tensor") * row_count
    segment, position = layout(
        seq_lengths[0], first_row - HALF + jnp.arange(wide_count), group_rows
    )
    cosine, sine = rotary_tables(position)
    bias = jnp.where(allowed_pairs(segment), 0.0, MASKED).astype(full)

    head_block = (size, row_count, head_wide)
    wide_block = (size, wide_count, head_wide)
    tokens = (row_count, D)
    turned = (size * hidden_wide, row_count)
    turned_spec = pl.BlockSpec((hidden_wide, row_count), lambda n, *_: (n, 0))
    matmul = 2 * row_count * D

    queries, keys, values, rows_wide, token = run(
        heads_kernel,
        "heads",
        [order, (hidden, None), (edges[0], None), (edges[1], None), (gains, None)]
        + [(cosine, None), (sine, None)]
        + [slabs(piece, 3 * head_wide) for piece in heads_pieces],
        [lead_out(head_block, low), lead_out(wide_block, low), lead_out(wide_block, low)]
        + [((wide_count, D), low, None)],
        [],
        3 * matmul * D,
    )
    down_all = gather_dp(tied(ffn_line[:, 2 * hidden_wide :], token))
    attended, logs, token = run(
        attend_kernel,
        "attend",
        [order, (bias, None), lead(queries), lead(keys), lead(values)],
        [lead_out(head_block, low), lead_out((size, row_count, LANES), full)],
        [],
        2 * matmul * D,
    )
    middle, rows_two, token = run(
        proj_kernel,
        "proj",
        [order, (hidden, None), (gains, None), lead(attended)]
        + [slabs(piece, head_wide, first=3) for piece in heads_pieces],
        [(tokens, full, None), (tokens, low, None)],
        [],
        matmul * D,
    )
    active, gate_side, up_side, token = run(
        gate_kernel,
        "gate",
        [order, (rows_two, None)] + gathered(in_all, 2 * hidden_wide),
        [(turned, low, turned_spec)] * 3,
        [
            pltpu.VMEM((D, row_count), low),
            pltpu.VMEM((hidden_wide, row_count), full),
            pltpu.VMEM((hidden_wide, row_count), full),
        ],
        2 * matmul * FF,
    )

    down_grads, cot, token = run(
        down_grad_kernel,
        "down_grad",
        [order, (cot_in, None), turned_block(active, hidden_wide)],
        [gathered_out(size, hidden_wide), (tokens, low, None)],
        [],
        matmul * FF,
    )
    down_line = scatter_dp(down_grads)
    down_sum = lax.psum_scatter(down_line, "tensor", scatter_dimension=0, tiled=False)
    half = size // 2
    in_grads, gate_grad, up_grad, token = run(
        in_grad_kernel,
        "in_grad",
        [order, (cot, None), (rows_two, None)]
        + [turned_block(gate_side, hidden_wide), turned_block(up_side, hidden_wide)]
        + gathered(down_all, hidden_wide),
        [gathered_out(size, 2 * hidden_wide)] + [(turned, low, turned_spec)] * 2,
        [pltpu.VMEM((D, row_count), low), pltpu.VMEM((hidden_wide, row_count), full)],
        3 * matmul * FF,
    )
    in_line = scatter_dp(in_grads)
    in_sum = lax.psum_scatter(in_line, "tensor", scatter_dimension=0, tiled=False)
    grad_middle, grad_low, gain_two, token = run(
        middle_grad_kernel,
        "middle_grad",
        [order, (middle, None), (cot, None), (gains, None)]
        + [turned_block(side, hidden_wide) for side in (gate_grad, up_grad)]
        + gathered(in_all, 2 * hidden_wide),
        [(tokens, full, None), (tokens, low, None), ((8, D), full, None)],
        [pltpu.VMEM(tokens, full)],
        2 * matmul * FF,
    )

    def core_hop(outs):
        return (outs[:4], flip(outs[4], 1))

    def core_sums(own, received):
        entries = own[0].shape[0]
        received = received.reshape((-1,) + received.shape[2:])
        return [
            [(part, e), (received, n * entries + e)]
            for n, part in enumerate(own)
            for e in range(entries)
        ]

    def far_hop(sums):
        return (flip(sums[6], 2), flip(sums[7], 4))

    def far_sums(sums, arrived):
        return [[(sums[4],), (arrived[0],)], [(sums[3],), (arrived[1],)]]

    def near_hop(sums, added):
        return (flip(sums[2], 2), flip(added[0], 4), flip(added[1], 2), flip(sums[5], 4))

    def near_sums(sums, arrived):
        return [
            [(sums[0],), (arrived[0],), (arrived[1],)],
            [(sums[1],), (arrived[2],), (arrived[3],)],
        ]

    def attend_grad(part, count, name, after):
        return run(
            attend_grad_kernel,
            name,
            [order, (bias, None), (cosine, None), (sine, None), (grad_low, None), (rows_wide, None)]
            + [lead(array, part) for array in (queries, keys, values, attended, logs)]
            + [slabs(piece, head_wide, part, first=3) for piece in heads_pieces],
            piece_outs(count, head_rows)
            + [
                lead_out((count, row_count, head_wide), low),
                lead_out((count, 2, wide_count, head_wide), low),
            ],
            [
                pltpu.VMEM((wide_count, head_wide), full),
                pltpu.VMEM((wide_count, head_wide), full),
                pltpu.VMEM((row_count, head_wide), low),
            ],
            3 * count * matmul * D,
            after=after,
            steps=count,
        )

    *odd_outs, odd_queries, odd_pairs, token = attend_grad(ODD, half, "attend_grad_odd", ())
    odd_core = core_hop(odd_outs)
    *even_outs, even_queries, even_pairs, token = attend_grad(
        EVEN, half, "attend_grad_even", (token, down_line)
    )
    even_core = core_hop(even_outs)
    odd, token = blend("sums_one", core_sums(*odd_core), (token,))
    odd_far = far_hop(odd)
    pairs = [even_pairs[0], odd_pairs[0], even_pairs[1], odd_pairs[1]]
    edge_after = jnp.stack([pair[:, -HALF:] for pair in pairs[-1:] + pairs[:-1]])
    edge_before = jnp.stack([pair[:, :HALF] for pair in pairs[1:] + pairs[:1]])
    edges = (shift(edge_after, 1), shift(edge_before, -1))
    grad_input, gain_one, token = run(
        input_grad_kernel,
        "input_grad",
        [order, (hidden, None), (gains, None), (grad_middle, None)]
        + [lead(array) for array in (even_queries, even_pairs, odd_queries, odd_pairs)]
        + [lead(array, count=2) for array in edges]
        + [slabs(piece, 3 * head_wide, count=2) for piece in heads_pieces],
        [(tokens, full, None), ((8, D), full, None)],
        [pltpu.VMEM((row_count, head_wide), low), pltpu.VMEM(tokens, full)],
        3 * matmul * D,
        after=(token,),
        steps=half,
    )
    (*even, odd_y, odd_x), token = blend(
        "sums_two", core_sums(*even_core) + far_sums(odd, odd_far), (token, in_line)
    )
    even_far = far_hop(even)
    odd_near = near_hop(odd, (odd_y, odd_x))
    gain_sum, gain_steps = gain_scatter(tied(jnp.concatenate([gain_one[:1], gain_two[:1]]), token))
    hidden_out, token = run(
        down_kernel,
        "down",
        [order, (middle, None), turned_block(active, hidden_wide)]
        + gathered(down_all, hidden_wide),
        [(tokens, low, None)],
        [pltpu.VMEM(tokens, full)],
        matmul * FF,
        after=(token,),
    )
    (*odd_parts, even_y, even_x), token = blend(
        "sums_three",
        near_sums(odd, odd_near) + far_sums(even, even_far),
        (token, down_sum, gain_steps[1]),
    )
    even_near = near_hop(even, (even_y, even_x))
    odd_parts = [far_scatter(part) for part in odd_parts]

    def line_round(parts, step, arrived=None):
        to_after, to_before = parts[size - step], parts[step]
        if arrived is not None:
            to_after, to_before = add_low(to_after, arrived[0]), add_low(to_before, arrived[1])
        return line_hop(to_after, to_before, step)

    even_parts, token = blend("sums_four", near_sums(even, even_near), (token, in_sum, gain_steps[3]))
    even_parts = [far_scatter(part) for part in even_parts]
    heads_parts = [even_parts[0], odd_parts[0], even_parts[1], odd_parts[1]]
    heads_arrived = None
    for step in range(size - 1, 0, -1):
        heads_arrived = line_round(heads_parts, step, heads_arrived)
    heads_total = line_end(heads_parts[0], heads_arrived)
    if dp_size != PIECES:
        hidden_out, grad_input = to_relative(hidden_out, True), to_relative(grad_input, True)

    in_sum = in_sum.astype(full).T.reshape(w_in.shape)
    down_sum = down_sum.astype(full).T
    heads_sum = heads_total.T
    qkv_sum = jnp.concatenate(
        [
            heads_first(heads_sum[:, : 2 * head_wide]),
            heads_sum[:, None, 2 * head_wide : 3 * head_wide],
        ],
        axis=1,
    )
    proj_sum = heads_sum[:, 3 * head_wide :]
    qkv_one, qkv_two, qkv_new = adam_update(w_qkv, qkv_sum, qkv_first, qkv_second, D ** (-0.5))
    proj_one, proj_two, proj_new = adam_update(
        w_proj, proj_sum, proj_first, proj_second, (D // HALF) ** (-0.5)
    )
    in_one, in_two, in_new = adam_update(w_in, in_sum, in_first, in_second, D ** (-0.5))
    down_one, down_two, down_new = adam_update(
        w_down, down_sum, down_first, down_second, (FF // 2) ** (-0.5)
    )
    gain_one, gain_two, gains_new = adam_update(
        norm_gains, gain_sum, gain_first, gain_second, GAIN_RATE
    )
    return (
        hidden_out,
        grad_input,
        qkv_one,
        qkv_two,
        qkv_new,
        proj_one,
        proj_two,
        proj_new,
        in_one,
        in_two,
        in_new,
        down_one,
        down_two,
        down_new,
        gain_one,
        gain_two,
        gains_new,
    )


def solution(mesh):
    placed = (
        P(("dp", "tensor"), None),
        P("dp", None),
        P(("dp", "tensor"), None),
        P("dp", None, "tensor"),
        P("dp", "tensor"),
        P("dp", None, "tensor"),
        P("dp", "tensor"),
        P(None, "dp"),
        P("dp", None, "tensor"),
        P("dp", None, "tensor"),
        P("dp", "tensor"),
        P("dp", "tensor"),
        P("dp", None, "tensor"),
        P("dp", None, "tensor"),
        P("dp", "tensor"),
        P("dp", "tensor"),
        P(None, "dp"),
        P(None, "dp"),
    )
    return jax.shard_map(
        local,
        mesh=mesh,
        in_specs=placed,
        out_specs=(
            P(("dp", "tensor"), None),
            P(("dp", "tensor"), None),
            P("dp", None, "tensor"),
            P("dp", None, "tensor"),
            P("dp", None, "tensor"),
            P("dp", "tensor"),
            P("dp", "tensor"),
            P("dp", "tensor"),
            P("dp", None, "tensor"),
            P("dp", None, "tensor"),
            P("dp", None, "tensor"),
            P("dp", "tensor"),
            P("dp", "tensor"),
            P("dp", "tensor"),
            P(None, "dp"),
            P(None, "dp"),
            P(None, "dp"),
        ),
        check_vma=False,
    )
```

```python
import functools
import math

import jax
import jax.numpy as jnp
from jax import lax
from jax.experimental import pallas as pl
from jax.experimental.pallas import tpu as pltpu
from jax.sharding import PartitionSpec as P

D = 1024
HEADS = 16
HEAD_DIM = 64
FF = 2624
HALF = 64
BLOCK = 128
STEP = 10

NORM_EPS = 1e-05
THETA_BASE = 10000.0
BETA_ONE = 0.9
BETA_TWO = 0.98
ADAM_EPS = 1e-06
WEIGHT_DECAY = 0.01
GAIN_RATE = 0.5
MASKED = -1e30


LANES = 128
PIECES = 8
SLAB_PAD = 16
VMEM_BYTES = 52 * 1024 * 1024
COST_FACTOR = 1e-3


def layout(lengths, token_index, group_rows):
    seq_ends = jnp.cumsum(lengths)
    seq_starts = seq_ends - lengths
    segment = jnp.sum((token_index[:, None] >= seq_ends[None, :]).astype(jnp.int32), axis=1)
    member = segment[:, None] == jnp.arange(lengths.shape[0])[None, :]
    position = token_index - jnp.sum(jnp.where(member, seq_starts[None, :], 0), axis=1)
    inside = (token_index >= 0) & (token_index < group_rows)
    return (jnp.where(inside, segment, -1), jnp.where(inside, position, 0))


def rotary_tables(position):
    half_dim = HEAD_DIM // 2
    exponent = jnp.arange(half_dim).astype(jnp.float32) * (2.0 / HEAD_DIM)
    inverse = jnp.power(jnp.float32(THETA_BASE), -exponent)
    angle_table = position.astype(jnp.float32)[:, None] * inverse[None, :]
    copies = LANES // half_dim
    return (jnp.tile(jnp.cos(angle_table), (1, copies)), jnp.tile(jnp.sin(angle_table), (1, copies)))


def windows(rows):
    count = (rows.shape[0] - 2 * HALF) // BLOCK
    return jnp.stack([rows[n * BLOCK : n * BLOCK + BLOCK + 2 * HALF] for n in range(count)])


def allowed_pairs(segment):
    key_seg = windows(segment)
    query_seg = segment[HALF:-HALF].reshape(-1, BLOCK)
    offset = jnp.arange(BLOCK)[:, None] + HALF - jnp.arange(BLOCK + 2 * HALF)[None, :]
    return (query_seg[:, :, None] == key_seg[:, None, :]) & (jnp.abs(offset) <= HALF)[None]


def adam_update(master, gradient, moment_one, moment_two, step_rate):
    one_new = BETA_ONE * moment_one + (1.0 - BETA_ONE) * gradient
    two_new = BETA_TWO * moment_two + (1.0 - BETA_TWO) * gradient * gradient
    one_hat = one_new / (1.0 - BETA_ONE**STEP)
    two_hat = two_new / (1.0 - BETA_TWO**STEP)
    master_new = master - step_rate * (
        one_hat / (jnp.sqrt(two_hat) + ADAM_EPS) + WEIGHT_DECAY * master
    )
    return (one_new, two_new, master_new)


def line_gather(slab, place):
    size = lax.axis_size("tensor")
    from_before, from_after = [slab], [slab]
    for step in range(1, size):
        from_before.append(
            lax.ppermute(from_before[-1], "tensor", [(n, n + 1) for n in range(step - 1, size - 1)])
        )
        from_after.append(
            lax.ppermute(from_after[-1], "tensor", [(n, n - 1) for n in range(1, size - step + 1)])
        )
    return jnp.stack(
        [slab]
        + [
            jnp.where(place >= step, from_before[step], from_after[size - step])
            for step in range(1, size)
        ]
    )


def tied(values, token):
    return values if token is None else jnp.where(token[0, 0] == 0, values, 0.0 * values)


def gather_hop(from_before, from_after, step):
    size = lax.axis_size("tensor")
    return (
        lax.ppermute(from_before, "tensor", [(n, n + 1) for n in range(step - 1, size - 1)]),
        lax.ppermute(from_after, "tensor", [(n, n - 1) for n in range(1, size - step + 1)]),
    )


def line_hop(to_after, to_before, step):
    size = lax.axis_size("tensor")
    return (
        lax.ppermute(to_after, "tensor", [(n, n + 1) for n in range(size - step)]),
        lax.ppermute(to_before, "tensor", [(n, n - 1) for n in range(step, size)]),
    )


def line_end(own, arrived):
    return sum((part.astype(jnp.float32) for part in arrived), own.astype(jnp.float32))


def gain_scatter(gains):
    steps = []
    for mask in [1, 4, 2] + far_bits()[::-1]:
        half = gains.shape[1] // 2
        steps.append(flip(gains[:, half:], mask))
        gains = gains[:, :half] + steps[-1]
    size = lax.axis_size("tensor")
    for mask in (1 << n for n in range(size.bit_length() - 1)):
        steps.append(lax.ppermute(gains, "tensor", [(n, n ^ mask) for n in range(size)]))
        gains = gains + steps[-1]
    return (gains, steps)


def flip(rows, mask):
    return lax.ppermute(rows, "dp", [(n, n ^ mask) for n in range(lax.axis_size("dp"))])


def far_bits():
    size = lax.axis_size("dp")
    return [1 << n for n in range(3, size.bit_length() - 1)]


def gather_near(slab, place):
    piece = line_gather(slab, place)
    piece = piece.reshape(-1, piece.shape[-1])
    for mask in far_bits():
        piece = jnp.concatenate([piece, flip(piece, mask)], axis=1)
    return (piece, flip(piece, 2), flip(piece, 4))


def gather_far_hop(near, token=None):
    piece, by_x, by_y = near
    half = piece.shape[0] // 2
    return (flip(tied(by_x[:half], token), 4), flip(tied(by_y[half:], token), 2))


def gather_far(near, arrived=None, token=None):
    piece, by_x, by_y = near
    if arrived is None:
        arrived = gather_far_hop(near)
    far = tied(jnp.concatenate(arrived), token)
    mine = [piece, by_x, by_y, far]
    return mine + [flip(part, 1) for part in mine]


def add_low(left, right):
    return (left.astype(jnp.float32) + right.astype(jnp.float32)).astype(left.dtype)


def far_scatter(part):
    for mask in reversed(far_bits()):
        half = part.shape[1] // 2
        part = add_low(part[:, :half], flip(part[:, half:], mask))
    return part


def gather_dp(piece):
    if lax.axis_size("dp") == PIECES:
        return lax.all_gather(piece, "dp", axis=0)
    flat = piece.reshape(-1, piece.shape[-1])
    for mask in far_bits():
        flat = jnp.concatenate([flat, flip(flat, mask)], axis=1)
    pieces = gather_far((flat, flip(flat, 2), flip(flat, 4)))
    return jnp.stack(pieces).reshape((PIECES,) + piece.shape[:-1] + (LANES,))


def scatter_dp(grads):
    if lax.axis_size("dp") == PIECES:
        return lax.psum_scatter(grads, "dp", scatter_dimension=0, tiled=False)
    flat = grads.reshape(PIECES, -1, LANES)
    own, by_x, by_y, far = add_low(flat[:4], flip(flat[4:], 1))
    by_y = add_low(by_y, flip(far, 2))
    total = add_low(add_low(own, flip(by_x, 2)), flip(by_y, 4))
    return far_scatter(total).reshape(grads.shape[1:3] + (-1,))


def to_relative(rows, back=False):
    size = lax.axis_size("dp")
    place = lax.axis_index("dp")
    bits = size.bit_length() - 1
    lead = rows.shape[:-1]
    axes = len(lead)
    chunk = rows.shape[-1] // size
    wanted = [bits - 1, bits - 3, bits - 2] + list(range(bits - 3))
    order = list(range(axes)) + [axes + n for n in wanted] + [axes + bits]
    cube = rows.reshape(lead + (2,) * bits + (chunk,))
    if back:
        cube = jnp.transpose(cube, [order.index(n) for n in range(len(order))])
    for n in range(bits):
        cube = jnp.where((place >> (bits - 1 - n)) & 1 == 1, jnp.flip(cube, axes + n), cube)
    if not back:
        cube = jnp.transpose(cube, order)
    return cube.reshape(rows.shape)


def shift(rows, step):
    size = lax.axis_size("tensor")
    pairs = [(n, n + step) for n in range(size) if 0 <= n + step < size]
    return lax.ppermute(rows, "tensor", pairs)


NN = ((1,), (0,))
NT = ((1,), (1,))
TN = ((0,), (0,))


def dot(left, right, dims):
    return lax.dot_general(left, right, (dims, ((), ())), preferred_element_type=jnp.float32)


def wide(pieces, rows, slab=0):
    return jnp.concatenate([piece[slab, rows, :] for piece in pieces], axis=1)


def relative(order, ref, rows):
    return jnp.concatenate(
        [
            ref[rows, pl.ds(pl.multiple_of(order[n] * LANES, LANES), LANES)]
            for n in range(PIECES)
        ],
        axis=1,
    )


def normed(values):
    centered = values - jnp.mean(values, axis=-1, keepdims=True)
    scale = lax.rsqrt(jnp.mean(centered * centered, axis=-1, keepdims=True) + NORM_EPS)
    return (centered * scale, scale)


def norm_pull(hat, scale, gain, grad):
    scaled = grad * gain
    return scale * (
        scaled
        - jnp.mean(scaled, axis=-1, keepdims=True)
        - hat * jnp.mean(scaled * hat, axis=-1, keepdims=True)
    )


def row_steps(count, size, body):
    def step(n, carried):
        body(pl.ds(pl.multiple_of(n * size, size), size))
        return carried

    lax.fori_loop(0, count // size, step, 0)


def whole_spec(array):
    return pl.BlockSpec(array.shape, lambda *_: (0,) * len(array.shape))


def run(kernel, name, operands, outs, scratch, flops, after=(), steps=None):
    order, operands = operands[0], operands[1:]
    specs = [spec if spec is not None else whole_spec(array) for array, spec in operands]
    out_specs = [
        spec if spec is not None else pl.BlockSpec(shape, lambda *_, n=len(shape): (0,) * n)
        for shape, dtype, spec in outs
    ]
    moved = sum(array.size * array.dtype.itemsize for array, _ in operands)
    moved += sum(math.prod(shape) * jnp.dtype(dtype).itemsize for shape, dtype, _ in outs)
    kept, made = len(operands), len(outs)

    def body(order_ref, *refs):
        refs = refs[:kept] + refs[kept + len(after) :]
        token = refs[kept + made]
        token[...] = jnp.zeros_like(token)
        kernel(order_ref, *refs[: kept + made], *refs[kept + made + 1 :])

    return pl.pallas_call(
        body,
        grid_spec=pltpu.PrefetchScalarGridSpec(
            num_scalar_prefetch=1,
            grid=(steps or lax.axis_size("tensor"),),
            in_specs=specs + [pl.BlockSpec(memory_space=pl.ANY)] * len(after),
            out_specs=out_specs + [pl.BlockSpec((8, LANES), lambda *_: (0, 0))],
            scratch_shapes=scratch,
        ),
        out_shape=[jax.ShapeDtypeStruct(shape, dtype) for shape, dtype, _ in outs]
        + [jax.ShapeDtypeStruct((8, LANES), jnp.int32)],
        compiler_params=pltpu.CompilerParams(
            dimension_semantics=("arbitrary",), vmem_limit_bytes=VMEM_BYTES
        ),
        cost_estimate=pl.CostEstimate(
            flops=int(COST_FACTOR * flops), bytes_accessed=LANES, transcendentals=0
        ),
        name=name,
    )(order, *[array for array, _ in operands], *after)


def held_back(value, after):
    def body(value_ref, *refs):
        refs[-1][...] = value_ref[...]

    return pl.pallas_call(
        body,
        in_specs=[pl.BlockSpec(memory_space=pltpu.VMEM)]
        + [pl.BlockSpec(memory_space=pl.ANY)] * len(after),
        out_specs=pl.BlockSpec(memory_space=pltpu.VMEM),
        out_shape=jax.ShapeDtypeStruct(value.shape, value.dtype),
        name="held_back",
    )(value, *after)


def blend(name, jobs, after):
    halves = 2
    operands, specs, out_specs, shapes, counts, cut = [], [], [], [], [], []
    for terms in jobs:
        rows, lanes = terms[0][0].shape[-2:]
        small = rows % (16 * halves) != 0 or rows < 512
        height = rows if small else rows // halves
        for term in terms:
            operands.append(term[0])
            if len(term) == 1:
                specs.append(pl.BlockSpec((height, lanes), lambda i, s=small: (0 if s else i, 0)))
            else:
                specs.append(
                    pl.BlockSpec(
                        (None, height, lanes),
                        lambda i, s=small, n=term[1]: (n, 0 if s else i, 0),
                    )
                )
        out_specs.append(pl.BlockSpec((height, lanes), lambda i, s=small: (0 if s else i, 0)))
        shapes.append(jax.ShapeDtypeStruct((rows, lanes), jnp.bfloat16))
        counts.append(len(terms))
        cut.append(small)

    def body(*refs):
        ins = refs[: len(operands)]
        outs = refs[len(operands) + len(after) :]
        outs[-1][...] = jnp.zeros_like(outs[-1])
        first = 0
        for n, count in enumerate(counts):
            terms = ins[first : first + count]
            first += count

            def add(out=outs[n], terms=terms):
                out[...] = sum(
                    (term[...].astype(jnp.float32) for term in terms[1:]),
                    terms[0][...].astype(jnp.float32),
                ).astype(jnp.bfloat16)

            pl.when((pl.program_id(0) == 0) | (not cut[n]))(add)

    *sums, token = pl.pallas_call(
        body,
        grid=(halves,),
        in_specs=specs + [pl.BlockSpec(memory_space=pl.ANY)] * len(after),
        out_specs=out_specs + [pl.BlockSpec((8, LANES), lambda i: (0, 0))],
        out_shape=shapes + [jax.ShapeDtypeStruct((8, LANES), jnp.int32)],
        compiler_params=pltpu.CompilerParams(
            dimension_semantics=("arbitrary",), vmem_limit_bytes=VMEM_BYTES
        ),
        name=name,
    )(*operands, *after)
    return (sums, token)


ALL, ODD, EVEN = (0, 1), (1, 2), (0, 2)


def slabs(piece, rows, part=ALL, first=0, count=1):
    return (
        piece,
        pl.BlockSpec((count, rows, LANES), lambda n, *_: (part[0] + part[1] * n, first, 0)),
    )


def gathered(array, rows, part=ALL, count=1):
    return [
        (
            array,
            pl.BlockSpec(
                (None, count, rows, LANES),
                lambda n, order, p=p: (order[p], part[0] + part[1] * n, 0, 0),
            ),
        )
        for p in range(PIECES)
    ]


def gathered_out(parts, rows):
    return (
        (PIECES, parts, rows, LANES),
        jnp.bfloat16,
        pl.BlockSpec((PIECES, 1, rows, LANES), lambda n, order: (0, order[PIECES + n], 0, 0)),
    )


def store_gathered(order, ref, rows, values):
    values = values.astype(jnp.bfloat16)
    for n in range(PIECES):
        ref[order[n], 0, rows, :] = values[:, n * LANES : (n + 1) * LANES]


def lead(array, part=ALL, count=1):
    shape = (count,) + array.shape[1:]
    return (
        array,
        pl.BlockSpec(shape, lambda n, *_: (part[0] + part[1] * n,) + (0,) * (len(shape) - 1)),
    )


def turned_block(array, rows, part=ALL):
    return (array, pl.BlockSpec((rows, array.shape[1]), lambda n, *_: (part[0] + part[1] * n, 0)))


def lead_out(shape, dtype):
    return (shape, dtype, pl.BlockSpec((1,) + shape[1:], lambda n, *_: (n,) + (0,) * (len(shape) - 1)))


def piece_outs(parts, rows):
    low = jnp.bfloat16
    own = pl.BlockSpec((1, rows, LANES), lambda n, *_: (n, 0, 0))
    other = pl.BlockSpec((4, 1, rows, LANES), lambda n, *_: (0, n, 0, 0))
    return [((parts, rows, LANES), low, own)] * 4 + [((4, parts, rows, LANES), low, other)]


def store_pieces(refs, rows, values):
    values = values.astype(jnp.bfloat16)
    for n in range(4):
        refs[n][0, rows, :] = values[:, n * LANES : (n + 1) * LANES]
        refs[4][n, 0, rows, :] = values[:, (n + 4) * LANES : (n + 5) * LANES]


def heads_kernel(order, hidden, before, after, gains, cosine, sine, *refs):
    pieces, (q_out, k_out, v_out, rows_wide) = refs[:PIECES], refs[PIECES:]
    row_count = hidden.shape[0]
    gain = gains[0:1, :]

    def norm_rows(source, rows, first):
        values = relative(order, source, rows).astype(jnp.float32)
        return (normed(values)[0] * gain).astype(jnp.bfloat16)

    @pl.when(pl.program_id(0) == 0)
    def _():
        rows_wide[0:HALF, :] = norm_rows(before, slice(0, HALF), 0)
        rows_wide[HALF + row_count :, :] = norm_rows(after, slice(0, HALF), 0)

        def one(rows):
            values = norm_rows(hidden, rows, 0)
            rows_wide[pl.ds(pl.multiple_of(rows.start + HALF, HALF), HALF), :] = values

        row_steps(row_count, HALF, one)

    width = 2 * LANES

    def turned(mixed, rows):
        front, back = mixed[:, :LANES], mixed[:, LANES:]
        cos, sin = cosine[rows, :], sine[rows, :]
        return (front * cos - back * sin, back * cos + front * sin)

    inner = slice(HALF, HALF + row_count)
    scale = HEAD_DIM ** (-0.5)
    front, back = turned(dot(rows_wide[inner, :], wide(pieces, slice(0, width)), NT), inner)
    q_out[0, :, :LANES] = (front.astype(jnp.bfloat16) * scale).astype(jnp.bfloat16)
    q_out[0, :, LANES:] = (back.astype(jnp.bfloat16) * scale).astype(jnp.bfloat16)
    front, back = turned(
        dot(rows_wide[...], wide(pieces, slice(width, 2 * width)), NT), slice(None)
    )
    k_out[0, :, :LANES] = front.astype(jnp.bfloat16)
    k_out[0, :, LANES:] = back.astype(jnp.bfloat16)
    v_out[0] = dot(rows_wide[...], wide(pieces, slice(2 * width, 3 * width)), NT).astype(
        jnp.bfloat16
    )


def head_masks():
    lane = lax.broadcasted_iota(jnp.int32, (1, 2 * LANES), 1)
    turned = [((lane % LANES) // 32 == n).astype(jnp.float32).astype(jnp.bfloat16) for n in range(4)]
    plain = [(lane // HEAD_DIM == n).astype(jnp.float32).astype(jnp.bfloat16) for n in range(4)]
    return (turned, plain)


def attend_kernel(order, bias, q_in, k_in, v_in, out, log_out):
    turned, plain = head_masks()
    lane = lax.broadcasted_iota(jnp.int32, (BLOCK, LANES), 1)

    def block(n, carried):
        rows = pl.ds(pl.multiple_of(n * BLOCK, BLOCK), BLOCK)
        span = pl.ds(pl.multiple_of(n * BLOCK, BLOCK), BLOCK + 2 * HALF)
        queries, keys, values = q_in[0, rows, :], k_in[0, span, :], v_in[0, span, :]
        masked = bias[n]
        total = jnp.zeros((BLOCK, 2 * LANES), jnp.float32)
        logs = jnp.zeros((BLOCK, LANES), jnp.float32)
        for h in range(4):
            scores = dot(queries * turned[h], keys, NT) + masked
            row_top = jnp.max(scores, axis=-1, keepdims=True)
            lifted = jnp.exp(scores - row_top)
            row_total = jnp.sum(lifted, axis=-1, keepdims=True)
            probs_low = (lifted * (1.0 / row_total)).astype(jnp.bfloat16)
            total = total + dot(probs_low, values * plain[h], NN)
            logs = jnp.where(lane == h, row_top + jnp.log(row_total), logs)
        out[0, rows, :] = total.astype(jnp.bfloat16)
        log_out[0, rows, :] = logs
        return carried

    lax.fori_loop(0, bias.shape[0], block, 0)


def proj_kernel(order, hidden, gains, attended, *refs):
    pieces, (middle, rows_two) = refs[:PIECES], refs[PIECES:]
    step = pl.program_id(0)

    @pl.when(step == 0)
    def _():
        def one(rows):
            middle[rows, :] = relative(order, hidden, rows).astype(jnp.float32)

        row_steps(hidden.shape[0], HALF, one)

    middle[...] += dot(attended[0], wide(pieces, slice(None)), NN)

    @pl.when(step == pl.num_programs(0) - 1)
    def _():
        def one(rows):
            rows_two[rows, :] = (normed(middle[rows, :])[0] * gains[1:2, :]).astype(jnp.bfloat16)

        row_steps(hidden.shape[0], HALF, one)


def gate_kernel(order, rows_two, *refs):
    pieces, (active, gate_side, up_side, rows_turned, gate, up) = refs[:PIECES], refs[PIECES:]

    @pl.when(pl.program_id(0) == 0)
    def _():
        rows_turned[...] = rows_two[...].T

    count = gate.shape[0]
    gate[...] = dot(wide(pieces, slice(0, count)), rows_turned[...], NN)
    up[...] = dot(wide(pieces, slice(count, 2 * count)), rows_turned[...], NN)

    def one(rows):
        x, u = gate[rows, :], up[rows, :]
        below = 0.5 * (1.0 + lax.erf(x * (0.5**0.5)))
        density = jnp.exp(-0.5 * x * x) * ((2.0 * math.pi) ** -0.5)
        lifted = x * below
        active[rows, :] = (lifted * u).astype(jnp.bfloat16)
        gate_side[rows, :] = (u * (below + x * density)).astype(jnp.bfloat16)
        up_side[rows, :] = lifted.astype(jnp.bfloat16)

    row_steps(count, 16, one)


def down_kernel(order, middle, active, *refs):
    pieces, (out, total) = refs[:PIECES], refs[PIECES:]
    step = pl.program_id(0)

    @pl.when(step == 0)
    def _():
        total[...] = middle[...]

    total[...] += dot(active[...], wide(pieces, slice(None)), TN)

    @pl.when(step == pl.num_programs(0) - 1)
    def _():
        for n in range(PIECES):
            lanes = pl.ds(pl.multiple_of(order[n] * LANES, LANES), LANES)
            out[:, lanes] = total[:, n * LANES : (n + 1) * LANES].astype(jnp.bfloat16)


def down_grad_kernel(order, cotangent, active, *refs):
    grads, cot_out = refs

    @pl.when(pl.program_id(0) == 0)
    def _():
        def one(rows):
            cot_out[rows, :] = relative(order, cotangent, rows)

        row_steps(cotangent.shape[0], HALF, one)

    store_gathered(order, grads, slice(None), dot(active[...], cot_out[...], NN))


def in_grad_kernel(order, cot, rows_two, gate_side, up_side, *refs):
    pieces, (grads, gate_out, up_out, cot_turned, grad_active) = refs[:PIECES], refs[PIECES:]

    @pl.when(pl.program_id(0) == 0)
    def _():
        cot_turned[...] = cot[...].T

    count = grad_active.shape[0]
    grad_active[...] = dot(wide(pieces, slice(None)), cot_turned[...], NN)

    def one(rows):
        grad = grad_active[rows, :]
        gate_out[rows, :] = (grad * gate_side[rows, :].astype(jnp.float32)).astype(jnp.bfloat16)
        up_out[rows, :] = (grad * up_side[rows, :].astype(jnp.float32)).astype(jnp.bfloat16)

    row_steps(count, 16, one)
    store_gathered(order, grads, slice(0, count), dot(gate_out[...], rows_two[...], NN))
    store_gathered(order, grads, slice(count, 2 * count), dot(up_out[...], rows_two[...], NN))


def middle_grad_kernel(order, middle, cot, gains, *refs):
    sides, pieces, refs = refs[:2], refs[2 : 2 + PIECES], refs[2 + PIECES :]
    grad_middle, grad_low, gain_out, total = refs
    step = pl.program_id(0)
    count = sides[0].shape[0]

    @pl.when(step == 0)
    def _():
        total[...] = jnp.zeros_like(total)
        gain_out[...] = jnp.zeros_like(gain_out)

    for n, side in enumerate(sides):
        total[...] += dot(side[...], wide(pieces, slice(n * count, (n + 1) * count)), TN)

    @pl.when(step == pl.num_programs(0) - 1)
    def _():
        def one(rows):
            grad = total[rows, :]
            hat, scale = normed(middle[rows, :])
            result = cot[rows, :].astype(jnp.float32) + norm_pull(hat, scale, gains[1:2, :], grad)
            grad_middle[rows, :] = result
            grad_low[rows, :] = result.astype(jnp.bfloat16)
            gain_out[0:1, :] += jnp.sum(grad * hat, axis=0, keepdims=True)

        row_steps(middle.shape[0], HALF, one)


def attend_grad_kernel(
    order, bias, cosine, sine, grad_low, rows_wide, q_in, k_in, v_in, attended, logs, *refs
):
    pieces, refs = refs[:PIECES], refs[PIECES:]
    weight_grads, (query_out, pair_out, grad_keys, grad_values, grad_out) = refs[:5], refs[5:]
    turned, plain = head_masks()
    row_count = grad_low.shape[0]
    low = jnp.bfloat16
    width = 2 * LANES
    grad_out[...] = dot(grad_low[...], wide(pieces, slice(None)), NT).astype(low)
    grad_keys[...] = jnp.zeros_like(grad_keys)
    grad_values[...] = jnp.zeros_like(grad_values)

    def back(values, rows):
        front, rear = values[:, :LANES], values[:, LANES:]
        cos, sin = cosine[rows, :], sine[rows, :]
        return (front * cos + rear * sin, rear * cos - front * sin)

    def block(n, carried):
        rows = pl.ds(pl.multiple_of(n * BLOCK, BLOCK), BLOCK)
        span = pl.ds(pl.multiple_of(n * BLOCK, BLOCK), BLOCK + 2 * HALF)
        queries, keys, values = q_in[0, rows, :], k_in[0, span, :], v_in[0, span, :]
        grad_rows = grad_out[rows, :]
        masked = bias[n]
        log_rows = logs[0, rows, :]
        grad_query = jnp.zeros((BLOCK, width), jnp.float32)
        grad_key = jnp.zeros((BLOCK + 2 * HALF, width), jnp.float32)
        grad_value = jnp.zeros((BLOCK + 2 * HALF, width), jnp.float32)
        for h in range(4):
            query_head, grad_head = queries * turned[h], grad_rows * plain[h]
            scores = dot(query_head, keys, NT) + masked
            probs = jnp.exp(scores - log_rows[:, h : h + 1])
            grad_probs = dot(grad_head, values, NT)
            row_delta = jnp.sum(probs * grad_probs, axis=-1, keepdims=True)
            grad_scores = (probs * (grad_probs - row_delta)).astype(low)
            grad_query = grad_query + dot(grad_scores, keys * turned[h], NN)
            grad_key = grad_key + dot(grad_scores, query_head, TN)
            grad_value = grad_value + dot(probs.astype(low), grad_head, TN)
        place = pl.ds(pl.multiple_of(n * BLOCK + HALF, HALF), BLOCK)
        front, rear = back(grad_query * HEAD_DIM ** (-0.5), place)
        query_out[0, rows, :LANES] = front.astype(low)
        query_out[0, rows, LANES:] = rear.astype(low)
        grad_keys[span, :] += grad_key
        grad_values[span, :] += grad_value
        return carried

    lax.fori_loop(0, bias.shape[0], block, 0)
    front, rear = back(grad_keys[...], slice(None))
    pair_out[0, 0, :, :LANES] = front.astype(low)
    pair_out[0, 0, :, LANES:] = rear.astype(low)
    pair_out[0, 1] = grad_values[...].astype(low)
    inner = slice(HALF, HALF + row_count)
    store_pieces(weight_grads, slice(0, width), dot(query_out[0], rows_wide[inner, :], TN))
    for c in range(2):
        rows = slice((1 + c) * width, (2 + c) * width)
        store_pieces(weight_grads, rows, dot(pair_out[0, c], rows_wide[...], TN))
    store_pieces(weight_grads, slice(3 * width, 4 * width), dot(attended[0], grad_low[...], TN))


def input_grad_kernel(order, hidden, gains, grad_middle, *refs):
    even, odd, (before, after), refs = refs[:2], refs[2:4], refs[4:6], refs[6:]
    pieces, (grad_input, gain_out, mixed, total) = refs[:PIECES], refs[PIECES:]
    step = pl.program_id(0)
    row_count = hidden.shape[0]
    width = 2 * LANES
    last = row_count - HALF

    @pl.when(step == 0)
    def _():
        total[...] = jnp.zeros_like(total)
        gain_out[...] = jnp.zeros_like(gain_out)

    def sum_low(left, right):
        return (left.astype(jnp.float32) + right.astype(jnp.float32)).astype(jnp.bfloat16)

    def add(slab, queries, pairs):
        total[...] += dot(queries[0], wide(pieces, slice(0, width), slab), NN)
        for c in range(2):
            mixed[...] = pairs[0, c, HALF : HALF + row_count, :]
            mixed[0:HALF, :] = sum_low(mixed[0:HALF, :], before[slab, c])
            mixed[last:, :] = sum_low(mixed[last:, :], after[slab, c])
            rows = slice((1 + c) * width, (2 + c) * width)
            total[...] += dot(mixed[...], wide(pieces, rows, slab), NN)

    add(0, *even)
    add(1, *odd)

    @pl.when(step == pl.num_programs(0) - 1)
    def _():
        def one(rows):
            grad = total[rows, :]
            hat, scale = normed(relative(order, hidden, rows).astype(jnp.float32))
            result = grad_middle[rows, :] + norm_pull(hat, scale, gains[0:1, :], grad)
            for n in range(PIECES):
                lanes = pl.ds(pl.multiple_of(order[n] * LANES, LANES), LANES)
                grad_input[rows, lanes] = result[:, n * LANES : (n + 1) * LANES]
            gain_out[0:1, :] += jnp.sum(grad * hat, axis=0, keepdims=True)

        row_steps(row_count, HALF, one)


def local(
    hidden_in,
    seq_lengths,
    cotangent,
    w_qkv,
    w_proj,
    w_in,
    w_down,
    norm_gains,
    qkv_first,
    qkv_second,
    proj_first,
    proj_second,
    in_first,
    in_second,
    down_first,
    down_second,
    gain_first,
    gain_second,
):
    row_count = hidden_in.shape[0]
    wide_count = row_count + 2 * HALF
    size = lax.axis_size("tensor")
    dp_size = lax.axis_size("dp")
    group_rows = row_count * size
    low, full = jnp.bfloat16, jnp.float32
    chunk = norm_gains.shape[1]
    head_wide = w_proj.shape[1]
    head_rows = 4 * head_wide
    slab_rows = head_rows + SLAB_PAD
    hidden_wide = w_down.shape[1]
    head_count, half_dim = head_wide // HEAD_DIM, HEAD_DIM // 2

    def halves_first(weight):
        split = weight.reshape(chunk, 2, head_count, 2, half_dim)
        return jnp.transpose(split, (0, 1, 3, 2, 4)).reshape(chunk, 2 * head_wide)

    def heads_first(weight):
        split = weight.reshape(chunk, 2, 2, head_count, half_dim)
        return jnp.transpose(split, (0, 1, 3, 2, 4)).reshape(chunk, 2, head_wide)

    heads_slab = jnp.concatenate(
        [
            jnp.concatenate(
                [halves_first(w_qkv[:, :2].astype(low)), w_qkv[:, 2].astype(low), w_proj.astype(low)],
                axis=1,
            ).T,
            jnp.pad(norm_gains.astype(low), ((0, SLAB_PAD - 2), (0, 0))),
        ]
    )
    ffn_slab = jnp.concatenate(
        [w_in.astype(low).reshape(chunk, 2 * hidden_wide), w_down.astype(low)], axis=1
    ).T
    if dp_size == PIECES:
        apart = jnp.array([0, 2, 4, 6, 1, 3, 5, 7], jnp.int32)
        order = lax.axis_index("dp").astype(jnp.int32) ^ apart
        hidden, cot_in = hidden_in, cotangent
    else:
        order = jnp.arange(PIECES, dtype=jnp.int32)
        hidden, cot_in = to_relative(hidden_in), to_relative(cotangent)

    place = lax.axis_index("tensor").astype(jnp.int32)
    owners = (place + size - jnp.arange(size, dtype=jnp.int32)) % size
    order = jnp.concatenate([order, owners])
    edges = (shift(hidden[-HALF:], 1), shift(hidden[:HALF], -1))
    zeros = jnp.zeros((8, LANES), jnp.int32)
    heads_near = gather_near(heads_slab, place)
    ffn_slab = tied(ffn_slab, held_back(zeros, heads_near[:1]))
    first = gather_hop(ffn_slab, ffn_slab, 1)
    second = gather_hop(*first, 2)
    token = held_back(zeros, (*heads_near[1:], *second))
    heads_far = gather_far_hop(heads_near, token)
    third = gather_hop(tied(second[0], token), tied(second[1], token), 3)
    start = place + held_back(zeros, (*heads_far, *third))[0, 0]
    ffn_line = jnp.stack(
        [
            ffn_slab,
            jnp.where(start >= 1, first[0], third[1]),
            jnp.where(start >= 2, second[0], second[1]),
            jnp.where(start >= 3, third[0], first[1]),
        ]
    )
    in_all = gather_dp(ffn_line[:, : 2 * hidden_wide])
    heads_pieces = [
        piece.reshape(size, -1, LANES) for piece in gather_far(heads_near, heads_far)
    ]
    gains = jnp.concatenate(
        [piece[0, head_rows : head_rows + 8] for piece in heads_pieces], axis=1
    ).astype(full)

    first_row = lax.axis_index("tensor") * row_count
    segment, position = layout(
        seq_lengths[0], first_row - HALF + jnp.arange(wide_count), group_rows
    )
    cosine, sine = rotary_tables(position)
    bias = jnp.where(allowed_pairs(segment), 0.0, MASKED).astype(full)

    head_block = (size, row_count, head_wide)
    wide_block = (size, wide_count, head_wide)
    tokens = (row_count, D)
    turned = (size * hidden_wide, row_count)
    turned_spec = pl.BlockSpec((hidden_wide, row_count), lambda n, *_: (n, 0))
    matmul = 2 * row_count * D

    queries, keys, values, rows_wide, token = run(
        heads_kernel,
        "heads",
        [order, (hidden, None), (edges[0], None), (edges[1], None), (gains, None)]
        + [(cosine, None), (sine, None)]
        + [slabs(piece, 3 * head_wide) for piece in heads_pieces],
        [lead_out(head_block, low), lead_out(wide_block, low), lead_out(wide_block, low)]
        + [((wide_count, D), low, None)],
        [],
        3 * matmul * D,
    )
    down_all = gather_dp(tied(ffn_line[:, 2 * hidden_wide :], token))
    attended, logs, token = run(
        attend_kernel,
        "attend",
        [order, (bias, None), lead(queries), lead(keys), lead(values)],
        [lead_out(head_block, low), lead_out((size, row_count, LANES), full)],
        [],
        2 * matmul * D,
    )
    middle, rows_two, token = run(
        proj_kernel,
        "proj",
        [order, (hidden, None), (gains, None), lead(attended)]
        + [slabs(piece, head_wide, first=3) for piece in heads_pieces],
        [(tokens, full, None), (tokens, low, None)],
        [],
        matmul * D,
    )
    active, gate_side, up_side, token = run(
        gate_kernel,
        "gate",
        [order, (rows_two, None)] + gathered(in_all, 2 * hidden_wide),
        [(turned, low, turned_spec)] * 3,
        [
            pltpu.VMEM((D, row_count), low),
            pltpu.VMEM((hidden_wide, row_count), full),
            pltpu.VMEM((hidden_wide, row_count), full),
        ],
        2 * matmul * FF,
    )

    down_grads, cot, token = run(
        down_grad_kernel,
        "down_grad",
        [order, (cot_in, None), turned_block(active, hidden_wide)],
        [gathered_out(size, hidden_wide), (tokens, low, None)],
        [],
        matmul * FF,
    )
    down_line = scatter_dp(down_grads)
    half = size // 2
    in_grads, gate_grad, up_grad, token = run(
        in_grad_kernel,
        "in_grad",
        [order, (cot, None), (rows_two, None)]
        + [turned_block(gate_side, hidden_wide), turned_block(up_side, hidden_wide)]
        + gathered(down_all, hidden_wide),
        [gathered_out(size, 2 * hidden_wide)] + [(turned, low, turned_spec)] * 2,
        [pltpu.VMEM((D, row_count), low), pltpu.VMEM((hidden_wide, row_count), full)],
        3 * matmul * FF,
    )
    in_line = scatter_dp(in_grads)
    grad_middle, grad_low, gain_two, token = run(
        middle_grad_kernel,
        "middle_grad",
        [order, (middle, None), (cot, None), (gains, None)]
        + [turned_block(side, hidden_wide) for side in (gate_grad, up_grad)]
        + gathered(in_all, 2 * hidden_wide),
        [(tokens, full, None), (tokens, low, None), ((8, D), full, None)],
        [pltpu.VMEM(tokens, full)],
        2 * matmul * FF,
    )

    def core_hop(outs):
        return (outs[:4], flip(outs[4], 1))

    def core_sums(own, received):
        entries = own[0].shape[0]
        received = received.reshape((-1,) + received.shape[2:])
        return [
            [(part, e), (received, n * entries + e)]
            for n, part in enumerate(own)
            for e in range(entries)
        ]

    def far_hop(sums):
        return (flip(sums[6], 2), flip(sums[7], 4))

    def far_sums(sums, arrived):
        return [[(sums[4],), (arrived[0],)], [(sums[3],), (arrived[1],)]]

    def near_hop(sums, added):
        return (flip(sums[2], 2), flip(added[0], 4), flip(added[1], 2), flip(sums[5], 4))

    def near_sums(sums, arrived):
        return [
            [(sums[0],), (arrived[0],), (arrived[1],)],
            [(sums[1],), (arrived[2],), (arrived[3],)],
        ]

    def attend_grad(part, count, name, after):
        return run(
            attend_grad_kernel,
            name,
            [order, (bias, None), (cosine, None), (sine, None), (grad_low, None), (rows_wide, None)]
            + [lead(array, part) for array in (queries, keys, values, attended, logs)]
            + [slabs(piece, head_wide, part, first=3) for piece in heads_pieces],
            piece_outs(count, head_rows)
            + [
                lead_out((count, row_count, head_wide), low),
                lead_out((count, 2, wide_count, head_wide), low),
            ],
            [
                pltpu.VMEM((wide_count, head_wide), full),
                pltpu.VMEM((wide_count, head_wide), full),
                pltpu.VMEM((row_count, head_wide), low),
            ],
            3 * count * matmul * D,
            after=after,
            steps=count,
        )

    *odd_outs, odd_queries, odd_pairs, token = attend_grad(ODD, half, "attend_grad_odd", ())
    odd_core = core_hop(odd_outs)
    *even_outs, even_queries, even_pairs, token = attend_grad(
        EVEN, half, "attend_grad_even", (token,)
    )
    even_core, even_token = core_hop(even_outs), token
    odd, token = blend("sums_one", core_sums(*odd_core), (token,))
    odd_far = far_hop(odd)
    pairs = [even_pairs[0], odd_pairs[0], even_pairs[1], odd_pairs[1]]
    edge_after = jnp.stack([pair[:, -HALF:] for pair in pairs[-1:] + pairs[:-1]])
    edge_before = jnp.stack([pair[:, :HALF] for pair in pairs[1:] + pairs[:1]])
    edges = (shift(edge_after, 1), shift(edge_before, -1))
    down_sum = lax.psum_scatter(
        tied(down_line, even_token), "tensor", scatter_dimension=0, tiled=False
    )
    hidden_out, token = run(
        down_kernel,
        "down",
        [order, (middle, None), turned_block(active, hidden_wide)]
        + gathered(down_all, hidden_wide),
        [(tokens, low, None)],
        [pltpu.VMEM(tokens, full)],
        matmul * FF,
        after=(token,),
    )
    (*even, odd_y, odd_x), token = blend(
        "sums_two", core_sums(*even_core) + far_sums(odd, odd_far), (token,)
    )
    even_far = far_hop(even)
    odd_near = near_hop(odd, (odd_y, odd_x))
    grad_input, gain_one, token = run(
        input_grad_kernel,
        "input_grad",
        [order, (hidden, None), (gains, None), (grad_middle, None)]
        + [lead(array) for array in (even_queries, even_pairs, odd_queries, odd_pairs)]
        + [lead(array, count=2) for array in edges]
        + [slabs(piece, 3 * head_wide, count=2) for piece in heads_pieces],
        [(tokens, full, None), ((8, D), full, None)],
        [pltpu.VMEM((row_count, head_wide), low), pltpu.VMEM(tokens, full)],
        3 * matmul * D,
        after=(token,),
        steps=half,
    )
    in_sum = lax.psum_scatter(
        tied(in_line, token), "tensor", scatter_dimension=0, tiled=False
    )
    (*odd_parts, even_y, even_x), token = blend(
        "sums_three",
        near_sums(odd, odd_near) + far_sums(even, even_far),
        (token,),
    )
    even_near = near_hop(even, (even_y, even_x))
    odd_parts = [far_scatter(part) for part in odd_parts]

    def line_round(parts, step, arrived=None):
        to_after, to_before = parts[size - step], parts[step]
        if arrived is not None:
            to_after, to_before = add_low(to_after, arrived[0]), add_low(to_before, arrived[1])
        return line_hop(to_after, to_before, step)

    even_parts, token = blend("sums_four", near_sums(even, even_near), (token, down_sum))
    gain_sum, _ = gain_scatter(tied(jnp.concatenate([gain_one[:1], gain_two[:1]]), token))
    even_parts = [far_scatter(part) for part in even_parts]
    heads_parts = [even_parts[0], odd_parts[0], even_parts[1], odd_parts[1]]
    heads_arrived = line_round(heads_parts, 3)
    heads_arrived = line_round(heads_parts, 2, heads_arrived)
    last_token = held_back(zeros, (in_sum, *heads_arrived))
    heads_parts[1:] = [tied(part, last_token) for part in heads_parts[1:]]
    heads_arrived = line_round(heads_parts, 1, heads_arrived)
    heads_total = line_end(heads_parts[0], heads_arrived)
    if dp_size != PIECES:
        hidden_out, grad_input = to_relative(hidden_out, True), to_relative(grad_input, True)

    in_sum = in_sum.astype(full).T.reshape(w_in.shape)
    down_sum = down_sum.astype(full).T
    heads_sum = heads_total.T
    qkv_sum = jnp.concatenate(
        [
            heads_first(heads_sum[:, : 2 * head_wide]),
            heads_sum[:, None, 2 * head_wide : 3 * head_wide],
        ],
        axis=1,
    )
    proj_sum = heads_sum[:, 3 * head_wide :]
    qkv_one, qkv_two, qkv_new = adam_update(w_qkv, qkv_sum, qkv_first, qkv_second, D ** (-0.5))
    proj_one, proj_two, proj_new = adam_update(
        w_proj, proj_sum, proj_first, proj_second, (D // HALF) ** (-0.5)
    )
    in_one, in_two, in_new = adam_update(w_in, in_sum, in_first, in_second, D ** (-0.5))
    down_one, down_two, down_new = adam_update(
        w_down, down_sum, down_first, down_second, (FF // 2) ** (-0.5)
    )
    gain_one, gain_two, gains_new = adam_update(
        norm_gains, gain_sum, gain_first, gain_second, GAIN_RATE
    )
    return (
        hidden_out,
        grad_input,
        qkv_one,
        qkv_two,
        qkv_new,
        proj_one,
        proj_two,
        proj_new,
        in_one,
        in_two,
        in_new,
        down_one,
        down_two,
        down_new,
        gain_one,
        gain_two,
        gains_new,
    )


def solution(mesh):
    placed = (
        P(("dp", "tensor"), None),
        P("dp", None),
        P(("dp", "tensor"), None),
        P("dp", None, "tensor"),
        P("dp", "tensor"),
        P("dp", None, "tensor"),
        P("dp", "tensor"),
        P(None, "dp"),
        P("dp", None, "tensor"),
        P("dp", None, "tensor"),
        P("dp", "tensor"),
        P("dp", "tensor"),
        P("dp", None, "tensor"),
        P("dp", None, "tensor"),
        P("dp", "tensor"),
        P("dp", "tensor"),
        P(None, "dp"),
        P(None, "dp"),
    )
    return jax.shard_map(
        local,
        mesh=mesh,
        in_specs=placed,
        out_specs=(
            P(("dp", "tensor"), None),
            P(("dp", "tensor"), None),
            P("dp", None, "tensor"),
            P("dp", None, "tensor"),
            P("dp", None, "tensor"),
            P("dp", "tensor"),
            P("dp", "tensor"),
            P("dp", "tensor"),
            P("dp", None, "tensor"),
            P("dp", None, "tensor"),
            P("dp", None, "tensor"),
            P("dp", "tensor"),
            P("dp", "tensor"),
            P("dp", "tensor"),
            P(None, "dp"),
            P(None, "dp"),
            P(None, "dp"),
        ),
        check_vma=False,
    )
```

```python
import functools
import math

import jax
import jax.numpy as jnp
from jax import lax
from jax.experimental import pallas as pl
from jax.experimental.pallas import tpu as pltpu
from jax.sharding import PartitionSpec as P

D = 1024
HEADS = 16
HEAD_DIM = 64
FF = 2624
HALF = 64
BLOCK = 128
STEP = 10

NORM_EPS = 1e-05
THETA_BASE = 10000.0
BETA_ONE = 0.9
BETA_TWO = 0.98
ADAM_EPS = 1e-06
WEIGHT_DECAY = 0.01
GAIN_RATE = 0.5
MASKED = -1e30


LANES = 128
PIECES = 8
SLAB_PAD = 16
VMEM_BYTES = 52 * 1024 * 1024
COST_FACTOR = 1e-3


def layout(lengths, token_index, group_rows):
    seq_ends = jnp.cumsum(lengths)
    seq_starts = seq_ends - lengths
    segment = jnp.sum((token_index[:, None] >= seq_ends[None, :]).astype(jnp.int32), axis=1)
    member = segment[:, None] == jnp.arange(lengths.shape[0])[None, :]
    position = token_index - jnp.sum(jnp.where(member, seq_starts[None, :], 0), axis=1)
    inside = (token_index >= 0) & (token_index < group_rows)
    return (jnp.where(inside, segment, -1), jnp.where(inside, position, 0))


def rotary_tables(position):
    half_dim = HEAD_DIM // 2
    exponent = jnp.arange(half_dim).astype(jnp.float32) * (2.0 / HEAD_DIM)
    inverse = jnp.power(jnp.float32(THETA_BASE), -exponent)
    angle_table = position.astype(jnp.float32)[:, None] * inverse[None, :]
    copies = LANES // half_dim
    return (jnp.tile(jnp.cos(angle_table), (1, copies)), jnp.tile(jnp.sin(angle_table), (1, copies)))


def windows(rows):
    count = (rows.shape[0] - 2 * HALF) // BLOCK
    return jnp.stack([rows[n * BLOCK : n * BLOCK + BLOCK + 2 * HALF] for n in range(count)])


def allowed_pairs(segment):
    key_seg = windows(segment)
    query_seg = segment[HALF:-HALF].reshape(-1, BLOCK)
    offset = jnp.arange(BLOCK)[:, None] + HALF - jnp.arange(BLOCK + 2 * HALF)[None, :]
    return (query_seg[:, :, None] == key_seg[:, None, :]) & (jnp.abs(offset) <= HALF)[None]


def adam_update(master, gradient, moment_one, moment_two, step_rate):
    one_new = BETA_ONE * moment_one + (1.0 - BETA_ONE) * gradient
    two_new = BETA_TWO * moment_two + (1.0 - BETA_TWO) * gradient * gradient
    one_hat = one_new / (1.0 - BETA_ONE**STEP)
    two_hat = two_new / (1.0 - BETA_TWO**STEP)
    master_new = master - step_rate * (
        one_hat / (jnp.sqrt(two_hat) + ADAM_EPS) + WEIGHT_DECAY * master
    )
    return (one_new, two_new, master_new)


def line_gather(slab, place):
    size = lax.axis_size("tensor")
    from_before, from_after = [slab], [slab]
    for step in range(1, size):
        from_before.append(
            lax.ppermute(from_before[-1], "tensor", [(n, n + 1) for n in range(step - 1, size - 1)])
        )
        from_after.append(
            lax.ppermute(from_after[-1], "tensor", [(n, n - 1) for n in range(1, size - step + 1)])
        )
    return jnp.stack(
        [slab]
        + [
            jnp.where(place >= step, from_before[step], from_after[size - step])
            for step in range(1, size)
        ]
    )


def tied(values, token):
    if token is None:
        return values
    token = token if values.shape[-1] == LANES else token[0, 0]
    return jnp.where(token == 0, values, 0.0 * values)


def gather_hop(from_before, from_after, step):
    size = lax.axis_size("tensor")
    return (
        lax.ppermute(from_before, "tensor", [(n, n + 1) for n in range(step - 1, size - 1)]),
        lax.ppermute(from_after, "tensor", [(n, n - 1) for n in range(1, size - step + 1)]),
    )


def line_hop(to_after, to_before, step):
    size = lax.axis_size("tensor")
    return (
        lax.ppermute(to_after, "tensor", [(n, n + 1) for n in range(size - step)]),
        lax.ppermute(to_before, "tensor", [(n, n - 1) for n in range(step, size)]),
    )


def line_end(own, arrived):
    return sum((part.astype(jnp.float32) for part in arrived), own.astype(jnp.float32))


def gain_scatter(gains):
    steps = []
    for mask in [1, 4, 2] + far_bits()[::-1]:
        half = gains.shape[1] // 2
        steps.append(flip(gains[:, half:], mask))
        gains = gains[:, :half] + steps[-1]
    size = lax.axis_size("tensor")
    for mask in (1 << n for n in range(size.bit_length() - 1)):
        steps.append(lax.ppermute(gains, "tensor", [(n, n ^ mask) for n in range(size)]))
        gains = gains + steps[-1]
    return (gains, steps)


def flip(rows, mask):
    return lax.ppermute(rows, "dp", [(n, n ^ mask) for n in range(lax.axis_size("dp"))])


def far_bits():
    size = lax.axis_size("dp")
    return [1 << n for n in range(3, size.bit_length() - 1)]


def gather_near(slab, place):
    piece = line_gather(slab, place)
    piece = piece.reshape(-1, piece.shape[-1])
    for mask in far_bits():
        piece = jnp.concatenate([piece, flip(piece, mask)], axis=1)
    return (piece, flip(piece, 2), flip(piece, 4))


def gather_far_hop(near, token=None):
    piece, by_x, by_y = near
    half = piece.shape[0] // 2
    return (flip(tied(by_x[:half], token), 4), flip(tied(by_y[half:], token), 2))


def gather_far(near, arrived=None, token=None):
    piece, by_x, by_y = near
    if arrived is None:
        arrived = gather_far_hop(near)
    far = tied(jnp.concatenate(arrived), token)
    mine = [piece, by_x, by_y, far]
    return mine + [flip(part, 1) for part in mine]


def add_low(left, right):
    return (left.astype(jnp.float32) + right.astype(jnp.float32)).astype(left.dtype)


def far_scatter(part):
    for mask in reversed(far_bits()):
        half = part.shape[1] // 2
        part = add_low(part[:, :half], flip(part[:, half:], mask))
    return part


def gather_dp(piece):
    if lax.axis_size("dp") == PIECES:
        return lax.all_gather(piece, "dp", axis=0)
    flat = piece.reshape(-1, piece.shape[-1])
    for mask in far_bits():
        flat = jnp.concatenate([flat, flip(flat, mask)], axis=1)
    pieces = gather_far((flat, flip(flat, 2), flip(flat, 4)))
    return jnp.stack(pieces).reshape((PIECES,) + piece.shape[:-1] + (LANES,))


def scatter_dp(grads):
    if lax.axis_size("dp") == PIECES:
        return lax.psum_scatter(grads, "dp", scatter_dimension=0, tiled=False)
    flat = grads.reshape(PIECES, -1, LANES)
    own, by_x, by_y, far = add_low(flat[:4], flip(flat[4:], 1))
    by_y = add_low(by_y, flip(far, 2))
    total = add_low(add_low(own, flip(by_x, 2)), flip(by_y, 4))
    return far_scatter(total).reshape(grads.shape[1:3] + (-1,))


def to_relative(rows, back=False):
    size = lax.axis_size("dp")
    place = lax.axis_index("dp")
    bits = size.bit_length() - 1
    lead = rows.shape[:-1]
    axes = len(lead)
    chunk = rows.shape[-1] // size
    wanted = [bits - 1, bits - 3, bits - 2] + list(range(bits - 3))
    order = list(range(axes)) + [axes + n for n in wanted] + [axes + bits]
    cube = rows.reshape(lead + (2,) * bits + (chunk,))
    if back:
        cube = jnp.transpose(cube, [order.index(n) for n in range(len(order))])
    for n in range(bits):
        cube = jnp.where((place >> (bits - 1 - n)) & 1 == 1, jnp.flip(cube, axes + n), cube)
    if not back:
        cube = jnp.transpose(cube, order)
    return cube.reshape(rows.shape)


def shift(rows, step):
    size = lax.axis_size("tensor")
    pairs = [(n, n + step) for n in range(size) if 0 <= n + step < size]
    return lax.ppermute(rows, "tensor", pairs)


NN = ((1,), (0,))
NT = ((1,), (1,))
TN = ((0,), (0,))


def dot(left, right, dims):
    return lax.dot_general(left, right, (dims, ((), ())), preferred_element_type=jnp.float32)


def wide(pieces, rows, slab=0):
    return jnp.concatenate([piece[slab, rows, :] for piece in pieces], axis=1)


def relative(order, ref, rows):
    return jnp.concatenate(
        [
            ref[rows, pl.ds(pl.multiple_of(order[n] * LANES, LANES), LANES)]
            for n in range(PIECES)
        ],
        axis=1,
    )


def normed(values):
    centered = values - jnp.mean(values, axis=-1, keepdims=True)
    scale = lax.rsqrt(jnp.mean(centered * centered, axis=-1, keepdims=True) + NORM_EPS)
    return (centered * scale, scale)


def norm_pull(hat, scale, gain, grad):
    scaled = grad * gain
    return scale * (
        scaled
        - jnp.mean(scaled, axis=-1, keepdims=True)
        - hat * jnp.mean(scaled * hat, axis=-1, keepdims=True)
    )


def row_steps(count, size, body):
    def step(n, carried):
        body(pl.ds(pl.multiple_of(n * size, size), size))
        return carried

    lax.fori_loop(0, count // size, step, 0)


def whole_spec(array):
    return pl.BlockSpec(array.shape, lambda *_: (0,) * len(array.shape))


def run(kernel, name, operands, outs, scratch, flops, after=(), steps=None):
    order, operands = operands[0], operands[1:]
    specs = [spec if spec is not None else whole_spec(array) for array, spec in operands]
    out_specs = [
        spec if spec is not None else pl.BlockSpec(shape, lambda *_, n=len(shape): (0,) * n)
        for shape, dtype, spec in outs
    ]
    moved = sum(array.size * array.dtype.itemsize for array, _ in operands)
    moved += sum(math.prod(shape) * jnp.dtype(dtype).itemsize for shape, dtype, _ in outs)
    kept, made = len(operands), len(outs)

    def body(order_ref, *refs):
        refs = refs[:kept] + refs[kept + len(after) :]
        token = refs[kept + made]
        token[...] = jnp.zeros_like(token)
        kernel(order_ref, *refs[: kept + made], *refs[kept + made + 1 :])

    return pl.pallas_call(
        body,
        grid_spec=pltpu.PrefetchScalarGridSpec(
            num_scalar_prefetch=1,
            grid=(steps or lax.axis_size("tensor"),),
            in_specs=specs + [pl.BlockSpec(memory_space=pl.ANY)] * len(after),
            out_specs=out_specs + [pl.BlockSpec((1, LANES), lambda *_: (0, 0))],
            scratch_shapes=scratch,
        ),
        out_shape=[jax.ShapeDtypeStruct(shape, dtype) for shape, dtype, _ in outs]
        + [jax.ShapeDtypeStruct((1, LANES), jnp.int32)],
        compiler_params=pltpu.CompilerParams(
            dimension_semantics=("arbitrary",), vmem_limit_bytes=VMEM_BYTES
        ),
        cost_estimate=pl.CostEstimate(
            flops=int(COST_FACTOR * flops), bytes_accessed=LANES, transcendentals=0
        ),
        name=name,
    )(order, *[array for array, _ in operands], *after)


def held_back(value, after):
    def body(value_ref, *refs):
        refs[-1][...] = value_ref[...]

    return pl.pallas_call(
        body,
        in_specs=[pl.BlockSpec(memory_space=pltpu.VMEM)]
        + [pl.BlockSpec(memory_space=pl.ANY)] * len(after),
        out_specs=pl.BlockSpec(memory_space=pltpu.VMEM),
        out_shape=jax.ShapeDtypeStruct(value.shape, value.dtype),
        name="held_back",
    )(value, *after)


def blend(name, jobs, after):
    halves = 2
    operands, specs, out_specs, shapes, counts, cut = [], [], [], [], [], []
    for terms in jobs:
        rows, lanes = terms[0][0].shape[-2:]
        small = rows % (16 * halves) != 0 or rows < 512
        height = rows if small else rows // halves
        for term in terms:
            operands.append(term[0])
            if len(term) == 1:
                specs.append(pl.BlockSpec((height, lanes), lambda i, s=small: (0 if s else i, 0)))
            else:
                specs.append(
                    pl.BlockSpec(
                        (None, height, lanes),
                        lambda i, s=small, n=term[1]: (n, 0 if s else i, 0),
                    )
                )
        out_specs.append(pl.BlockSpec((height, lanes), lambda i, s=small: (0 if s else i, 0)))
        shapes.append(jax.ShapeDtypeStruct((rows, lanes), jnp.bfloat16))
        counts.append(len(terms))
        cut.append(small)

    def body(*refs):
        ins = refs[: len(operands)]
        outs = refs[len(operands) + len(after) :]
        outs[-1][...] = jnp.zeros_like(outs[-1])
        first = 0
        for n, count in enumerate(counts):
            terms = ins[first : first + count]
            first += count

            def add(out=outs[n], terms=terms):
                out[...] = sum(
                    (term[...].astype(jnp.float32) for term in terms[1:]),
                    terms[0][...].astype(jnp.float32),
                ).astype(jnp.bfloat16)

            pl.when((pl.program_id(0) == 0) | (not cut[n]))(add)

    *sums, token = pl.pallas_call(
        body,
        grid=(halves,),
        in_specs=specs + [pl.BlockSpec(memory_space=pl.ANY)] * len(after),
        out_specs=out_specs + [pl.BlockSpec((1, LANES), lambda i: (0, 0))],
        out_shape=shapes + [jax.ShapeDtypeStruct((1, LANES), jnp.int32)],
        compiler_params=pltpu.CompilerParams(
            dimension_semantics=("arbitrary",), vmem_limit_bytes=VMEM_BYTES
        ),
        name=name,
    )(*operands, *after)
    return (sums, token)


ALL, ODD, EVEN = (0, 1), (1, 2), (0, 2)


def slabs(piece, rows, part=ALL, first=0, count=1):
    return (
        piece,
        pl.BlockSpec((count, rows, LANES), lambda n, *_: (part[0] + part[1] * n, first, 0)),
    )


def gathered(array, rows, part=ALL, count=1):
    return [
        (
            array,
            pl.BlockSpec(
                (None, count, rows, LANES),
                lambda n, order, p=p: (order[p], part[0] + part[1] * n, 0, 0),
            ),
        )
        for p in range(PIECES)
    ]


def gathered_out(parts, rows):
    return (
        (PIECES, parts, rows, LANES),
        jnp.bfloat16,
        pl.BlockSpec((PIECES, 1, rows, LANES), lambda n, order: (0, order[PIECES + n], 0, 0)),
    )


def store_gathered(order, ref, rows, values):
    values = values.astype(jnp.bfloat16)
    for n in range(PIECES):
        ref[order[n], 0, rows, :] = values[:, n * LANES : (n + 1) * LANES]


def lead(array, part=ALL, count=1):
    shape = (count,) + array.shape[1:]
    return (
        array,
        pl.BlockSpec(shape, lambda n, *_: (part[0] + part[1] * n,) + (0,) * (len(shape) - 1)),
    )


def turned_block(array, rows, part=ALL):
    return (array, pl.BlockSpec((rows, array.shape[1]), lambda n, *_: (part[0] + part[1] * n, 0)))


def lead_out(shape, dtype):
    return (shape, dtype, pl.BlockSpec((1,) + shape[1:], lambda n, *_: (n,) + (0,) * (len(shape) - 1)))


def piece_outs(parts, rows):
    low = jnp.bfloat16
    own = pl.BlockSpec((1, rows, LANES), lambda n, *_: (n, 0, 0))
    other = pl.BlockSpec((4, 1, rows, LANES), lambda n, *_: (0, n, 0, 0))
    return [((parts, rows, LANES), low, own)] * 4 + [((4, parts, rows, LANES), low, other)]


def store_pieces(refs, rows, values):
    values = values.astype(jnp.bfloat16)
    for n in range(4):
        refs[n][0, rows, :] = values[:, n * LANES : (n + 1) * LANES]
        refs[4][n, 0, rows, :] = values[:, (n + 4) * LANES : (n + 5) * LANES]


def heads_kernel(order, hidden, before, after, gains, cosine, sine, *refs):
    pieces, (q_out, k_out, v_out, rows_wide) = refs[:PIECES], refs[PIECES:]
    row_count = hidden.shape[0]
    gain = gains[0:1, :]

    def norm_rows(source, rows, first):
        values = relative(order, source, rows).astype(jnp.float32)
        return (normed(values)[0] * gain).astype(jnp.bfloat16)

    @pl.when(pl.program_id(0) == 0)
    def _():
        rows_wide[0:HALF, :] = norm_rows(before, slice(0, HALF), 0)
        rows_wide[HALF + row_count :, :] = norm_rows(after, slice(0, HALF), 0)

        def one(rows):
            values = norm_rows(hidden, rows, 0)
            rows_wide[pl.ds(pl.multiple_of(rows.start + HALF, HALF), HALF), :] = values

        row_steps(row_count, HALF, one)

    width = 2 * LANES

    def turned(mixed, rows):
        front, back = mixed[:, :LANES], mixed[:, LANES:]
        cos, sin = cosine[rows, :], sine[rows, :]
        return (front * cos - back * sin, back * cos + front * sin)

    inner = slice(HALF, HALF + row_count)
    scale = HEAD_DIM ** (-0.5)
    front, back = turned(dot(rows_wide[inner, :], wide(pieces, slice(0, width)), NT), inner)
    q_out[0, :, :LANES] = (front.astype(jnp.bfloat16) * scale).astype(jnp.bfloat16)
    q_out[0, :, LANES:] = (back.astype(jnp.bfloat16) * scale).astype(jnp.bfloat16)
    front, back = turned(
        dot(rows_wide[...], wide(pieces, slice(width, 2 * width)), NT), slice(None)
    )
    k_out[0, :, :LANES] = front.astype(jnp.bfloat16)
    k_out[0, :, LANES:] = back.astype(jnp.bfloat16)
    v_out[0] = dot(rows_wide[...], wide(pieces, slice(2 * width, 3 * width)), NT).astype(
        jnp.bfloat16
    )


def head_masks():
    lane = lax.broadcasted_iota(jnp.int32, (1, 2 * LANES), 1)
    turned = [((lane % LANES) // 32 == n).astype(jnp.float32).astype(jnp.bfloat16) for n in range(4)]
    plain = [(lane // HEAD_DIM == n).astype(jnp.float32).astype(jnp.bfloat16) for n in range(4)]
    return (turned, plain)


def attend_kernel(order, bias, q_in, k_in, v_in, out, log_out):
    turned, plain = head_masks()
    lane = lax.broadcasted_iota(jnp.int32, (BLOCK, LANES), 1)

    def block(n, carried):
        rows = pl.ds(pl.multiple_of(n * BLOCK, BLOCK), BLOCK)
        span = pl.ds(pl.multiple_of(n * BLOCK, BLOCK), BLOCK + 2 * HALF)
        queries, keys, values = q_in[0, rows, :], k_in[0, span, :], v_in[0, span, :]
        masked = bias[n]
        total = jnp.zeros((BLOCK, 2 * LANES), jnp.float32)
        logs = jnp.zeros((BLOCK, LANES), jnp.float32)
        for h in range(4):
            scores = dot(queries * turned[h], keys, NT) + masked
            row_top = jnp.max(scores, axis=-1, keepdims=True)
            lifted = jnp.exp(scores - row_top)
            row_total = jnp.sum(lifted, axis=-1, keepdims=True)
            probs_low = (lifted * (1.0 / row_total)).astype(jnp.bfloat16)
            total = total + dot(probs_low, values * plain[h], NN)
            logs = jnp.where(lane == h, row_top + jnp.log(row_total), logs)
        out[0, rows, :] = total.astype(jnp.bfloat16)
        log_out[0, rows, :] = logs
        return carried

    lax.fori_loop(0, bias.shape[0], block, 0)


def proj_kernel(order, hidden, gains, attended, *refs):
    pieces, (middle, rows_two) = refs[:PIECES], refs[PIECES:]
    step = pl.program_id(0)

    @pl.when(step == 0)
    def _():
        def one(rows):
            middle[rows, :] = relative(order, hidden, rows).astype(jnp.float32)

        row_steps(hidden.shape[0], HALF, one)

    middle[...] += dot(attended[0], wide(pieces, slice(None)), NN)

    @pl.when(step == pl.num_programs(0) - 1)
    def _():
        def one(rows):
            rows_two[rows, :] = (normed(middle[rows, :])[0] * gains[1:2, :]).astype(jnp.bfloat16)

        row_steps(hidden.shape[0], HALF, one)


def gate_kernel(order, rows_two, *refs):
    pieces, (active, gate_side, up_side, rows_turned, gate, up) = refs[:PIECES], refs[PIECES:]

    @pl.when(pl.program_id(0) == 0)
    def _():
        rows_turned[...] = rows_two[...].T

    count = gate.shape[0]
    gate[...] = dot(wide(pieces, slice(0, count)), rows_turned[...], NN)
    up[...] = dot(wide(pieces, slice(count, 2 * count)), rows_turned[...], NN)

    def one(rows):
        x, u = gate[rows, :], up[rows, :]
        below = 0.5 * (1.0 + lax.erf(x * (0.5**0.5)))
        density = jnp.exp(-0.5 * x * x) * ((2.0 * math.pi) ** -0.5)
        lifted = x * below
        active[rows, :] = (lifted * u).astype(jnp.bfloat16)
        gate_side[rows, :] = (u * (below + x * density)).astype(jnp.bfloat16)
        up_side[rows, :] = lifted.astype(jnp.bfloat16)

    row_steps(count, 16, one)


def down_kernel(order, middle, active, *refs):
    pieces, (out, total) = refs[:PIECES], refs[PIECES:]
    step = pl.program_id(0)

    @pl.when(step == 0)
    def _():
        total[...] = middle[...]

    total[...] += dot(active[...], wide(pieces, slice(None)), TN)

    @pl.when(step == pl.num_programs(0) - 1)
    def _():
        for n in range(PIECES):
            lanes = pl.ds(pl.multiple_of(order[n] * LANES, LANES), LANES)
            out[:, lanes] = total[:, n * LANES : (n + 1) * LANES].astype(jnp.bfloat16)


def down_grad_kernel(order, cotangent, active, *refs):
    grads, cot_out = refs

    @pl.when(pl.program_id(0) == 0)
    def _():
        def one(rows):
            cot_out[rows, :] = relative(order, cotangent, rows)

        row_steps(cotangent.shape[0], HALF, one)

    store_gathered(order, grads, slice(None), dot(active[...], cot_out[...], NN))


def in_grad_kernel(order, cot, rows_two, gate_side, up_side, *refs):
    pieces, (grads, gate_out, up_out, cot_turned, grad_active) = refs[:PIECES], refs[PIECES:]

    @pl.when(pl.program_id(0) == 0)
    def _():
        cot_turned[...] = cot[...].T

    count = grad_active.shape[0]
    grad_active[...] = dot(wide(pieces, slice(None)), cot_turned[...], NN)

    def one(rows):
        grad = grad_active[rows, :]
        gate_out[rows, :] = (grad * gate_side[rows, :].astype(jnp.float32)).astype(jnp.bfloat16)
        up_out[rows, :] = (grad * up_side[rows, :].astype(jnp.float32)).astype(jnp.bfloat16)

    row_steps(count, 16, one)
    store_gathered(order, grads, slice(0, count), dot(gate_out[...], rows_two[...], NN))
    store_gathered(order, grads, slice(count, 2 * count), dot(up_out[...], rows_two[...], NN))


def middle_grad_kernel(order, middle, cot, gains, *refs):
    sides, pieces, refs = refs[:2], refs[2 : 2 + PIECES], refs[2 + PIECES :]
    grad_middle, grad_low, gain_out, total = refs
    step = pl.program_id(0)
    count = sides[0].shape[0]

    @pl.when(step == 0)
    def _():
        total[...] = jnp.zeros_like(total)
        gain_out[...] = jnp.zeros_like(gain_out)

    for n, side in enumerate(sides):
        total[...] += dot(side[...], wide(pieces, slice(n * count, (n + 1) * count)), TN)

    @pl.when(step == pl.num_programs(0) - 1)
    def _():
        def one(rows):
            grad = total[rows, :]
            hat, scale = normed(middle[rows, :])
            result = cot[rows, :].astype(jnp.float32) + norm_pull(hat, scale, gains[1:2, :], grad)
            grad_middle[rows, :] = result
            grad_low[rows, :] = result.astype(jnp.bfloat16)
            gain_out[0:1, :] += jnp.sum(grad * hat, axis=0, keepdims=True)

        row_steps(middle.shape[0], HALF, one)


def attend_grad_kernel(
    order, bias, cosine, sine, grad_low, rows_wide, q_in, k_in, v_in, attended, logs, *refs
):
    pieces, refs = refs[:PIECES], refs[PIECES:]
    weight_grads, (query_out, pair_out, grad_keys, grad_values, grad_out) = refs[:5], refs[5:]
    turned, plain = head_masks()
    row_count = grad_low.shape[0]
    low = jnp.bfloat16
    width = 2 * LANES
    grad_out[...] = dot(grad_low[...], wide(pieces, slice(None)), NT).astype(low)
    grad_keys[...] = jnp.zeros_like(grad_keys)
    grad_values[...] = jnp.zeros_like(grad_values)

    def back(values, rows):
        front, rear = values[:, :LANES], values[:, LANES:]
        cos, sin = cosine[rows, :], sine[rows, :]
        return (front * cos + rear * sin, rear * cos - front * sin)

    def block(n, carried):
        rows = pl.ds(pl.multiple_of(n * BLOCK, BLOCK), BLOCK)
        span = pl.ds(pl.multiple_of(n * BLOCK, BLOCK), BLOCK + 2 * HALF)
        queries, keys, values = q_in[0, rows, :], k_in[0, span, :], v_in[0, span, :]
        grad_rows = grad_out[rows, :]
        masked = bias[n]
        log_rows = logs[0, rows, :]
        grad_query = jnp.zeros((BLOCK, width), jnp.float32)
        grad_key = jnp.zeros((BLOCK + 2 * HALF, width), jnp.float32)
        grad_value = jnp.zeros((BLOCK + 2 * HALF, width), jnp.float32)
        for h in range(4):
            query_head, grad_head = queries * turned[h], grad_rows * plain[h]
            scores = dot(query_head, keys, NT) + masked
            probs = jnp.exp(scores - log_rows[:, h : h + 1])
            grad_probs = dot(grad_head, values, NT)
            row_delta = jnp.sum(probs * grad_probs, axis=-1, keepdims=True)
            grad_scores = (probs * (grad_probs - row_delta)).astype(low)
            grad_query = grad_query + dot(grad_scores, keys * turned[h], NN)
            grad_key = grad_key + dot(grad_scores, query_head, TN)
            grad_value = grad_value + dot(probs.astype(low), grad_head, TN)
        place = pl.ds(pl.multiple_of(n * BLOCK + HALF, HALF), BLOCK)
        front, rear = back(grad_query * HEAD_DIM ** (-0.5), place)
        query_out[0, rows, :LANES] = front.astype(low)
        query_out[0, rows, LANES:] = rear.astype(low)
        grad_keys[span, :] += grad_key
        grad_values[span, :] += grad_value
        return carried

    lax.fori_loop(0, bias.shape[0], block, 0)
    front, rear = back(grad_keys[...], slice(None))
    pair_out[0, 0, :, :LANES] = front.astype(low)
    pair_out[0, 0, :, LANES:] = rear.astype(low)
    pair_out[0, 1] = grad_values[...].astype(low)
    inner = slice(HALF, HALF + row_count)
    store_pieces(weight_grads, slice(0, width), dot(query_out[0], rows_wide[inner, :], TN))
    for c in range(2):
        rows = slice((1 + c) * width, (2 + c) * width)
        store_pieces(weight_grads, rows, dot(pair_out[0, c], rows_wide[...], TN))
    store_pieces(weight_grads, slice(3 * width, 4 * width), dot(attended[0], grad_low[...], TN))


def input_grad_kernel(order, hidden, gains, grad_middle, *refs):
    even, odd, (before, after), refs = refs[:2], refs[2:4], refs[4:6], refs[6:]
    pieces, (grad_input, gain_out, mixed, total) = refs[:PIECES], refs[PIECES:]
    step = pl.program_id(0)
    row_count = hidden.shape[0]
    width = 2 * LANES
    last = row_count - HALF

    @pl.when(step == 0)
    def _():
        total[...] = jnp.zeros_like(total)
        gain_out[...] = jnp.zeros_like(gain_out)

    def sum_low(left, right):
        return (left.astype(jnp.float32) + right.astype(jnp.float32)).astype(jnp.bfloat16)

    def add(slab, queries, pairs):
        total[...] += dot(queries[0], wide(pieces, slice(0, width), slab), NN)
        for c in range(2):
            mixed[...] = pairs[0, c, HALF : HALF + row_count, :]
            mixed[0:HALF, :] = sum_low(mixed[0:HALF, :], before[slab, c])
            mixed[last:, :] = sum_low(mixed[last:, :], after[slab, c])
            rows = slice((1 + c) * width, (2 + c) * width)
            total[...] += dot(mixed[...], wide(pieces, rows, slab), NN)

    add(0, *even)
    add(1, *odd)

    @pl.when(step == pl.num_programs(0) - 1)
    def _():
        def one(rows):
            grad = total[rows, :]
            hat, scale = normed(relative(order, hidden, rows).astype(jnp.float32))
            result = grad_middle[rows, :] + norm_pull(hat, scale, gains[0:1, :], grad)
            for n in range(PIECES):
                lanes = pl.ds(pl.multiple_of(order[n] * LANES, LANES), LANES)
                grad_input[rows, lanes] = result[:, n * LANES : (n + 1) * LANES]
            gain_out[0:1, :] += jnp.sum(grad * hat, axis=0, keepdims=True)

        row_steps(row_count, HALF, one)


def local(
    hidden_in,
    seq_lengths,
    cotangent,
    w_qkv,
    w_proj,
    w_in,
    w_down,
    norm_gains,
    qkv_first,
    qkv_second,
    proj_first,
    proj_second,
    in_first,
    in_second,
    down_first,
    down_second,
    gain_first,
    gain_second,
):
    row_count = hidden_in.shape[0]
    wide_count = row_count + 2 * HALF
    size = lax.axis_size("tensor")
    dp_size = lax.axis_size("dp")
    group_rows = row_count * size
    low, full = jnp.bfloat16, jnp.float32
    chunk = norm_gains.shape[1]
    head_wide = w_proj.shape[1]
    head_rows = 4 * head_wide
    slab_rows = head_rows + SLAB_PAD
    hidden_wide = w_down.shape[1]
    head_count, half_dim = head_wide // HEAD_DIM, HEAD_DIM // 2

    def halves_first(weight):
        split = weight.reshape(chunk, 2, head_count, 2, half_dim)
        return jnp.transpose(split, (0, 1, 3, 2, 4)).reshape(chunk, 2 * head_wide)

    def heads_first(weight):
        split = weight.reshape(chunk, 2, 2, head_count, half_dim)
        return jnp.transpose(split, (0, 1, 3, 2, 4)).reshape(chunk, 2, head_wide)

    heads_slab = jnp.concatenate(
        [
            jnp.concatenate(
                [halves_first(w_qkv[:, :2].astype(low)), w_qkv[:, 2].astype(low), w_proj.astype(low)],
                axis=1,
            ).T,
            jnp.pad(norm_gains.astype(low), ((0, SLAB_PAD - 2), (0, 0))),
        ]
    )
    ffn_slab = jnp.concatenate(
        [w_in.astype(low).reshape(chunk, 2 * hidden_wide), w_down.astype(low)], axis=1
    ).T
    if dp_size == PIECES:
        apart = jnp.array([0, 2, 4, 6, 1, 3, 5, 7], jnp.int32)
        order = lax.axis_index("dp").astype(jnp.int32) ^ apart
        hidden, cot_in = hidden_in, cotangent
    else:
        order = jnp.arange(PIECES, dtype=jnp.int32)
        hidden, cot_in = to_relative(hidden_in), to_relative(cotangent)

    place = lax.axis_index("tensor").astype(jnp.int32)
    owners = (place + size - jnp.arange(size, dtype=jnp.int32)) % size
    order = jnp.concatenate([order, owners])
    edges = (shift(hidden[-HALF:], 1), shift(hidden[:HALF], -1))
    zeros = jnp.zeros((1, LANES), jnp.int32)
    heads_near = gather_near(heads_slab, place)
    ffn_slab = tied(ffn_slab, held_back(zeros, heads_near[:1]))
    first = gather_hop(ffn_slab, ffn_slab, 1)
    second = gather_hop(*first, 2)
    token = held_back(zeros, (*heads_near[1:], *second, *edges))
    heads_far = gather_far_hop(heads_near, token)
    third = gather_hop(tied(second[0], token), tied(second[1], token), 3)
    start = place + held_back(zeros, (*heads_far, *third))
    start = start if chunk == LANES else start[0, 0]
    ffn_line = jnp.stack(
        [
            ffn_slab,
            jnp.where(start >= 1, first[0], third[1]),
            jnp.where(start >= 2, second[0], second[1]),
            jnp.where(start >= 3, third[0], first[1]),
        ]
    )
    in_all = gather_dp(ffn_line[:, : 2 * hidden_wide])
    heads_pieces = [
        piece.reshape(size, -1, LANES) for piece in gather_far(heads_near, heads_far)
    ]
    gains = jnp.concatenate(
        [piece[0, head_rows : head_rows + 8] for piece in heads_pieces], axis=1
    ).astype(full)

    first_row = lax.axis_index("tensor") * row_count
    segment, position = layout(
        seq_lengths[0], first_row - HALF + jnp.arange(wide_count), group_rows
    )
    cosine, sine = rotary_tables(position)
    bias = jnp.where(allowed_pairs(segment), 0.0, MASKED).astype(full)

    head_block = (size, row_count, head_wide)
    wide_block = (size, wide_count, head_wide)
    tokens = (row_count, D)
    turned = (size * hidden_wide, row_count)
    turned_spec = pl.BlockSpec((hidden_wide, row_count), lambda n, *_: (n, 0))
    matmul = 2 * row_count * D

    queries, keys, values, rows_wide, token = run(
        heads_kernel,
        "heads",
        [order, (hidden, None), (edges[0], None), (edges[1], None), (gains, None)]
        + [(cosine, None), (sine, None)]
        + [slabs(piece, 3 * head_wide) for piece in heads_pieces],
        [lead_out(head_block, low), lead_out(wide_block, low), lead_out(wide_block, low)]
        + [((wide_count, D), low, None)],
        [],
        3 * matmul * D,
    )
    down_all = gather_dp(tied(ffn_line[:, 2 * hidden_wide :], token))
    attended, logs, token = run(
        attend_kernel,
        "attend",
        [order, (bias, None), lead(queries), lead(keys), lead(values)],
        [lead_out(head_block, low), lead_out((size, row_count, LANES), full)],
        [],
        2 * matmul * D,
    )
    middle, rows_two, token = run(
        proj_kernel,
        "proj",
        [order, (hidden, None), (gains, None), lead(attended)]
        + [slabs(piece, head_wide, first=3) for piece in heads_pieces],
        [(tokens, full, None), (tokens, low, None)],
        [],
        matmul * D,
    )
    active, gate_side, up_side, token = run(
        gate_kernel,
        "gate",
        [order, (rows_two, None)] + gathered(in_all, 2 * hidden_wide),
        [(turned, low, turned_spec)] * 3,
        [
            pltpu.VMEM((D, row_count), low),
            pltpu.VMEM((hidden_wide, row_count), full),
            pltpu.VMEM((hidden_wide, row_count), full),
        ],
        2 * matmul * FF,
    )

    down_grads, cot, token = run(
        down_grad_kernel,
        "down_grad",
        [order, (cot_in, None), turned_block(active, hidden_wide)],
        [gathered_out(size, hidden_wide), (tokens, low, None)],
        [],
        matmul * FF,
    )
    down_line = scatter_dp(down_grads)
    half = size // 2
    in_grads, gate_grad, up_grad, token = run(
        in_grad_kernel,
        "in_grad",
        [order, (cot, None), (rows_two, None)]
        + [turned_block(gate_side, hidden_wide), turned_block(up_side, hidden_wide)]
        + gathered(down_all, hidden_wide),
        [gathered_out(size, 2 * hidden_wide)] + [(turned, low, turned_spec)] * 2,
        [pltpu.VMEM((D, row_count), low), pltpu.VMEM((hidden_wide, row_count), full)],
        3 * matmul * FF,
    )
    in_line = scatter_dp(in_grads)
    grad_middle, grad_low, gain_two, token = run(
        middle_grad_kernel,
        "middle_grad",
        [order, (middle, None), (cot, None), (gains, None)]
        + [turned_block(side, hidden_wide) for side in (gate_grad, up_grad)]
        + gathered(in_all, 2 * hidden_wide),
        [(tokens, full, None), (tokens, low, None), ((8, D), full, None)],
        [pltpu.VMEM(tokens, full)],
        2 * matmul * FF,
    )

    def core_hop(outs):
        return (outs[:4], flip(outs[4], 1))

    def core_sums(own, received):
        entries = own[0].shape[0]
        received = received.reshape((-1,) + received.shape[2:])
        return [
            [(part, e), (received, n * entries + e)]
            for n, part in enumerate(own)
            for e in range(entries)
        ]

    def far_hop(sums):
        return (flip(sums[6], 2), flip(sums[7], 4))

    def far_sums(sums, arrived):
        return [[(sums[4],), (arrived[0],)], [(sums[3],), (arrived[1],)]]

    def near_hop(sums, added):
        return (flip(sums[2], 2), flip(added[0], 4), flip(added[1], 2), flip(sums[5], 4))

    def near_sums(sums, arrived):
        return [
            [(sums[0],), (arrived[0],), (arrived[1],)],
            [(sums[1],), (arrived[2],), (arrived[3],)],
        ]

    def attend_grad(part, count, name, after):
        return run(
            attend_grad_kernel,
            name,
            [order, (bias, None), (cosine, None), (sine, None), (grad_low, None), (rows_wide, None)]
            + [lead(array, part) for array in (queries, keys, values, attended, logs)]
            + [slabs(piece, head_wide, part, first=3) for piece in heads_pieces],
            piece_outs(count, head_rows)
            + [
                lead_out((count, row_count, head_wide), low),
                lead_out((count, 2, wide_count, head_wide), low),
            ],
            [
                pltpu.VMEM((wide_count, head_wide), full),
                pltpu.VMEM((wide_count, head_wide), full),
                pltpu.VMEM((row_count, head_wide), low),
            ],
            3 * count * matmul * D,
            after=after,
            steps=count,
        )

    *odd_outs, odd_queries, odd_pairs, token = attend_grad(ODD, half, "attend_grad_odd", ())
    odd_core = core_hop(odd_outs)
    *even_outs, even_queries, even_pairs, token = attend_grad(
        EVEN, half, "attend_grad_even", (token,)
    )
    even_core = core_hop(even_outs)
    odd, token = blend("sums_one", core_sums(*odd_core), (token,))
    odd_far = far_hop(odd)
    pairs = [even_pairs[0], odd_pairs[0], even_pairs[1], odd_pairs[1]]
    edge_after = jnp.stack([pair[:, -HALF:] for pair in pairs[-1:] + pairs[:-1]])
    edge_before = jnp.stack([pair[:, :HALF] for pair in pairs[1:] + pairs[:1]])
    edges = (shift(edge_after, 1), shift(edge_before, -1))
    hidden_out, token = run(
        down_kernel,
        "down",
        [order, (middle, None), turned_block(active, hidden_wide)]
        + gathered(down_all, hidden_wide),
        [(tokens, low, None)],
        [pltpu.VMEM(tokens, full)],
        matmul * FF,
        after=(token,),
    )
    (*even, odd_y, odd_x), token = blend(
        "sums_two", core_sums(*even_core) + far_sums(odd, odd_far), (token,)
    )
    even_far = far_hop(even)
    odd_near = near_hop(odd, (odd_y, odd_x))
    ffn_sum = lax.psum_scatter(
        tied(jnp.concatenate([in_line, down_line], axis=1), token),
        "tensor",
        scatter_dimension=0,
        tiled=False,
    )
    grad_input, gain_one, token = run(
        input_grad_kernel,
        "input_grad",
        [order, (hidden, None), (gains, None), (grad_middle, None)]
        + [lead(array) for array in (even_queries, even_pairs, odd_queries, odd_pairs)]
        + [lead(array, count=2) for array in edges]
        + [slabs(piece, 3 * head_wide, count=2) for piece in heads_pieces],
        [(tokens, full, None), ((8, D), full, None)],
        [pltpu.VMEM((row_count, head_wide), low), pltpu.VMEM(tokens, full)],
        3 * matmul * D,
        after=(token,),
        steps=half,
    )
    (*odd_parts, even_y, even_x), token = blend(
        "sums_three",
        near_sums(odd, odd_near) + far_sums(even, even_far),
        (token,),
    )
    even_near = near_hop(even, (even_y, even_x))
    odd_parts = [far_scatter(part) for part in odd_parts]

    def line_round(parts, step, arrived=None):
        to_after, to_before = parts[size - step], parts[step]
        if arrived is not None:
            to_after, to_before = add_low(to_after, arrived[0]), add_low(to_before, arrived[1])
        return line_hop(to_after, to_before, step)

    even_parts, token = blend("sums_four", near_sums(even, even_near), (token))
    gain_sum, _ = gain_scatter(tied(jnp.concatenate([gain_one[:1], gain_two[:1]]), token))
    even_parts = [far_scatter(part) for part in even_parts]
    heads_parts = [even_parts[0], odd_parts[0], even_parts[1], odd_parts[1]]
    heads_arrived = line_round(heads_parts, 3)
    heads_arrived = line_round(heads_parts, 2, heads_arrived)
    last_token = held_back(zeros, (ffn_sum, *heads_arrived))
    heads_parts[1:] = [tied(part, last_token) for part in heads_parts[1:]]
    heads_arrived = line_round(heads_parts, 1, heads_arrived)
    heads_total = line_end(heads_parts[0], heads_arrived)
    if dp_size != PIECES:
        hidden_out, grad_input = to_relative(hidden_out, True), to_relative(grad_input, True)

    ffn_sum = ffn_sum.astype(full).T
    in_sum = ffn_sum[:, : 2 * hidden_wide].reshape(w_in.shape)
    down_sum = ffn_sum[:, 2 * hidden_wide :]
    heads_sum = heads_total.T
    qkv_sum = jnp.concatenate(
        [
            heads_first(heads_sum[:, : 2 * head_wide]),
            heads_sum[:, None, 2 * head_wide : 3 * head_wide],
        ],
        axis=1,
    )
    proj_sum = heads_sum[:, 3 * head_wide :]
    qkv_one, qkv_two, qkv_new = adam_update(w_qkv, qkv_sum, qkv_first, qkv_second, D ** (-0.5))
    proj_one, proj_two, proj_new = adam_update(
        w_proj, proj_sum, proj_first, proj_second, (D // HALF) ** (-0.5)
    )
    in_one, in_two, in_new = adam_update(w_in, in_sum, in_first, in_second, D ** (-0.5))
    down_one, down_two, down_new = adam_update(
        w_down, down_sum, down_first, down_second, (FF // 2) ** (-0.5)
    )
    gain_one, gain_two, gains_new = adam_update(
        norm_gains, gain_sum, gain_first, gain_second, GAIN_RATE
    )
    return (
        hidden_out,
        grad_input,
        qkv_one,
        qkv_two,
        qkv_new,
        proj_one,
        proj_two,
        proj_new,
        in_one,
        in_two,
        in_new,
        down_one,
        down_two,
        down_new,
        gain_one,
        gain_two,
        gains_new,
    )


def solution(mesh):
    placed = (
        P(("dp", "tensor"), None),
        P("dp", None),
        P(("dp", "tensor"), None),
        P("dp", None, "tensor"),
        P("dp", "tensor"),
        P("dp", None, "tensor"),
        P("dp", "tensor"),
        P(None, "dp"),
        P("dp", None, "tensor"),
        P("dp", None, "tensor"),
        P("dp", "tensor"),
        P("dp", "tensor"),
        P("dp", None, "tensor"),
        P("dp", None, "tensor"),
        P("dp", "tensor"),
        P("dp", "tensor"),
        P(None, "dp"),
        P(None, "dp"),
    )
    return jax.shard_map(
        local,
        mesh=mesh,
        in_specs=placed,
        out_specs=(
            P(("dp", "tensor"), None),
            P(("dp", "tensor"), None),
            P("dp", None, "tensor"),
            P("dp", None, "tensor"),
            P("dp", None, "tensor"),
            P("dp", "tensor"),
            P("dp", "tensor"),
            P("dp", "tensor"),
            P("dp", None, "tensor"),
            P("dp", None, "tensor"),
            P("dp", None, "tensor"),
            P("dp", "tensor"),
            P("dp", "tensor"),
            P("dp", "tensor"),
            P(None, "dp"),
            P(None, "dp"),
            P(None, "dp"),
        ),
        check_vma=False,
    )
```

```python
import functools
import math

import jax
import jax.numpy as jnp
from jax import lax
from jax.experimental import pallas as pl
from jax.experimental.pallas import tpu as pltpu
from jax.sharding import PartitionSpec as P

D = 1024
HEADS = 16
HEAD_DIM = 64
FF = 2624
HALF = 64
BLOCK = 128
STEP = 10

NORM_EPS = 1e-05
THETA_BASE = 10000.0
BETA_ONE = 0.9
BETA_TWO = 0.98
ADAM_EPS = 1e-06
WEIGHT_DECAY = 0.01
GAIN_RATE = 0.5
MASKED = -1e30


LANES = 128
PIECES = 8
SLAB_PAD = 16
VMEM_BYTES = 52 * 1024 * 1024
COST_FACTOR = 1e-3


def layout(lengths, token_index, group_rows):
    seq_ends = jnp.cumsum(lengths)
    seq_starts = seq_ends - lengths
    segment = jnp.sum((token_index[:, None] >= seq_ends[None, :]).astype(jnp.int32), axis=1)
    member = segment[:, None] == jnp.arange(lengths.shape[0])[None, :]
    position = token_index - jnp.sum(jnp.where(member, seq_starts[None, :], 0), axis=1)
    inside = (token_index >= 0) & (token_index < group_rows)
    return (jnp.where(inside, segment, -1), jnp.where(inside, position, 0))


def rotary_tables(position):
    half_dim = HEAD_DIM // 2
    exponent = jnp.arange(half_dim).astype(jnp.float32) * (2.0 / HEAD_DIM)
    inverse = jnp.power(jnp.float32(THETA_BASE), -exponent)
    angle_table = position.astype(jnp.float32)[:, None] * inverse[None, :]
    copies = LANES // half_dim
    return (jnp.tile(jnp.cos(angle_table), (1, copies)), jnp.tile(jnp.sin(angle_table), (1, copies)))


def windows(rows):
    count = (rows.shape[0] - 2 * HALF) // BLOCK
    return jnp.stack([rows[n * BLOCK : n * BLOCK + BLOCK + 2 * HALF] for n in range(count)])


def allowed_pairs(segment):
    key_seg = windows(segment)
    query_seg = segment[HALF:-HALF].reshape(-1, BLOCK)
    offset = jnp.arange(BLOCK)[:, None] + HALF - jnp.arange(BLOCK + 2 * HALF)[None, :]
    return (query_seg[:, :, None] == key_seg[:, None, :]) & (jnp.abs(offset) <= HALF)[None]


def adam_update(master, gradient, moment_one, moment_two, step_rate):
    one_new = BETA_ONE * moment_one + (1.0 - BETA_ONE) * gradient
    two_new = BETA_TWO * moment_two + (1.0 - BETA_TWO) * gradient * gradient
    one_hat = one_new / (1.0 - BETA_ONE**STEP)
    two_hat = two_new / (1.0 - BETA_TWO**STEP)
    master_new = master - step_rate * (
        one_hat / (jnp.sqrt(two_hat) + ADAM_EPS) + WEIGHT_DECAY * master
    )
    return (one_new, two_new, master_new)


def line_gather(slab, place):
    size = lax.axis_size("tensor")
    from_before, from_after = [slab], [slab]
    for step in range(1, size):
        from_before.append(
            lax.ppermute(from_before[-1], "tensor", [(n, n + 1) for n in range(step - 1, size - 1)])
        )
        from_after.append(
            lax.ppermute(from_after[-1], "tensor", [(n, n - 1) for n in range(1, size - step + 1)])
        )
    return jnp.stack(
        [slab]
        + [
            jnp.where(place >= step, from_before[step], from_after[size - step])
            for step in range(1, size)
        ]
    )


def tied(values, token):
    if token is None:
        return values
    token = token if values.shape[-1] == LANES else token[0, 0]
    return jnp.where(token == 0, values, 0.0 * values)


def gather_hop(from_before, from_after, step):
    size = lax.axis_size("tensor")
    return (
        lax.ppermute(from_before, "tensor", [(n, n + 1) for n in range(step - 1, size - 1)]),
        lax.ppermute(from_after, "tensor", [(n, n - 1) for n in range(1, size - step + 1)]),
    )


def line_hop(to_after, to_before, step):
    size = lax.axis_size("tensor")
    return (
        lax.ppermute(to_after, "tensor", [(n, n + 1) for n in range(size - step)]),
        lax.ppermute(to_before, "tensor", [(n, n - 1) for n in range(step, size)]),
    )


def line_end(own, arrived):
    return sum((part.astype(jnp.float32) for part in arrived), own.astype(jnp.float32))


def gain_scatter(gains):
    steps = []
    for mask in [1, 4, 2] + far_bits()[::-1]:
        half = gains.shape[1] // 2
        steps.append(flip(gains[:, half:], mask))
        gains = gains[:, :half] + steps[-1]
    size = lax.axis_size("tensor")
    for mask in (1 << n for n in range(size.bit_length() - 1)):
        steps.append(lax.ppermute(gains, "tensor", [(n, n ^ mask) for n in range(size)]))
        gains = gains + steps[-1]
    return (gains, steps)


def flip(rows, mask):
    return lax.ppermute(rows, "dp", [(n, n ^ mask) for n in range(lax.axis_size("dp"))])


def far_bits():
    size = lax.axis_size("dp")
    return [1 << n for n in range(3, size.bit_length() - 1)]


def gather_near(slab, place):
    piece = line_gather(slab, place)
    piece = piece.reshape(-1, piece.shape[-1])
    for mask in far_bits():
        piece = jnp.concatenate([piece, flip(piece, mask)], axis=1)
    return (piece, flip(piece, 2), flip(piece, 4))


def gather_far_hop(near, token=None):
    piece, by_x, by_y = near
    half = piece.shape[0] // 2
    return (flip(tied(by_x[:half], token), 4), flip(tied(by_y[half:], token), 2))


def gather_far(near, arrived=None, token=None):
    piece, by_x, by_y = near
    if arrived is None:
        arrived = gather_far_hop(near)
    far = tied(jnp.concatenate(arrived), token)
    mine = [piece, by_x, by_y, far]
    return mine + [flip(part, 1) for part in mine]


def add_low(left, right):
    return (left.astype(jnp.float32) + right.astype(jnp.float32)).astype(left.dtype)


def far_scatter(part):
    for mask in reversed(far_bits()):
        half = part.shape[1] // 2
        part = add_low(part[:, :half], flip(part[:, half:], mask))
    return part


def gather_dp(piece):
    if lax.axis_size("dp") == PIECES:
        return lax.all_gather(piece, "dp", axis=0)
    flat = piece.reshape(-1, piece.shape[-1])
    for mask in far_bits():
        flat = jnp.concatenate([flat, flip(flat, mask)], axis=1)
    pieces = gather_far((flat, flip(flat, 2), flip(flat, 4)))
    return jnp.stack(pieces).reshape((PIECES,) + piece.shape[:-1] + (LANES,))


def scatter_dp(grads):
    if lax.axis_size("dp") == PIECES:
        return lax.psum_scatter(grads, "dp", scatter_dimension=0, tiled=False)
    flat = grads.reshape(PIECES, -1, LANES)
    own, by_x, by_y, far = add_low(flat[:4], flip(flat[4:], 1))
    by_y = add_low(by_y, flip(far, 2))
    total = add_low(add_low(own, flip(by_x, 2)), flip(by_y, 4))
    return far_scatter(total).reshape(grads.shape[1:3] + (-1,))


def to_relative(rows, back=False):
    size = lax.axis_size("dp")
    place = lax.axis_index("dp")
    bits = size.bit_length() - 1
    lead = rows.shape[:-1]
    axes = len(lead)
    chunk = rows.shape[-1] // size
    wanted = [bits - 1, bits - 3, bits - 2] + list(range(bits - 3))
    order = list(range(axes)) + [axes + n for n in wanted] + [axes + bits]
    cube = rows.reshape(lead + (2,) * bits + (chunk,))
    if back:
        cube = jnp.transpose(cube, [order.index(n) for n in range(len(order))])
    for n in range(bits):
        cube = jnp.where((place >> (bits - 1 - n)) & 1 == 1, jnp.flip(cube, axes + n), cube)
    if not back:
        cube = jnp.transpose(cube, order)
    return cube.reshape(rows.shape)


def shift(rows, step):
    size = lax.axis_size("tensor")
    pairs = [(n, n + step) for n in range(size) if 0 <= n + step < size]
    return lax.ppermute(rows, "tensor", pairs)


NN = ((1,), (0,))
NT = ((1,), (1,))
TN = ((0,), (0,))


def dot(left, right, dims):
    return lax.dot_general(left, right, (dims, ((), ())), preferred_element_type=jnp.float32)


def wide(pieces, rows, slab=0):
    return jnp.concatenate([piece[slab, rows, :] for piece in pieces], axis=1)


def relative(order, ref, rows):
    return jnp.concatenate(
        [
            ref[rows, pl.ds(pl.multiple_of(order[n] * LANES, LANES), LANES)]
            for n in range(PIECES)
        ],
        axis=1,
    )


def normed(values):
    centered = values - jnp.mean(values, axis=-1, keepdims=True)
    scale = lax.rsqrt(jnp.mean(centered * centered, axis=-1, keepdims=True) + NORM_EPS)
    return (centered * scale, scale)


def norm_pull(hat, scale, gain, grad):
    scaled = grad * gain
    return scale * (
        scaled
        - jnp.mean(scaled, axis=-1, keepdims=True)
        - hat * jnp.mean(scaled * hat, axis=-1, keepdims=True)
    )


def row_steps(count, size, body):
    def step(n, carried):
        body(pl.ds(pl.multiple_of(n * size, size), size))
        return carried

    lax.fori_loop(0, count // size, step, 0)


def whole_spec(array):
    return pl.BlockSpec(array.shape, lambda *_: (0,) * len(array.shape))


def run(kernel, name, operands, outs, scratch, flops, after=(), steps=None):
    order, operands = operands[0], operands[1:]
    specs = [spec if spec is not None else whole_spec(array) for array, spec in operands]
    out_specs = [
        spec if spec is not None else pl.BlockSpec(shape, lambda *_, n=len(shape): (0,) * n)
        for shape, dtype, spec in outs
    ]
    moved = sum(array.size * array.dtype.itemsize for array, _ in operands)
    moved += sum(math.prod(shape) * jnp.dtype(dtype).itemsize for shape, dtype, _ in outs)
    kept, made = len(operands), len(outs)

    def body(order_ref, *refs):
        refs = refs[:kept] + refs[kept + len(after) :]
        token = refs[kept + made]
        token[...] = jnp.zeros_like(token)
        kernel(order_ref, *refs[: kept + made], *refs[kept + made + 1 :])

    return pl.pallas_call(
        body,
        grid_spec=pltpu.PrefetchScalarGridSpec(
            num_scalar_prefetch=1,
            grid=(steps or lax.axis_size("tensor"),),
            in_specs=specs + [pl.BlockSpec(memory_space=pl.ANY)] * len(after),
            out_specs=out_specs + [pl.BlockSpec((1, LANES), lambda *_: (0, 0))],
            scratch_shapes=scratch,
        ),
        out_shape=[jax.ShapeDtypeStruct(shape, dtype) for shape, dtype, _ in outs]
        + [jax.ShapeDtypeStruct((1, LANES), jnp.int32)],
        compiler_params=pltpu.CompilerParams(
            dimension_semantics=("arbitrary",), vmem_limit_bytes=VMEM_BYTES
        ),
        cost_estimate=pl.CostEstimate(
            flops=int(COST_FACTOR * flops), bytes_accessed=LANES, transcendentals=0
        ),
        name=name,
    )(order, *[array for array, _ in operands], *after)


def held_back(value, after):
    def body(value_ref, *refs):
        refs[-1][...] = value_ref[...]

    return pl.pallas_call(
        body,
        in_specs=[pl.BlockSpec(memory_space=pltpu.VMEM)]
        + [pl.BlockSpec(memory_space=pl.ANY)] * len(after),
        out_specs=pl.BlockSpec(memory_space=pltpu.VMEM),
        out_shape=jax.ShapeDtypeStruct(value.shape, value.dtype),
        name="held_back",
    )(value, *after)


def blend(name, jobs, after):
    halves = 2
    operands, specs, out_specs, shapes, counts, cut = [], [], [], [], [], []
    for terms in jobs:
        rows, lanes = terms[0][0].shape[-2:]
        small = rows % (16 * halves) != 0 or rows < 512
        height = rows if small else rows // halves
        for term in terms:
            operands.append(term[0])
            if len(term) == 1:
                specs.append(pl.BlockSpec((height, lanes), lambda i, s=small: (0 if s else i, 0)))
            else:
                specs.append(
                    pl.BlockSpec(
                        (None, height, lanes),
                        lambda i, s=small, n=term[1]: (n, 0 if s else i, 0),
                    )
                )
        out_specs.append(pl.BlockSpec((height, lanes), lambda i, s=small: (0 if s else i, 0)))
        shapes.append(jax.ShapeDtypeStruct((rows, lanes), jnp.bfloat16))
        counts.append(len(terms))
        cut.append(small)

    def body(*refs):
        ins = refs[: len(operands)]
        outs = refs[len(operands) + len(after) :]
        outs[-1][...] = jnp.zeros_like(outs[-1])
        first = 0
        for n, count in enumerate(counts):
            terms = ins[first : first + count]
            first += count

            def add(out=outs[n], terms=terms):
                out[...] = sum(
                    (term[...].astype(jnp.float32) for term in terms[1:]),
                    terms[0][...].astype(jnp.float32),
                ).astype(jnp.bfloat16)

            pl.when((pl.program_id(0) == 0) | (not cut[n]))(add)

    *sums, token = pl.pallas_call(
        body,
        grid=(halves,),
        in_specs=specs + [pl.BlockSpec(memory_space=pl.ANY)] * len(after),
        out_specs=out_specs + [pl.BlockSpec((1, LANES), lambda i: (0, 0))],
        out_shape=shapes + [jax.ShapeDtypeStruct((1, LANES), jnp.int32)],
        compiler_params=pltpu.CompilerParams(
            dimension_semantics=("arbitrary",), vmem_limit_bytes=VMEM_BYTES
        ),
        name=name,
    )(*operands, *after)
    return (sums, token)


ALL, ODD, EVEN = (0, 1), (1, 2), (0, 2)


def slabs(piece, rows, part=ALL, first=0, count=1):
    return (
        piece,
        pl.BlockSpec((count, rows, LANES), lambda n, *_: (part[0] + part[1] * n, first, 0)),
    )


def gathered(array, rows, part=ALL, count=1):
    return [
        (
            array,
            pl.BlockSpec(
                (None, count, rows, LANES),
                lambda n, order, p=p: (order[p], part[0] + part[1] * n, 0, 0),
            ),
        )
        for p in range(PIECES)
    ]


def gathered_out(parts, rows):
    return (
        (PIECES, parts, rows, LANES),
        jnp.bfloat16,
        pl.BlockSpec((PIECES, 1, rows, LANES), lambda n, order: (0, order[PIECES + n], 0, 0)),
    )


def store_gathered(order, ref, rows, values):
    values = values.astype(jnp.bfloat16)
    for n in range(PIECES):
        ref[order[n], 0, rows, :] = values[:, n * LANES : (n + 1) * LANES]


def lead(array, part=ALL, count=1):
    shape = (count,) + array.shape[1:]
    return (
        array,
        pl.BlockSpec(shape, lambda n, *_: (part[0] + part[1] * n,) + (0,) * (len(shape) - 1)),
    )


def turned_block(array, rows, part=ALL):
    return (array, pl.BlockSpec((rows, array.shape[1]), lambda n, *_: (part[0] + part[1] * n, 0)))


def lead_out(shape, dtype):
    return (shape, dtype, pl.BlockSpec((1,) + shape[1:], lambda n, *_: (n,) + (0,) * (len(shape) - 1)))


def piece_outs(parts, rows):
    low = jnp.bfloat16
    own = pl.BlockSpec((1, rows, LANES), lambda n, *_: (n, 0, 0))
    other = pl.BlockSpec((4, 1, rows, LANES), lambda n, *_: (0, n, 0, 0))
    return [((parts, rows, LANES), low, own)] * 4 + [((4, parts, rows, LANES), low, other)]


def store_pieces(refs, rows, values):
    values = values.astype(jnp.bfloat16)
    for n in range(4):
        refs[n][0, rows, :] = values[:, n * LANES : (n + 1) * LANES]
        refs[4][n, 0, rows, :] = values[:, (n + 4) * LANES : (n + 5) * LANES]


def heads_kernel(order, hidden, before, after, gains, cosine, sine, *refs):
    pieces, (q_out, k_out, v_out, rows_wide) = refs[:PIECES], refs[PIECES:]
    row_count = hidden.shape[0]
    gain = gains[0:1, :]

    def norm_rows(source, rows, first):
        values = relative(order, source, rows).astype(jnp.float32)
        return (normed(values)[0] * gain).astype(jnp.bfloat16)

    @pl.when(pl.program_id(0) == 0)
    def _():
        rows_wide[0:HALF, :] = norm_rows(before, slice(0, HALF), 0)
        rows_wide[HALF + row_count :, :] = norm_rows(after, slice(0, HALF), 0)

        def one(rows):
            values = norm_rows(hidden, rows, 0)
            rows_wide[pl.ds(pl.multiple_of(rows.start + HALF, HALF), HALF), :] = values

        row_steps(row_count, HALF, one)

    width = 2 * LANES

    def turned(mixed, rows):
        front, back = mixed[:, :LANES], mixed[:, LANES:]
        cos, sin = cosine[rows, :], sine[rows, :]
        return (front * cos - back * sin, back * cos + front * sin)

    inner = slice(HALF, HALF + row_count)
    scale = HEAD_DIM ** (-0.5)
    front, back = turned(dot(rows_wide[inner, :], wide(pieces, slice(0, width)), NT), inner)
    q_out[0, :, :LANES] = (front.astype(jnp.bfloat16) * scale).astype(jnp.bfloat16)
    q_out[0, :, LANES:] = (back.astype(jnp.bfloat16) * scale).astype(jnp.bfloat16)
    front, back = turned(
        dot(rows_wide[...], wide(pieces, slice(width, 2 * width)), NT), slice(None)
    )
    k_out[0, :, :LANES] = front.astype(jnp.bfloat16)
    k_out[0, :, LANES:] = back.astype(jnp.bfloat16)
    v_out[0] = dot(rows_wide[...], wide(pieces, slice(2 * width, 3 * width)), NT).astype(
        jnp.bfloat16
    )


def head_masks():
    lane = lax.broadcasted_iota(jnp.int32, (1, 2 * LANES), 1)
    turned = [((lane % LANES) // 32 == n).astype(jnp.float32).astype(jnp.bfloat16) for n in range(4)]
    plain = [(lane // HEAD_DIM == n).astype(jnp.float32).astype(jnp.bfloat16) for n in range(4)]
    return (turned, plain)


def attend_kernel(order, bias, q_in, k_in, v_in, out, log_out):
    turned, plain = head_masks()
    lane = lax.broadcasted_iota(jnp.int32, (BLOCK, LANES), 1)

    def block(n, carried):
        rows = pl.ds(pl.multiple_of(n * BLOCK, BLOCK), BLOCK)
        span = pl.ds(pl.multiple_of(n * BLOCK, BLOCK), BLOCK + 2 * HALF)
        queries, keys, values = q_in[0, rows, :], k_in[0, span, :], v_in[0, span, :]
        masked = bias[n]
        total = jnp.zeros((BLOCK, 2 * LANES), jnp.float32)
        logs = jnp.zeros((BLOCK, LANES), jnp.float32)
        for h in range(4):
            scores = dot(queries * turned[h], keys, NT) + masked
            row_top = jnp.max(scores, axis=-1, keepdims=True)
            lifted = jnp.exp(scores - row_top)
            row_total = jnp.sum(lifted, axis=-1, keepdims=True)
            probs_low = (lifted * (1.0 / row_total)).astype(jnp.bfloat16)
            total = total + dot(probs_low, values * plain[h], NN)
            logs = jnp.where(lane == h, row_top + jnp.log(row_total), logs)
        out[0, rows, :] = total.astype(jnp.bfloat16)
        log_out[0, rows, :] = logs
        return carried

    lax.fori_loop(0, bias.shape[0], block, 0)


def proj_kernel(order, hidden, gains, attended, *refs):
    pieces, (middle, rows_two) = refs[:PIECES], refs[PIECES:]
    step = pl.program_id(0)

    @pl.when(step == 0)
    def _():
        def one(rows):
            middle[rows, :] = relative(order, hidden, rows).astype(jnp.float32)

        row_steps(hidden.shape[0], HALF, one)

    middle[...] += dot(attended[0], wide(pieces, slice(None)), NN)

    @pl.when(step == pl.num_programs(0) - 1)
    def _():
        def one(rows):
            rows_two[rows, :] = (normed(middle[rows, :])[0] * gains[1:2, :]).astype(jnp.bfloat16)

        row_steps(hidden.shape[0], HALF, one)


def gate_kernel(order, rows_two, *refs):
    pieces, (active, gate_side, up_side, rows_turned, gate, up) = refs[:PIECES], refs[PIECES:]

    @pl.when(pl.program_id(0) == 0)
    def _():
        rows_turned[...] = rows_two[...].T

    count = gate.shape[0]
    gate[...] = dot(wide(pieces, slice(0, count)), rows_turned[...], NN)
    up[...] = dot(wide(pieces, slice(count, 2 * count)), rows_turned[...], NN)

    def one(rows):
        x, u = gate[rows, :], up[rows, :]
        below = 0.5 * (1.0 + lax.erf(x * (0.5**0.5)))
        density = jnp.exp(-0.5 * x * x) * ((2.0 * math.pi) ** -0.5)
        lifted = x * below
        active[rows, :] = (lifted * u).astype(jnp.bfloat16)
        gate_side[rows, :] = (u * (below + x * density)).astype(jnp.bfloat16)
        up_side[rows, :] = lifted.astype(jnp.bfloat16)

    row_steps(count, 16, one)


def down_kernel(order, middle, active, *refs):
    pieces, (out, total) = refs[:PIECES], refs[PIECES:]
    step = pl.program_id(0)

    @pl.when(step == 0)
    def _():
        total[...] = middle[...]

    total[...] += dot(active[...], wide(pieces, slice(None)), TN)

    @pl.when(step == pl.num_programs(0) - 1)
    def _():
        for n in range(PIECES):
            lanes = pl.ds(pl.multiple_of(order[n] * LANES, LANES), LANES)
            out[:, lanes] = total[:, n * LANES : (n + 1) * LANES].astype(jnp.bfloat16)


def down_grad_kernel(order, cotangent, active, *refs):
    grads, cot_out = refs

    @pl.when(pl.program_id(0) == 0)
    def _():
        def one(rows):
            cot_out[rows, :] = relative(order, cotangent, rows)

        row_steps(cotangent.shape[0], HALF, one)

    store_gathered(order, grads, slice(None), dot(active[...], cot_out[...], NN))


def in_grad_kernel(order, cot, rows_two, gate_side, up_side, *refs):
    pieces, (grads, gate_out, up_out, cot_turned, grad_active) = refs[:PIECES], refs[PIECES:]

    @pl.when(pl.program_id(0) == 0)
    def _():
        cot_turned[...] = cot[...].T

    count = grad_active.shape[0]
    grad_active[...] = dot(wide(pieces, slice(None)), cot_turned[...], NN)

    def one(rows):
        grad = grad_active[rows, :]
        gate_out[rows, :] = (grad * gate_side[rows, :].astype(jnp.float32)).astype(jnp.bfloat16)
        up_out[rows, :] = (grad * up_side[rows, :].astype(jnp.float32)).astype(jnp.bfloat16)

    row_steps(count, 16, one)
    store_gathered(order, grads, slice(0, count), dot(gate_out[...], rows_two[...], NN))
    store_gathered(order, grads, slice(count, 2 * count), dot(up_out[...], rows_two[...], NN))


def middle_grad_kernel(order, middle, cot, gains, *refs):
    sides, pieces, refs = refs[:2], refs[2 : 2 + PIECES], refs[2 + PIECES :]
    grad_middle, grad_low, gain_out, total = refs
    step = pl.program_id(0)
    count = sides[0].shape[0]

    @pl.when(step == 0)
    def _():
        total[...] = jnp.zeros_like(total)
        gain_out[...] = jnp.zeros_like(gain_out)

    for n, side in enumerate(sides):
        total[...] += dot(side[...], wide(pieces, slice(n * count, (n + 1) * count)), TN)

    @pl.when(step == pl.num_programs(0) - 1)
    def _():
        def one(rows):
            grad = total[rows, :]
            hat, scale = normed(middle[rows, :])
            result = cot[rows, :].astype(jnp.float32) + norm_pull(hat, scale, gains[1:2, :], grad)
            grad_middle[rows, :] = result
            grad_low[rows, :] = result.astype(jnp.bfloat16)
            gain_out[0:1, :] += jnp.sum(grad * hat, axis=0, keepdims=True)

        row_steps(middle.shape[0], HALF, one)


def attend_grad_kernel(
    order, bias, cosine, sine, grad_low, rows_wide, q_in, k_in, v_in, attended, logs, *refs
):
    pieces, refs = refs[:PIECES], refs[PIECES:]
    weight_grads, (query_out, pair_out, grad_keys, grad_values, grad_out) = refs[:5], refs[5:]
    turned, plain = head_masks()
    row_count = grad_low.shape[0]
    low = jnp.bfloat16
    width = 2 * LANES
    grad_out[...] = dot(grad_low[...], wide(pieces, slice(None)), NT).astype(low)
    grad_keys[...] = jnp.zeros_like(grad_keys)
    grad_values[...] = jnp.zeros_like(grad_values)

    def back(values, rows):
        front, rear = values[:, :LANES], values[:, LANES:]
        cos, sin = cosine[rows, :], sine[rows, :]
        return (front * cos + rear * sin, rear * cos - front * sin)

    def block(n, carried):
        rows = pl.ds(pl.multiple_of(n * BLOCK, BLOCK), BLOCK)
        span = pl.ds(pl.multiple_of(n * BLOCK, BLOCK), BLOCK + 2 * HALF)
        queries, keys, values = q_in[0, rows, :], k_in[0, span, :], v_in[0, span, :]
        grad_rows = grad_out[rows, :]
        masked = bias[n]
        log_rows = logs[0, rows, :]
        grad_query = jnp.zeros((BLOCK, width), jnp.float32)
        grad_key = jnp.zeros((BLOCK + 2 * HALF, width), jnp.float32)
        grad_value = jnp.zeros((BLOCK + 2 * HALF, width), jnp.float32)
        for h in range(4):
            query_head, grad_head = queries * turned[h], grad_rows * plain[h]
            scores = dot(query_head, keys, NT) + masked
            probs = jnp.exp(scores - log_rows[:, h : h + 1])
            grad_probs = dot(grad_head, values, NT)
            row_delta = jnp.sum(probs * grad_probs, axis=-1, keepdims=True)
            grad_scores = (probs * (grad_probs - row_delta)).astype(low)
            grad_query = grad_query + dot(grad_scores, keys * turned[h], NN)
            grad_key = grad_key + dot(grad_scores, query_head, TN)
            grad_value = grad_value + dot(probs.astype(low), grad_head, TN)
        place = pl.ds(pl.multiple_of(n * BLOCK + HALF, HALF), BLOCK)
        front, rear = back(grad_query * HEAD_DIM ** (-0.5), place)
        query_out[0, rows, :LANES] = front.astype(low)
        query_out[0, rows, LANES:] = rear.astype(low)
        grad_keys[span, :] += grad_key
        grad_values[span, :] += grad_value
        return carried

    lax.fori_loop(0, bias.shape[0], block, 0)
    front, rear = back(grad_keys[...], slice(None))
    pair_out[0, 0, :, :LANES] = front.astype(low)
    pair_out[0, 0, :, LANES:] = rear.astype(low)
    pair_out[0, 1] = grad_values[...].astype(low)
    inner = slice(HALF, HALF + row_count)
    store_pieces(weight_grads, slice(0, width), dot(query_out[0], rows_wide[inner, :], TN))
    for c in range(2):
        rows = slice((1 + c) * width, (2 + c) * width)
        store_pieces(weight_grads, rows, dot(pair_out[0, c], rows_wide[...], TN))
    store_pieces(weight_grads, slice(3 * width, 4 * width), dot(attended[0], grad_low[...], TN))


def input_grad_kernel(order, hidden, gains, grad_middle, *refs):
    even, odd, (before, after), refs = refs[:2], refs[2:4], refs[4:6], refs[6:]
    pieces, (grad_input, gain_out, mixed, total) = refs[:PIECES], refs[PIECES:]
    step = pl.program_id(0)
    row_count = hidden.shape[0]
    width = 2 * LANES
    last = row_count - HALF

    @pl.when(step == 0)
    def _():
        total[...] = jnp.zeros_like(total)
        gain_out[...] = jnp.zeros_like(gain_out)

    def sum_low(left, right):
        return (left.astype(jnp.float32) + right.astype(jnp.float32)).astype(jnp.bfloat16)

    def add(slab, queries, pairs):
        total[...] += dot(queries[0], wide(pieces, slice(0, width), slab), NN)
        for c in range(2):
            mixed[...] = pairs[0, c, HALF : HALF + row_count, :]
            mixed[0:HALF, :] = sum_low(mixed[0:HALF, :], before[slab, c])
            mixed[last:, :] = sum_low(mixed[last:, :], after[slab, c])
            rows = slice((1 + c) * width, (2 + c) * width)
            total[...] += dot(mixed[...], wide(pieces, rows, slab), NN)

    add(0, *even)
    add(1, *odd)

    @pl.when(step == pl.num_programs(0) - 1)
    def _():
        def one(rows):
            grad = total[rows, :]
            hat, scale = normed(relative(order, hidden, rows).astype(jnp.float32))
            result = grad_middle[rows, :] + norm_pull(hat, scale, gains[0:1, :], grad)
            for n in range(PIECES):
                lanes = pl.ds(pl.multiple_of(order[n] * LANES, LANES), LANES)
                grad_input[rows, lanes] = result[:, n * LANES : (n + 1) * LANES]
            gain_out[0:1, :] += jnp.sum(grad * hat, axis=0, keepdims=True)

        row_steps(row_count, HALF, one)


def local(
    hidden_in,
    seq_lengths,
    cotangent,
    w_qkv,
    w_proj,
    w_in,
    w_down,
    norm_gains,
    qkv_first,
    qkv_second,
    proj_first,
    proj_second,
    in_first,
    in_second,
    down_first,
    down_second,
    gain_first,
    gain_second,
):
    row_count = hidden_in.shape[0]
    wide_count = row_count + 2 * HALF
    size = lax.axis_size("tensor")
    dp_size = lax.axis_size("dp")
    group_rows = row_count * size
    low, full = jnp.bfloat16, jnp.float32
    chunk = norm_gains.shape[1]
    head_wide = w_proj.shape[1]
    head_rows = 4 * head_wide
    slab_rows = head_rows + SLAB_PAD
    hidden_wide = w_down.shape[1]
    head_count, half_dim = head_wide // HEAD_DIM, HEAD_DIM // 2

    def halves_first(weight):
        split = weight.reshape(chunk, 2, head_count, 2, half_dim)
        return jnp.transpose(split, (0, 1, 3, 2, 4)).reshape(chunk, 2 * head_wide)

    def heads_first(weight):
        split = weight.reshape(chunk, 2, 2, head_count, half_dim)
        return jnp.transpose(split, (0, 1, 3, 2, 4)).reshape(chunk, 2, head_wide)

    heads_slab = jnp.concatenate(
        [
            jnp.concatenate(
                [halves_first(w_qkv[:, :2].astype(low)), w_qkv[:, 2].astype(low), w_proj.astype(low)],
                axis=1,
            ).T,
            jnp.pad(norm_gains.astype(low), ((0, SLAB_PAD - 2), (0, 0))),
        ]
    )
    ffn_slab = jnp.concatenate(
        [w_in.astype(low).reshape(chunk, 2 * hidden_wide), w_down.astype(low)], axis=1
    ).T
    if dp_size == PIECES:
        apart = jnp.array([0, 2, 4, 6, 1, 3, 5, 7], jnp.int32)
        order = lax.axis_index("dp").astype(jnp.int32) ^ apart
        hidden, cot_in = hidden_in, cotangent
    else:
        order = jnp.arange(PIECES, dtype=jnp.int32)
        hidden, cot_in = to_relative(hidden_in), to_relative(cotangent)

    place = lax.axis_index("tensor").astype(jnp.int32)
    owners = (place + size - jnp.arange(size, dtype=jnp.int32)) % size
    order = jnp.concatenate([order, owners])
    edges = (shift(hidden[-HALF:], 1), shift(hidden[:HALF], -1))
    zeros = jnp.zeros((1, LANES), jnp.int32)
    heads_near = gather_near(heads_slab, place)
    ffn_slab = tied(ffn_slab, held_back(zeros, heads_near[:1]))
    first = gather_hop(ffn_slab, ffn_slab, 1)
    second = gather_hop(*first, 2)
    token = held_back(zeros, (*heads_near[1:], *second))
    heads_far = gather_far_hop(heads_near, token)
    third = gather_hop(tied(second[0], token), tied(second[1], token), 3)
    start = place + held_back(zeros, (*heads_far, *third))
    start = start if chunk == LANES else start[0, 0]
    ffn_line = jnp.stack(
        [
            ffn_slab,
            jnp.where(start >= 1, first[0], third[1]),
            jnp.where(start >= 2, second[0], second[1]),
            jnp.where(start >= 3, third[0], first[1]),
        ]
    )
    in_all = gather_dp(ffn_line[:, : 2 * hidden_wide])
    heads_pieces = [
        piece.reshape(size, -1, LANES) for piece in gather_far(heads_near, heads_far)
    ]
    gains = jnp.concatenate(
        [piece[0, head_rows : head_rows + 8] for piece in heads_pieces], axis=1
    ).astype(full)

    first_row = lax.axis_index("tensor") * row_count
    segment, position = layout(
        seq_lengths[0], first_row - HALF + jnp.arange(wide_count), group_rows
    )
    cosine, sine = rotary_tables(position)
    bias = jnp.where(allowed_pairs(segment), 0.0, MASKED).astype(full)

    head_block = (size, row_count, head_wide)
    wide_block = (size, wide_count, head_wide)
    tokens = (row_count, D)
    turned = (size * hidden_wide, row_count)
    turned_spec = pl.BlockSpec((hidden_wide, row_count), lambda n, *_: (n, 0))
    matmul = 2 * row_count * D

    queries, keys, values, rows_wide, token = run(
        heads_kernel,
        "heads",
        [order, (hidden, None), (edges[0], None), (edges[1], None), (gains, None)]
        + [(cosine, None), (sine, None)]
        + [slabs(piece, 3 * head_wide) for piece in heads_pieces],
        [lead_out(head_block, low), lead_out(wide_block, low), lead_out(wide_block, low)]
        + [((wide_count, D), low, None)],
        [],
        3 * matmul * D,
    )
    down_all = gather_dp(tied(ffn_line[:, 2 * hidden_wide :], token))
    attended, logs, token = run(
        attend_kernel,
        "attend",
        [order, (bias, None), lead(queries), lead(keys), lead(values)],
        [lead_out(head_block, low), lead_out((size, row_count, LANES), full)],
        [],
        2 * matmul * D,
    )
    middle, rows_two, token = run(
        proj_kernel,
        "proj",
        [order, (hidden, None), (gains, None), lead(attended)]
        + [slabs(piece, head_wide, first=3) for piece in heads_pieces],
        [(tokens, full, None), (tokens, low, None)],
        [],
        matmul * D,
    )
    active, gate_side, up_side, token = run(
        gate_kernel,
        "gate",
        [order, (rows_two, None)] + gathered(in_all, 2 * hidden_wide),
        [(turned, low, turned_spec)] * 3,
        [
            pltpu.VMEM((D, row_count), low),
            pltpu.VMEM((hidden_wide, row_count), full),
            pltpu.VMEM((hidden_wide, row_count), full),
        ],
        2 * matmul * FF,
    )

    down_grads, cot, token = run(
        down_grad_kernel,
        "down_grad",
        [order, (cot_in, None), turned_block(active, hidden_wide)],
        [gathered_out(size, hidden_wide), (tokens, low, None)],
        [],
        matmul * FF,
    )
    down_line = scatter_dp(down_grads)
    half = size // 2
    in_grads, gate_grad, up_grad, token = run(
        in_grad_kernel,
        "in_grad",
        [order, (cot, None), (rows_two, None)]
        + [turned_block(gate_side, hidden_wide), turned_block(up_side, hidden_wide)]
        + gathered(down_all, hidden_wide),
        [gathered_out(size, 2 * hidden_wide)] + [(turned, low, turned_spec)] * 2,
        [pltpu.VMEM((D, row_count), low), pltpu.VMEM((hidden_wide, row_count), full)],
        3 * matmul * FF,
    )
    in_line = scatter_dp(in_grads)
    grad_middle, grad_low, gain_two, token = run(
        middle_grad_kernel,
        "middle_grad",
        [order, (middle, None), (cot, None), (gains, None)]
        + [turned_block(side, hidden_wide) for side in (gate_grad, up_grad)]
        + gathered(in_all, 2 * hidden_wide),
        [(tokens, full, None), (tokens, low, None), ((8, D), full, None)],
        [pltpu.VMEM(tokens, full)],
        2 * matmul * FF,
    )

    def core_hop(outs):
        return (outs[:4], flip(outs[4], 1))

    def core_sums(own, received):
        entries = own[0].shape[0]
        received = received.reshape((-1,) + received.shape[2:])
        return [
            [(part, e), (received, n * entries + e)]
            for n, part in enumerate(own)
            for e in range(entries)
        ]

    def far_hop(sums):
        return (flip(sums[6], 2), flip(sums[7], 4))

    def far_sums(sums, arrived):
        return [[(sums[4],), (arrived[0],)], [(sums[3],), (arrived[1],)]]

    def near_hop(sums, added):
        return (flip(sums[2], 2), flip(added[0], 4), flip(added[1], 2), flip(sums[5], 4))

    def near_sums(sums, arrived):
        return [
            [(sums[0],), (arrived[0],), (arrived[1],)],
            [(sums[1],), (arrived[2],), (arrived[3],)],
        ]

    def attend_grad(part, count, name, after):
        return run(
            attend_grad_kernel,
            name,
            [order, (bias, None), (cosine, None), (sine, None), (grad_low, None), (rows_wide, None)]
            + [lead(array, part) for array in (queries, keys, values, attended, logs)]
            + [slabs(piece, head_wide, part, first=3) for piece in heads_pieces],
            piece_outs(count, head_rows)
            + [
                lead_out((count, row_count, head_wide), low),
                lead_out((count, 2, wide_count, head_wide), low),
            ],
            [
                pltpu.VMEM((wide_count, head_wide), full),
                pltpu.VMEM((wide_count, head_wide), full),
                pltpu.VMEM((row_count, head_wide), low),
            ],
            3 * count * matmul * D,
            after=after,
            steps=count,
        )

    *odd_outs, odd_queries, odd_pairs, token = attend_grad(ODD, half, "attend_grad_odd", ())
    odd_core = core_hop(odd_outs)
    *even_outs, even_queries, even_pairs, token = attend_grad(
        EVEN, half, "attend_grad_even", (token,)
    )
    even_core = core_hop(even_outs)
    odd, token = blend("sums_one", core_sums(*odd_core), (token,))
    odd_far = far_hop(odd)
    pairs = [even_pairs[0], odd_pairs[0], even_pairs[1], odd_pairs[1]]
    edge_after = jnp.stack([pair[:, -HALF:] for pair in pairs[-1:] + pairs[:-1]])
    edge_before = jnp.stack([pair[:, :HALF] for pair in pairs[1:] + pairs[:1]])
    edges = (shift(edge_after, 1), shift(edge_before, -1))
    hidden_out, token = run(
        down_kernel,
        "down",
        [order, (middle, None), turned_block(active, hidden_wide)]
        + gathered(down_all, hidden_wide),
        [(tokens, low, None)],
        [pltpu.VMEM(tokens, full)],
        matmul * FF,
        after=(token,),
    )
    (*even, odd_y, odd_x), token = blend(
        "sums_two", core_sums(*even_core) + far_sums(odd, odd_far), (token,)
    )
    even_far = far_hop(even)
    odd_near = near_hop(odd, (odd_y, odd_x))
    grad_input, gain_one, token = run(
        input_grad_kernel,
        "input_grad",
        [order, (hidden, None), (gains, None), (grad_middle, None)]
        + [lead(array) for array in (even_queries, even_pairs, odd_queries, odd_pairs)]
        + [lead(array, count=2) for array in edges]
        + [slabs(piece, 3 * head_wide, count=2) for piece in heads_pieces],
        [(tokens, full, None), ((8, D), full, None)],
        [pltpu.VMEM((row_count, head_wide), low), pltpu.VMEM(tokens, full)],
        3 * matmul * D,
        after=(token,),
        steps=half,
    )
    (*odd_parts, even_y, even_x), token = blend(
        "sums_three",
        near_sums(odd, odd_near) + far_sums(even, even_far),
        (token,),
    )
    even_near = near_hop(even, (even_y, even_x))
    ffn_sum = lax.psum_scatter(
        tied(jnp.concatenate([in_line, down_line], axis=1), token),
        "tensor",
        scatter_dimension=0,
        tiled=False,
    )
    odd_parts = [far_scatter(part) for part in odd_parts]

    def line_round(parts, step, arrived=None):
        to_after, to_before = parts[size - step], parts[step]
        if arrived is not None:
            to_after, to_before = add_low(to_after, arrived[0]), add_low(to_before, arrived[1])
        return line_hop(to_after, to_before, step)

    even_parts, token = blend("sums_four", near_sums(even, even_near), (token))
    gain_sum, _ = gain_scatter(tied(jnp.concatenate([gain_one[:1], gain_two[:1]]), token))
    even_parts = [far_scatter(part) for part in even_parts]
    heads_parts = [even_parts[0], odd_parts[0], even_parts[1], odd_parts[1]]
    heads_arrived = line_round(heads_parts, 3)
    heads_arrived = line_round(heads_parts, 2, heads_arrived)
    last_token = held_back(zeros, (ffn_sum, *heads_arrived))
    heads_parts[1:] = [tied(part, last_token) for part in heads_parts[1:]]
    heads_arrived = line_round(heads_parts, 1, heads_arrived)
    heads_total = line_end(heads_parts[0], heads_arrived)
    if dp_size != PIECES:
        hidden_out, grad_input = to_relative(hidden_out, True), to_relative(grad_input, True)

    ffn_sum = ffn_sum.astype(full).T
    in_sum = ffn_sum[:, : 2 * hidden_wide].reshape(w_in.shape)
    down_sum = ffn_sum[:, 2 * hidden_wide :]
    heads_sum = heads_total.T
    qkv_sum = jnp.concatenate(
        [
            heads_first(heads_sum[:, : 2 * head_wide]),
            heads_sum[:, None, 2 * head_wide : 3 * head_wide],
        ],
        axis=1,
    )
    proj_sum = heads_sum[:, 3 * head_wide :]
    qkv_one, qkv_two, qkv_new = adam_update(w_qkv, qkv_sum, qkv_first, qkv_second, D ** (-0.5))
    proj_one, proj_two, proj_new = adam_update(
        w_proj, proj_sum, proj_first, proj_second, (D // HALF) ** (-0.5)
    )
    in_one, in_two, in_new = adam_update(w_in, in_sum, in_first, in_second, D ** (-0.5))
    down_one, down_two, down_new = adam_update(
        w_down, down_sum, down_first, down_second, (FF // 2) ** (-0.5)
    )
    gain_one, gain_two, gains_new = adam_update(
        norm_gains, gain_sum, gain_first, gain_second, GAIN_RATE
    )
    return (
        hidden_out,
        grad_input,
        qkv_one,
        qkv_two,
        qkv_new,
        proj_one,
        proj_two,
        proj_new,
        in_one,
        in_two,
        in_new,
        down_one,
        down_two,
        down_new,
        gain_one,
        gain_two,
        gains_new,
    )


def solution(mesh):
    placed = (
        P(("dp", "tensor"), None),
        P("dp", None),
        P(("dp", "tensor"), None),
        P("dp", None, "tensor"),
        P("dp", "tensor"),
        P("dp", None, "tensor"),
        P("dp", "tensor"),
        P(None, "dp"),
        P("dp", None, "tensor"),
        P("dp", None, "tensor"),
        P("dp", "tensor"),
        P("dp", "tensor"),
        P("dp", None, "tensor"),
        P("dp", None, "tensor"),
        P("dp", "tensor"),
        P("dp", "tensor"),
        P(None, "dp"),
        P(None, "dp"),
    )
    return jax.shard_map(
        local,
        mesh=mesh,
        in_specs=placed,
        out_specs=(
            P(("dp", "tensor"), None),
            P(("dp", "tensor"), None),
            P("dp", None, "tensor"),
            P("dp", None, "tensor"),
            P("dp", None, "tensor"),
            P("dp", "tensor"),
            P("dp", "tensor"),
            P("dp", "tensor"),
            P("dp", None, "tensor"),
            P("dp", None, "tensor"),
            P("dp", None, "tensor"),
            P("dp", "tensor"),
            P("dp", "tensor"),
            P("dp", "tensor"),
            P(None, "dp"),
            P(None, "dp"),
            P(None, "dp"),
        ),
        check_vma=False,
    )
```
